32 devices in a mesh: row: 4 (over y, core), col: 8 (over z, x).
Axes of the slice: x: 2, y: 2, z: 4, core: 2. Of those that a mesh axis runs over, the one named last changes fastest.
Arguments:
- tensor: bfloat16 [128, 384, 4096], P(None, 'col', 'row'), may hold values from -2 to 2
- first_factor: bfloat16 [64, 4096], P(None, ('row', 'col')), may hold values from -0.453125 to 0.453125
- second_factor: bfloat16 [64, 384], P(None, 'col'), may hold values from -1.4799 to 1.4799
Outputs:
- frames: float32 [64, 128], replicated
- mode_one: float32 [64, 4096], P(None, ('row', 'col'))
The draws below stay inside these ranges and needn't reach their ends.
All inputs are finite; a program needn't handle non-finite values.
Results may differ from the reference program's by a relative error of at most 0.004.
Values may be sent and summed in bfloat16 or wider, within the bound.
No kernel may reach another device: no remote copies, remote signals or barrier semaphores. Data moves between devices by JAX's collectives and lax.ppermute only.
A program may use at most 128 MiB of HBM per device.

```python
import jax
import jax.numpy as jnp
from jax import lax

R = 64
K = 128
I = 4096
J = 384


def factor_values(key, components, length):
    key_spread, key_noise, key_common = jax.random.split(key, 3)
    position = jnp.arange(length, dtype=jnp.float32) / length
    rising = jnp.exp(jnp.log(3.0) * position)
    spread = jnp.exp(jax.random.uniform(key_spread, (length,), jnp.float32, 0.0, jnp.log(10.0)))
    noise = jnp.clip(jax.random.normal(key_noise, (components, length), jnp.float32), -4.0, 4.0)
    common = 0.6 * jnp.clip(jax.random.normal(key_common, (length,), jnp.float32), -4.0, 4.0)
    values = (rising * spread)[None, :] * (noise + common[None, :]) / (8.0 * jnp.sqrt(jnp.float32(length)))
    return values.astype(jnp.bfloat16)


def draw_first_factor(key, part):
    return factor_values(jax.random.fold_in(key, 11), R, I)


def draw_second_factor(key, part):
    return factor_values(jax.random.fold_in(key, 23), R, J)


def raised(values, rng, source, target, shards_of, factor):
    def block_of(axis_at):
        return (jnp.arange(values.shape[axis_at]) // (values.shape[axis_at] // shards_of)).reshape((-1,) + (1,) * (values.ndim - 1 - axis_at))

    near = jax.random.permutation(rng, shards_of)[block_of(target)]
    second = (block_of(target) + shards_of // 2) % shards_of
    return jnp.where((block_of(source) == near) | (block_of(source) == second), factor * values, values)


def block_levels(rng, extent, cuts, least, top_value):
    gain, own = 1.0, jax.random.fold_in(rng, 6)
    for dim, shards_of in cuts:
        heights = jnp.exp(jax.random.uniform(jax.random.fold_in(own, dim), (shards_of,), jnp.float32, least / len(cuts), top_value / len(cuts)))
        gain = gain * jnp.repeat(heights, extent[dim] // shards_of).reshape([-1 if axis == dim else 1 for axis in range(len(extent))])
    return gain


def gaussian_with(stream_key, dims, scale, bound, shards, heavy, kind=jnp.bfloat16):
    entries = scale * jax.random.normal(stream_key, dims, jnp.float32)
    if shards:
        entries = entries * block_levels(stream_key, dims, shards, -0.22, 0.18)
    return jnp.clip(raised(entries, jax.random.fold_in(stream_key, 3), *heavy), -bound, bound).astype(kind)


def setup_inputs(seed: int = 0) -> dict:
    key_of = jax.random.split(jax.random.key(seed), 4)
    tensor = gaussian_with(key_of[0], (K, J, I), 0.35, 2.0, ((1, 8), (2, 4)), (1, 2, 8, 2.0))
    first_factor = draw_first_factor(jax.random.fold_in(key_of[3], 71), 0)
    second_factor = draw_second_factor(jax.random.fold_in(key_of[3], 71), 0)
    return {"tensor": tensor, "first_factor": first_factor, "second_factor": second_factor}


ridge_weight = 0.05

def ridge_solve(gram, right_side):
    order_size = gram.shape[0]
    factor_low = jnp.linalg.cholesky(gram + ridge_weight * jnp.eye(order_size, dtype=jnp.float32))
    middle = lax.linalg.triangular_solve(factor_low, right_side, left_side=True, lower=True)
    return lax.linalg.triangular_solve(factor_low, middle, left_side=True, lower=True, transpose_a=True)

def gram_of(factor):
    return jnp.dot(factor.astype(jnp.float32), factor.T.astype(jnp.float32), preferred_element_type=jnp.float32)

def mode_first_sum(tensor, frames, second):

    def step_frame(running, inputs):
        slab, frame_col = inputs
        weights = (frame_col[:, None] * second).astype(jnp.bfloat16)
        running = running + lax.dot_general(weights.astype(jnp.float32), slab.astype(jnp.float32), (((1,), (0,)), ((), ())), preferred_element_type=jnp.float32)
        return (running, None)
    start_sum = jnp.zeros((frames.shape[0], tensor.shape[2]), jnp.float32)
    result, _ = lax.scan(step_frame, start_sum, (tensor, frames.T))
    return result

def reference(tensor, first_factor, second_factor):
    gram_first = gram_of(first_factor)
    gram_second = gram_of(second_factor)
    second_values = second_factor.astype(jnp.float32)

    def frame_column(slab):
        projected = lax.dot_general(first_factor.astype(jnp.float32), slab.astype(jnp.float32), (((1,), (1,)), ((), ())), preferred_element_type=jnp.float32)
        return jnp.sum(projected * second_values, axis=1)
    frame_sum = lax.map(frame_column, tensor).T
    frames = ridge_solve(gram_first * gram_second, frame_sum)
    gram_frames = jnp.dot(frames, frames.T, precision=lax.Precision.HIGHEST)
    first_sum = mode_first_sum(tensor, frames, second_values)
    new_first = ridge_solve(gram_second * gram_frames, first_sum).astype(jnp.bfloat16)
    gram_new = gram_of(new_first)

    def step_second(running, inputs):
        slab, frame_col = inputs
        projected = lax.dot_general(new_first.astype(jnp.float32), slab.astype(jnp.float32), (((1,), (1,)), ((), ())), preferred_element_type=jnp.float32)
        return (running + projected * frame_col[:, None], None)
    start_second = jnp.zeros(second_values.shape, jnp.float32)
    second_sum, _ = lax.scan(step_second, start_second, (tensor, frames.T))
    new_second = ridge_solve(gram_new * gram_frames, second_sum)
    mode_one = mode_first_sum(tensor, frames, new_second)
    return (frames, mode_one)
```

```python
import functools

import jax
import jax.numpy as jnp
from jax import lax
from jax.experimental import pallas as pl
from jax.experimental.pallas import tpu as pltpu
from jax.sharding import PartitionSpec as P

ridge_weight = 0.05
HIGH = lax.Precision.HIGHEST
BOTH = ("row", "col")
F32, BF16 = jnp.float32, jnp.bfloat16
VM = pltpu.VMEM
MIB = 1 << 20


def vmem():
    return pl.BlockSpec(memory_space=VM)


def anywhere():
    return pl.BlockSpec(memory_space=pl.ANY)


def smem():
    return pl.BlockSpec(memory_space=pltpu.SMEM)


def params(mib=16):
    return pltpu.CompilerParams(vmem_limit_bytes=mib * MIB)


def dot(a, b, dims, precision=None):
    return lax.dot_general(a, b, (dims, ((), ())), precision=precision, preferred_element_type=F32)


def tree_sum(values):
    while len(values) > 1:
        values = [values[n] + values[n + 1] for n in range(0, len(values), 2)]
    return values[0]


def swap(x, axes, count, offset):
    return lax.ppermute(x, axes, [(n, n ^ offset) for n in range(count)])


def swaps(x, axes, count, offsets):
    return [x] + [swap(x, axes, count, o) for o in offsets[1:]]


def offsets_of(bits):
    found = [0]
    for bit in bits:
        found = found + [f + bit for f in found]
    return found


def prepare_body(groups, t_ref, b_ref, out_ref, wide_ref, slab, sems):
    frames, cols, _ = t_ref.shape

    def fetch(n):
        return pltpu.make_async_copy(t_ref.at[pl.ds(n * 16, 16)], slab.at[n], sems.at[n])

    for n in range(groups):
        fetch(n).start()
    for j in range(cols):
        wide_ref[j] = jnp.broadcast_to(b_ref[:, j : j + 1], wide_ref.shape[1:])
    to = lax.broadcasted_iota(jnp.int32, (256, 256), 0)
    at = lax.broadcasted_iota(jnp.int32, (256, 256), 1)
    turn = jnp.where((to // 16) + (to % 16) * 16 == at, 1.0, 0.0).astype(BF16)

    def step(n, _):
        fetch(n).wait()
        for g in range(cols // 16):
            block = slab[n, :, g * 16 : g * 16 + 16, :].reshape(256, -1)
            turned = dot(turn, block, ((1,), (0,))).astype(BF16).reshape(16, 16, -1)
            out_ref[g * 16 : g * 16 + 16, pl.ds(pl.multiple_of(n * 16, 16), 16), :] = turned
        return 0

    lax.fori_loop(0, groups, step, 0)


def prepare(tensor, second):
    frames, cols, rows = tensor.shape
    components = second.shape[0]
    groups = frames // 16
    return pl.pallas_call(
        functools.partial(prepare_body, groups),
        out_shape=(VM((cols, frames, rows), BF16), VM((cols, components, 128), F32)),
        in_specs=[anywhere(), vmem()],
        out_specs=(vmem(), vmem()),
        scratch_shapes=[VM((groups, 16, cols, rows), BF16), pltpu.SemaphoreType.DMA((groups,))],
        compiler_params=params(20),
        name="prepare",
    )(tensor, second)


def place(me_ref, pieces, full_ref):
    width = pieces[0].shape[1]
    if len(pieces) == 1:
        full_ref[...] = pieces[0][...].astype(full_ref.dtype)
        return
    for d, piece in enumerate(pieces):
        at = pl.multiple_of((me_ref[0] ^ d) * width, width)
        full_ref[:, pl.ds(at, width)] = piece[...].astype(full_ref.dtype)


def assemble_body(count, me_ref, *refs):
    pieces, (full_ref, gram_ref) = refs[:count], refs[count:]
    place(me_ref, pieces, full_ref)
    full = full_ref[...]
    gram_ref[...] = dot(full, full, ((1,), (1,)))


def assemble(me, pieces, total):
    components = pieces[0].shape[0]
    return pl.pallas_call(
        functools.partial(assemble_body, len(pieces)),
        out_shape=(
            jax.ShapeDtypeStruct((components, total), BF16),
            jax.ShapeDtypeStruct((components, components), F32),
        ),
        in_specs=[smem()] + [vmem()] * len(pieces),
        out_specs=(vmem(), vmem()),
        compiler_params=params(),
        name="assemble",
    )(me, *pieces)


def project_body(span, full_ref, second_ref, t_ref, out_ref, turned_ref):
    components = full_ref.shape[0]
    cols, frames, rows = t_ref.shape
    turned_ref[...] = full_ref[...].astype(F32).T.astype(BF16)
    weights = turned_ref[...]

    def step(n, total):
        block = t_ref[pl.ds(n * span, span)].reshape(span * frames, rows)
        product = dot(block, weights, ((1,), (0,))).reshape(span, frames, components)
        scale = second_ref[pl.ds(pl.multiple_of(n * span, span), span), :]
        for s in range(span):
            total = total + product[s] * scale[s : s + 1, :]
        return total

    total = lax.fori_loop(0, cols // span, step, jnp.zeros((frames, components), F32))
    out_ref[...] = total.T


def project(full, second_turned, turned):
    cols, frames, rows = turned.shape
    components = full.shape[0]
    return pl.pallas_call(
        functools.partial(project_body, 8),
        out_shape=jax.ShapeDtypeStruct((components, frames), F32),
        in_specs=[vmem()] * 3,
        out_specs=vmem(),
        scratch_shapes=[VM((rows, components), BF16)],
        compiler_params=params(),
        name="project",
    )(full, second_turned, turned)


def inverse(matrix):
    size = matrix.shape[0]
    row_at = lax.broadcasted_iota(jnp.int32, (size, size), 0)
    col_at = lax.broadcasted_iota(jnp.int32, (size, size), 1)
    matrix = matrix + jnp.where(row_at == col_at, ridge_weight, 0.0)
    for k in range(size):
        col = matrix[:, k : k + 1]
        row = matrix[k : k + 1, :]
        pivot = 1.0 / matrix[k : k + 1, k : k + 1]
        scaled = jnp.where(col_at[:1] == k, pivot, row * pivot)
        rest = jnp.where(col_at == k, 0.0, matrix) - col * scaled
        matrix = jnp.where(row_at == k, scaled, rest)
    return matrix


def first_inverse_body(grams, seconds, me_ref, *refs):
    gram_refs, second_refs = refs[:grams], refs[grams : grams + seconds]
    out_ref, gram_ref, all_ref = refs[grams + seconds :]
    height = second_refs[0].shape[0]
    for d, piece in enumerate(second_refs):
        at = pl.multiple_of((me_ref[0] ^ d) * height, height)
        all_ref[pl.ds(at, height), :] = piece[...].astype(F32)
    every = all_ref[...].T.astype(BF16)
    gram_second = dot(every, every, ((1,), (1,)))
    gram_ref[...] = gram_second
    out_ref[...] = inverse(tree_sum([g[...] for g in gram_refs]) * gram_second)


def first_inverse(me, grams, seconds):
    size = grams[0].shape[0]
    shape = jax.ShapeDtypeStruct((size, size), F32)
    total = sum(s.shape[0] for s in seconds)
    return pl.pallas_call(
        functools.partial(first_inverse_body, len(grams), len(seconds)),
        out_shape=(shape, shape),
        in_specs=[smem()] + [vmem()] * (len(grams) + len(seconds)),
        out_specs=(vmem(), vmem()),
        scratch_shapes=[VM((total, size), F32)],
        compiler_params=params(),
        name="first_inverse",
    )(me, *grams, *seconds)


def next_inverse_body(grams, *refs):
    out_ref = refs[-1]
    out_ref[...] = inverse(tree_sum([g[...] for g in refs[:grams]]) * refs[grams][...])


def next_inverse(grams, other):
    size = other.shape[0]
    return pl.pallas_call(
        functools.partial(next_inverse_body, len(grams)),
        out_shape=jax.ShapeDtypeStruct((size, size), F32),
        in_specs=[vmem()] * (len(grams) + 1),
        out_specs=vmem(),
        compiler_params=params(),
        name="next_inverse",
    )(*grams, other)


def hand_out(me_ref, sum_ref, outs):
    width = outs[0].shape[1]
    if len(outs) == 1:
        outs[0][...] = sum_ref[...]
        return
    for d, out in enumerate(outs):
        at = pl.multiple_of((me_ref[0] ^ d) * width, width)
        out[...] = sum_ref[:, pl.ds(at, width)]


def slab_body(sums, me_ref, inverse_ref, wide_ref, t_ref, *refs):
    parts, (frames_ref, gram_ref, z_ref, *outs), sum_ref = refs[:sums], refs[sums:-1], refs[-1]
    cols, _, rows = t_ref.shape
    components = inverse_ref.shape[0]
    frames = dot(inverse_ref[...], tree_sum([p[...] for p in parts]), ((1,), (0,)), HIGH)
    frames_ref[...] = frames
    gram_ref[...] = dot(frames, frames, ((1,), (1,)), HIGH)
    high = frames.astype(BF16)
    low = (frames - high.astype(F32)).astype(BF16)
    both = jnp.concatenate([high, low], axis=0)
    span, wide = 8, 256

    def chunk(c, _):
        lanes = pl.ds(pl.multiple_of(c * wide, wide), wide)

        def step(n, total):
            for s in range(span):
                j = n * span + s
                product = dot(both, t_ref[j, :, lanes], ((1,), (0,)))
                z = product[:components] + product[components:]
                z_ref[j, :, lanes] = z
                scale = wide_ref[j]
                total = total + z * jnp.concatenate([scale, scale], axis=1)
            return total

        start = jnp.zeros((components, wide), F32)
        sum_ref[:, lanes] = lax.fori_loop(0, cols // span, step, start)
        return 0

    lax.fori_loop(0, rows // wide, chunk, 0)
    hand_out(me_ref, sum_ref, outs)


def slab(me, inverse_first, wide, turned, parts, shares):
    cols, frames, rows = turned.shape
    components = inverse_first.shape[0]
    share = jax.ShapeDtypeStruct((components, rows // shares), F32)
    return pl.pallas_call(
        functools.partial(slab_body, len(parts)),
        out_shape=(
            jax.ShapeDtypeStruct((components, frames), F32),
            jax.ShapeDtypeStruct((components, components), F32),
            VM((cols, components, rows), F32),
        )
        + (share,) * shares,
        in_specs=[smem()] + [vmem()] * (3 + len(parts)),
        out_specs=(vmem(),) * (3 + shares),
        scratch_shapes=[VM((components, rows), F32)],
        compiler_params=params(),
        name="slab",
    )(me, inverse_first, wide, turned, *parts)


def update_body(inverse_ref, *refs):
    out_ref = refs[-1]
    summed = tree_sum([p[...] for p in refs[:-1]])
    out_ref[...] = dot(inverse_ref[...], summed, ((1,), (0,)), HIGH).astype(out_ref.dtype)


def update(inverse_now, parts):
    return pl.pallas_call(
        update_body,
        out_shape=jax.ShapeDtypeStruct(parts[0].shape, BF16),
        in_specs=[vmem()] * (1 + len(parts)),
        out_specs=vmem(),
        compiler_params=params(),
        name="update",
    )(inverse_now, *parts)


def second_body(full_ref, z_ref, out_ref):
    cols, components, rows = z_ref.shape
    lane = lax.broadcasted_iota(jnp.int32, (8, 128), 1)

    def step(n, _):
        at = pl.ds(pl.multiple_of(n * 8, 8), 8)
        mine = full_ref[at, :]
        total = jnp.zeros((8, 128), F32)
        for j in range(cols):
            product = z_ref[j, at, :] * mine
            folded = tree_sum([product[:, c * 128 : c * 128 + 128] for c in range(rows // 128)])
            total = jnp.where(lane == j, jnp.sum(folded, axis=1, keepdims=True), total)
        out_ref[at, :] = total
        return 0

    lax.fori_loop(0, components // 8, step, 0)


def second(full, z):
    components = full.shape[0]
    return pl.pallas_call(
        second_body,
        out_shape=jax.ShapeDtypeStruct((components, 128), F32),
        in_specs=[vmem()] * 2,
        out_specs=vmem(),
        compiler_params=params(),
        name="second",
    )(full.astype(F32), z)


def mode_body(sums, me_ref, inverse_ref, z_ref, *refs):
    parts, outs, (sum_ref, new_ref) = refs[:sums], refs[sums:-2], refs[-2:]
    cols, components, rows = z_ref.shape
    new_ref[...] = dot(inverse_ref[...], tree_sum([p[...] for p in parts]), ((1,), (0,)), HIGH)

    def step(n, _):
        at = pl.ds(pl.multiple_of(n * 8, 8), 8)
        scale = new_ref[at, :]
        total = jnp.zeros((8, rows), F32)
        for j in range(cols):
            total = total + z_ref[j, at, :] * scale[:, j : j + 1]
        sum_ref[at, :] = total
        return 0

    lax.fori_loop(0, components // 8, step, 0)
    hand_out(me_ref, sum_ref, outs)


def mode(me, inverse_now, z, parts, shares):
    cols, components, rows = z.shape
    share = jax.ShapeDtypeStruct((components, rows // shares), F32)
    return pl.pallas_call(
        functools.partial(mode_body, len(parts)),
        out_shape=(share,) * shares,
        in_specs=[smem()] + [vmem()] * (2 + len(parts)),
        out_specs=(vmem(),) * shares,
        scratch_shapes=[VM((components, rows), F32), VM((components, 128), F32)],
        compiler_params=params(),
        name="mode",
    )(me, inverse_now, z, *parts)


def local(tensor, first_factor, second_factor):
    frame_count, col_count, row_count = tensor.shape
    row_size, col_size = lax.axis_size("row"), lax.axis_size("col")
    every = row_size * col_size
    share_rows = row_count // col_size
    direct = share_rows % 128 == 0
    shares = col_size if direct else 1
    me = lax.axis_index("col").astype(jnp.int32).reshape(1)
    row_offsets = list(range(row_size))
    col_offsets = list(range(col_size))
    col_bits = [1 << b for b in range(col_size.bit_length() - 1)]
    row_bits = [col_size << b for b in range(row_size.bit_length() - 1)]

    def gather_rows(piece):
        if direct:
            return swaps(piece, "col", col_size, col_offsets)
        return [lax.all_gather(piece, "col", axis=1, tiled=True)]

    def scatter_rows(outs):
        if direct:
            return [outs[0]] + [swap(outs[o], "col", col_size, o) for o in col_offsets[1:]]
        return [lax.psum_scatter(outs[0], "col", scatter_dimension=1, tiled=True)]

    second_turned = second_factor.T
    first_pieces = gather_rows(first_factor)
    second_pieces = swaps(second_turned, "col", col_size, col_offsets)
    turned, wide = prepare(tensor, second_factor.astype(F32))
    first_full, gram_first = assemble(me, first_pieces, row_count)
    gram_parts = swaps(gram_first, "row", row_size, row_offsets)
    frame_part = project(first_full, second_turned.astype(F32), turned)
    inverse_first, gram_second = first_inverse(me, gram_parts, second_pieces)

    stages = [col_bits[:1] + row_bits, *(col_bits[b : b + 2] for b in range(1, len(col_bits), 2))]
    parts = [frame_part]
    for bits in stages:
        parts = swaps(tree_sum(parts), BOTH, every, offsets_of(bits))
    frames, gram_frames, z, *outs = slab(me, inverse_first, wide, turned, parts, shares)

    first_parts = scatter_rows(outs)
    inverse_second = next_inverse([gram_second], gram_frames)
    new_first = update(inverse_second, first_parts)

    full, gram_new = assemble(me, gather_rows(new_first), row_count)
    new_grams = swaps(gram_new, "row", row_size, row_offsets)
    second_parts = swaps(second(full, z), "row", row_size, row_offsets)
    inverse_third = next_inverse(new_grams, gram_frames)
    final = mode(me, inverse_third, z, second_parts, shares)
    return (frames, tree_sum(scatter_rows(final)))


def solution(mesh):
    return jax.shard_map(
        local,
        mesh=mesh,
        in_specs=(P(None, "col", "row"), P(None, ("row", "col")), P(None, "col")),
        out_specs=(P(), P(None, ("row", "col"))),
        check_vma=False,
    )
```

```python
import functools

import jax
import jax.numpy as jnp
from jax import lax
from jax.experimental import pallas as pl
from jax.experimental.pallas import tpu as pltpu
from jax.sharding import PartitionSpec as P

ridge_weight = 0.05
HIGH = lax.Precision.HIGHEST
BOTH = ("row", "col")
F32, BF16 = jnp.float32, jnp.bfloat16
VM = pltpu.VMEM
MIB = 1 << 20


def vmem():
    return pl.BlockSpec(memory_space=VM)


def hbm():
    return pl.BlockSpec(memory_space=pltpu.HBM)


def params(mib=16):
    return pltpu.CompilerParams(vmem_limit_bytes=mib * MIB)


def dot(a, b, dims, precision=None):
    return lax.dot_general(a, b, (dims, ((), ())), precision=precision, preferred_element_type=F32)


def tree_sum(values):
    while len(values) > 1:
        values = [values[n] + values[n + 1] for n in range(0, len(values), 2)]
    return values[0]


def exchange(x, axes):
    return lax.all_to_all(x, axes, 0, 0)


def prepare_body(groups, t_ref, b_ref, out_ref, wide_ref, slab, sems):
    frames, cols, _ = t_ref.shape

    def fetch(n):
        return pltpu.make_async_copy(t_ref.at[pl.ds(n * 16, 16)], slab.at[n], sems.at[n])

    for n in range(groups):
        fetch(n).start()
    for j in range(cols):
        wide_ref[j] = jnp.broadcast_to(b_ref[:, j : j + 1], wide_ref.shape[1:])
    to = lax.broadcasted_iota(jnp.int32, (256, 256), 0)
    at = lax.broadcasted_iota(jnp.int32, (256, 256), 1)
    turn = jnp.where((to // 16) + (to % 16) * 16 == at, 1.0, 0.0).astype(BF16)

    def step(n, _):
        fetch(n).wait()
        for g in range(cols // 16):
            block = slab[n, :, g * 16 : g * 16 + 16, :].reshape(256, -1)
            turned = dot(turn, block, ((1,), (0,))).astype(BF16).reshape(16, 16, -1)
            out_ref[g * 16 : g * 16 + 16, pl.ds(pl.multiple_of(n * 16, 16), 16), :] = turned
        return 0

    lax.fori_loop(0, groups, step, 0)


def prepare(tensor, second):
    frames, cols, rows = tensor.shape
    components = second.shape[0]
    groups = frames // 16
    return pl.pallas_call(
        functools.partial(prepare_body, groups),
        out_shape=(VM((cols, frames, rows), BF16), VM((cols, components, 128), F32)),
        in_specs=[hbm(), vmem()],
        out_specs=(vmem(), vmem()),
        scratch_shapes=[VM((groups, 16, cols, rows), BF16), pltpu.SemaphoreType.DMA((groups,))],
        compiler_params=params(20),
        name="prepare",
    )(tensor, second)


def copies(ref, value):
    for n in range(ref.shape[0]):
        ref[n] = value


def assemble_body(pieces_ref, others_ref, full_ref, gram_ref, other_ref):
    count, components, width = pieces_ref.shape
    for n in range(count):
        full_ref[:, n * width : n * width + width] = pieces_ref[n]
    full = full_ref[...]
    gram = dot(full, full, ((1,), (1,)))
    copies(gram_ref, jnp.concatenate([gram, gram], axis=1))
    total = jnp.zeros(other_ref.shape, F32)
    for n in range(others_ref.shape[0]):
        other = others_ref[n]
        total = total + dot(other, other, ((1,), (1,)))
    other_ref[...] = total


def assemble(pieces, others, spread):
    count, components, width = pieces.shape
    square = (components, components)
    return pl.pallas_call(
        assemble_body,
        out_shape=(
            jax.ShapeDtypeStruct((components, count * width), BF16),
            jax.ShapeDtypeStruct((spread, components, 2 * components), F32),
            jax.ShapeDtypeStruct(square, F32),
        ),
        in_specs=[vmem(), vmem()],
        out_specs=(vmem(),) * 3,
        compiler_params=params(),
        name="assemble",
    )(pieces, others)


def project_body(span, full_ref, second_ref, t_ref, out_ref, turned_ref):
    components = full_ref.shape[0]
    cols, frames, rows = t_ref.shape
    turned_ref[...] = full_ref[...].astype(F32).T.astype(BF16)
    weights = turned_ref[...]

    def step(n, total):
        block = t_ref[pl.ds(n * span, span)].reshape(span * frames, rows)
        product = dot(block, weights, ((1,), (0,))).reshape(span, frames, components)
        scale = second_ref[pl.ds(pl.multiple_of(n * span, span), span), :]
        for s in range(span):
            total = total + product[s] * scale[s : s + 1, :]
        return total

    total = lax.fori_loop(0, cols // span, step, jnp.zeros((frames, components), F32))
    out_ref[...] = total.T


def project(full, second_turned, turned):
    cols, frames, rows = turned.shape
    components = full.shape[0]
    return pl.pallas_call(
        functools.partial(project_body, 8),
        out_shape=jax.ShapeDtypeStruct((components, frames), F32),
        in_specs=[vmem()] * 3,
        out_specs=vmem(),
        scratch_shapes=[VM((rows, components), BF16)],
        compiler_params=params(),
        name="project",
    )(full, second_turned, turned)


def inverse(matrix):
    size = matrix.shape[0]
    row_at = lax.broadcasted_iota(jnp.int32, (size, size), 0)
    col_at = lax.broadcasted_iota(jnp.int32, (size, size), 1)
    matrix = matrix + jnp.where(row_at == col_at, ridge_weight, 0.0)
    for k in range(size):
        col = matrix[:, k : k + 1]
        row = matrix[k : k + 1, :]
        pivot = 1.0 / matrix[k : k + 1, k : k + 1]
        scaled = jnp.where(col_at[:1] == k, pivot, row * pivot)
        rest = jnp.where(col_at == k, 0.0, matrix) - col * scaled
        matrix = jnp.where(row_at == k, scaled, rest)
    return matrix


def inverse_body(grams_ref, other_ref, out_ref):
    gram = tree_sum([grams_ref[n] for n in range(grams_ref.shape[0])])
    out_ref[...] = inverse(gram[:, : other_ref.shape[0]] * other_ref[...])


def inverse_of(grams, other):
    return pl.pallas_call(
        inverse_body,
        out_shape=jax.ShapeDtypeStruct(other.shape, F32),
        in_specs=[vmem(), vmem()],
        out_specs=vmem(),
        compiler_params=params(),
        name="inverse",
    )(grams, other)


def spread_body(parts_ref, out_ref):
    copies(out_ref, tree_sum([parts_ref[n] for n in range(parts_ref.shape[0])]))


def spread_sum(parts):
    return pl.pallas_call(
        spread_body,
        out_shape=jax.ShapeDtypeStruct(parts.shape, F32),
        in_specs=[vmem()],
        out_specs=vmem(),
        compiler_params=params(),
        name="spread_sum",
    )(parts)


def hand_out(sum_ref, out_ref):
    count, _, width = out_ref.shape
    for n in range(count):
        out_ref[n] = sum_ref[:, n * width : n * width + width]


def slab_body(inverse_ref, sum_in_ref, wide_ref, t_ref, frames_ref, gram_ref, z_ref, out_ref, sum_ref):
    cols, _, rows = t_ref.shape
    components = inverse_ref.shape[0]
    frames = dot(inverse_ref[...], sum_in_ref[...], ((1,), (0,)), HIGH)
    frames_ref[...] = frames
    gram_ref[...] = dot(frames, frames, ((1,), (1,)), HIGH)
    high = frames.astype(BF16)
    low = (frames - high.astype(F32)).astype(BF16)
    both = jnp.concatenate([high, low], axis=0)
    span, wide = 8, 256

    def chunk(c, _):
        lanes = pl.ds(pl.multiple_of(c * wide, wide), wide)

        def step(n, total):
            for s in range(span):
                j = n * span + s
                product = dot(both, t_ref[j, :, lanes], ((1,), (0,)))
                z = product[:components] + product[components:]
                z_ref[j, :, lanes] = z
                scale = wide_ref[j]
                total = total + z * jnp.concatenate([scale, scale], axis=1)
            return total

        start = jnp.zeros((components, wide), F32)
        sum_ref[:, lanes] = lax.fori_loop(0, cols // span, step, start)
        return 0

    lax.fori_loop(0, rows // wide, chunk, 0)
    hand_out(sum_ref, out_ref)


def slab(inverse_first, frame_sum, wide, turned, shares):
    cols, frames, rows = turned.shape
    components = inverse_first.shape[0]
    return pl.pallas_call(
        slab_body,
        out_shape=(
            jax.ShapeDtypeStruct((components, frames), F32),
            jax.ShapeDtypeStruct((components, components), F32),
            VM((cols, components, rows), F32),
            jax.ShapeDtypeStruct((shares, components, rows // shares), F32),
        ),
        in_specs=[vmem()] * 4,
        out_specs=(vmem(),) * 4,
        scratch_shapes=[VM((components, rows), F32)],
        compiler_params=params(),
        name="slab",
    )(inverse_first, frame_sum, wide, turned)


def update_body(inverse_ref, parts_ref, out_ref):
    summed = tree_sum([parts_ref[n] for n in range(parts_ref.shape[0])])
    new = dot(inverse_ref[...], summed, ((1,), (0,)), HIGH).astype(BF16)
    copies(out_ref, new)


def update(inverse_now, parts, spread):
    return pl.pallas_call(
        update_body,
        out_shape=jax.ShapeDtypeStruct((spread,) + parts.shape[1:], BF16),
        in_specs=[vmem()] * 2,
        out_specs=vmem(),
        compiler_params=params(),
        name="update",
    )(inverse_now, parts)


def second_body(pieces_ref, z_ref, out_ref, full_ref):
    cols, components, rows = z_ref.shape
    count, _, width = pieces_ref.shape
    gram = jnp.zeros((components, components), F32)
    for n in range(count):
        piece = pieces_ref[n]
        gram = gram + dot(piece, piece, ((1,), (1,)))
        full_ref[:, n * width : n * width + width] = piece.astype(F32)
    lane = lax.broadcasted_iota(jnp.int32, (8, 128), 1)

    def step(n, _):
        at = pl.ds(pl.multiple_of(n * 8, 8), 8)
        mine = full_ref[at, :]
        total = jnp.zeros((8, 128), F32)
        for j in range(cols):
            product = z_ref[j, at, :] * mine
            folded = tree_sum([product[:, c * 128 : c * 128 + 128] for c in range(rows // 128)])
            total = jnp.where(lane == j, jnp.sum(folded, axis=1, keepdims=True), total)
        out_ref[0, at, :] = total
        return 0

    lax.fori_loop(0, components // 8, step, 0)
    both = jnp.concatenate([out_ref[0][:, :components], gram], axis=1)
    copies(out_ref, both)


def second(pieces, z, spread):
    cols, components, rows = z.shape
    return pl.pallas_call(
        second_body,
        out_shape=jax.ShapeDtypeStruct((spread, components, 2 * components), F32),
        in_specs=[vmem()] * 2,
        out_specs=vmem(),
        scratch_shapes=[VM((components, rows), F32)],
        compiler_params=params(),
        name="second",
    )(pieces, z)


def mode_body(parts_ref, gram_frames_ref, z_ref, out_ref, sum_ref, new_ref):
    cols, components, rows = z_ref.shape
    summed = tree_sum([parts_ref[n] for n in range(parts_ref.shape[0])])
    solver = inverse(summed[:, components:] * gram_frames_ref[...])
    new_ref[...] = dot(solver, summed, ((1,), (0,)), HIGH)

    def step(n, _):
        at = pl.ds(pl.multiple_of(n * 8, 8), 8)
        scale = new_ref[at, :]
        total = jnp.zeros((8, rows), F32)
        for j in range(cols):
            total = total + z_ref[j, at, :] * scale[:, j : j + 1]
        sum_ref[at, :] = total
        return 0

    lax.fori_loop(0, components // 8, step, 0)
    hand_out(sum_ref, out_ref)


def mode(parts, gram_frames, z, shares):
    cols, components, rows = z.shape
    return pl.pallas_call(
        mode_body,
        out_shape=jax.ShapeDtypeStruct((shares, components, rows // shares), F32),
        in_specs=[vmem()] * 3,
        out_specs=vmem(),
        scratch_shapes=[VM((components, rows), F32), VM((components, 2 * components), F32)],
        compiler_params=params(),
        name="mode",
    )(parts, gram_frames, z)


def local(tensor, first_factor, second_factor):
    frame_count, col_count, row_count = tensor.shape
    components = first_factor.shape[0]
    row_size, col_size = lax.axis_size("row"), lax.axis_size("col")
    every = row_size * col_size
    share_rows = row_count // col_size
    direct = share_rows % 128 == 0
    shares = col_size if direct else 1

    def whole(stack):
        return stack if direct else jnp.moveaxis(stack, 0, 1).reshape(1, components, row_count)

    def cut(stack):
        return stack if direct else jnp.moveaxis(stack.reshape(components, col_size, share_rows), 1, 0)

    padded = jnp.pad(second_factor, ((0, 0), (0, -col_count % 128)))
    joined = jnp.concatenate([first_factor, padded], axis=1)
    joined = exchange(jnp.broadcast_to(joined, (col_size, *joined.shape)), "col")
    turned, wide = prepare(tensor, second_factor.astype(F32))
    first_full, grams, gram_second = assemble(
        whole(joined[:, :, :share_rows]), joined[:, :, share_rows:], row_size
    )
    grams = exchange(grams, "row")
    frame_part = project(first_full, second_factor.T.astype(F32), turned)
    inverse_first = inverse_of(grams, gram_second)
    frame_parts = exchange(frame_part.reshape(every, 1, -1), BOTH)
    frame_sum = exchange(spread_sum(frame_parts), BOTH).reshape(components, frame_count)
    frames, gram_frames, z, out = slab(inverse_first, frame_sum, wide, turned, shares)

    first_parts = exchange(cut(out), "col")
    inverse_second = inverse_of(gram_second[None], gram_frames)
    new_first = exchange(update(inverse_second, first_parts, col_size), "col")
    second_parts = exchange(second(whole(new_first), z, row_size), "row")
    final = exchange(cut(mode(second_parts, gram_frames, z, shares)), "col")
    return (frames, tree_sum([final[n] for n in range(col_size)]))


def solution(mesh):
    return jax.shard_map(
        local,
        mesh=mesh,
        in_specs=(P(None, "col", "row"), P(None, ("row", "col")), P(None, "col")),
        out_specs=(P(), P(None, ("row", "col"))),
        check_vma=False,
    )
```

```python
import functools

import jax
import jax.numpy as jnp
from jax import lax
from jax.experimental import pallas as pl
from jax.experimental.pallas import tpu as pltpu
from jax.sharding import PartitionSpec as P

ridge_weight = 0.05
HIGH = lax.Precision.HIGHEST
BOTH = ("row", "col")
F32, BF16 = jnp.float32, jnp.bfloat16
VM = pltpu.VMEM
MIB = 1 << 20
GROUP = 16


def vmem():
    return pl.BlockSpec(memory_space=VM)


def anywhere():
    return pl.BlockSpec(memory_space=pl.ANY)


def smem():
    return pl.BlockSpec(memory_space=pltpu.SMEM)


def shaped(shape, dtype=F32):
    return jax.ShapeDtypeStruct(shape, dtype)


def call(body, outs, ins, operands, name, scratch=(), mib=16, us=1):
    several = isinstance(outs, tuple)
    return pl.pallas_call(
        body,
        out_shape=outs,
        in_specs=ins,
        out_specs=(vmem(),) * len(outs) if several else vmem(),
        scratch_shapes=scratch,
        compiler_params=pltpu.CompilerParams(vmem_limit_bytes=mib * MIB),
        cost_estimate=pl.CostEstimate(flops=0, bytes_accessed=int(us * 3_000_000), transcendentals=0),
        name=name,
    )(*operands)


def dot(a, b, dims, precision=None):
    return lax.dot_general(a, b, (dims, ((), ())), precision=precision, preferred_element_type=F32)


def swap(x, axes, count, offset):
    return lax.ppermute(x, axes, [(n, n ^ offset) for n in range(count)])


def join_body(a_ref, b_ref, out_ref):
    components = a_ref.shape[0]
    half = b_ref.shape[0] // 2
    out_ref[...] = jnp.zeros_like(out_ref)
    out_ref[0, :components, : a_ref.shape[1]] = a_ref[...]
    b = b_ref[...].astype(F32)
    pair = jnp.concatenate([b[:half], b[half:]], axis=1)
    pair = jnp.concatenate([pair, jnp.zeros((-half % 16, 2 * components), F32)], axis=0)
    out_ref[0, components:, :] = pair.astype(BF16)


def join(first, second_turned):
    components, half = first.shape[0], second_turned.shape[0] // 2
    height = components + half + (-half % 16)
    return call(
        join_body,
        shaped((1, height, 128), BF16),
        [vmem()] * 2,
        (first, second_turned),
        "join",
    )


def stack_body(a_ref, b_ref, after_ref, out_ref):
    del after_ref
    count = a_ref.shape[0]
    out_ref[:count] = a_ref[...]
    out_ref[count:] = b_ref[...]


def stack(a, b, after):
    shape = (2 * a.shape[0],) + a.shape[1:]
    specs = [vmem()] * 2 + [anywhere()]
    return call(stack_body, shaped(shape, a.dtype), specs, (a, b, after), "stack", us=0.2)


def add_body(a_ref, b_ref, after_ref, out_ref):
    del after_ref
    out_ref[...] = a_ref[...] + b_ref[...]


def add(a, b, after):
    specs = [vmem()] * 2 + [anywhere()]
    return call(add_body, shaped(a.shape, a.dtype), specs, (a, b, after), "add", us=0.2)


def prepare_body(at, t_ref, b_ref, after_ref, out_ref, wide_ref, slab, sems):
    del after_ref
    blocks = slab.shape[0]

    def fetch(n):
        return pltpu.make_async_copy(
            t_ref.at[pl.ds(n * GROUP, GROUP), pl.ds(at, GROUP)], slab.at[n], sems.at[n]
        )

    for n in range(blocks):
        fetch(n).start()
    for j in range(GROUP):
        wide_ref[j] = jnp.broadcast_to(b_ref[:, at + j : at + j + 1], wide_ref.shape[1:])
    to = lax.broadcasted_iota(jnp.int32, (256, 256), 0)
    of = lax.broadcasted_iota(jnp.int32, (256, 256), 1)
    turn = jnp.where((to // GROUP) + (to % GROUP) * GROUP == of, 1.0, 0.0).astype(BF16)

    def step(n, _):
        fetch(n).wait()
        block = slab[n].reshape(GROUP * GROUP, -1)
        turned = dot(turn, block, ((1,), (0,))).astype(BF16).reshape(GROUP, GROUP, -1)
        out_ref[:, pl.ds(pl.multiple_of(n * GROUP, GROUP), GROUP), :] = turned
        return 0

    lax.fori_loop(0, blocks, step, 0)


def prepare(tensor, second, at, after):
    frames, _, rows = tensor.shape
    components = second.shape[0]
    blocks = frames // GROUP
    return call(
        functools.partial(prepare_body, at),
        (VM((GROUP, frames, rows), BF16), VM((GROUP, components, 128), F32)),
        [anywhere(), vmem(), anywhere()],
        (tensor, second, after),
        "prepare",
        [VM((blocks, GROUP, GROUP, rows), BF16), pltpu.SemaphoreType.DMA((blocks,))],
        us=2,
    )


def place(at, blocks, width, full_ref):
    for offset, block in blocks:
        if len(blocks) == 1:
            full_ref[...] = block.astype(full_ref.dtype)
        else:
            lanes = pl.ds(pl.multiple_of((at ^ offset) * width, width), width)
            full_ref[:, lanes] = block.astype(full_ref.dtype)


def assemble_first_body(offsets, me_ref, *refs):
    stacks, (turned_ref, gram_ref, other_ref), (full_ref, every_ref) = refs[:-6], refs[-5:-2], refs[-2:]
    components = full_ref.shape[0]
    blocks = [s[n] for s in stacks for n in range(s.shape[0])]
    width = blocks[0].shape[1]
    place(me_ref[0], [(o, b[:components]) for o, b in zip(offsets, blocks)], width, full_ref)
    full = full_ref[...]
    gram_ref[...] = dot(full.astype(BF16), full.astype(BF16), ((1,), (1,)))
    turned_ref[...] = full.T.astype(BF16)
    height = blocks[0].shape[0] - components
    for o, b in zip(offsets, blocks):
        every_ref[pl.ds(pl.multiple_of((me_ref[0] ^ o) * height, height), height), :] = b[components:].astype(F32)
    every = every_ref[...].T.astype(BF16)
    both = dot(every, every, ((1,), (1,)))
    other_ref[...] = both[:components, :components] + both[components:, components:]


def assemble_first(me, stacks, after, offsets, components, rows):
    height = stacks[0].shape[1] - components
    square = shaped((components, components))
    return call(
        functools.partial(assemble_first_body, offsets),
        (shaped((rows, components), BF16), square, square),
        [smem()] + [vmem()] * len(stacks) + [anywhere()],
        (me, *stacks, after),
        "assemble_first",
        [VM((components, rows), F32), VM((height * len(offsets), 2 * components), F32)],
    )


def project_body(last, span, turned_ref, second_ref, t_ref, sum_ref, after_ref, out_ref):
    del after_ref
    components = turned_ref.shape[1]
    cols, frames, rows = t_ref.shape
    weights = turned_ref[...]
    total = sum_ref[...]
    for n in range(0, cols, span):
        block = t_ref[n : n + span].reshape(span * frames, rows)
        product = dot(block, weights, ((1,), (0,))).reshape(span, frames, components)
        for s in range(span):
            total = total + product[s] * second_ref[n + s : n + s + 1, :]
    out_ref[...] = total.T if last else total


def project(turned, second_turned, t, total, after, last):
    frames, components = total.shape
    shape = (components, frames) if last else (frames, components)
    return call(
        functools.partial(project_body, last, 8),
        shaped(shape),
        [vmem()] * 4 + [anywhere()],
        (turned, second_turned, t, total, after),
        "project",
        us=1.5,
    )


def eliminate(matrix, start, stop):
    size = matrix.shape[0]
    row_at = lax.broadcasted_iota(jnp.int32, (size, size), 0)
    col_at = lax.broadcasted_iota(jnp.int32, (size, size), 1)
    lane = col_at[:1]
    for k in range(start, stop, 2):
        a = jnp.broadcast_to(matrix[:, k : k + 1], matrix.shape)
        b = jnp.broadcast_to(matrix[:, k + 1 : k + 2], matrix.shape)
        inverse_a = 1.0 / a[k : k + 1]
        low = a[k + 1 : k + 2] * inverse_a
        inverse_b = 1.0 / (b[k + 1 : k + 2] - b[k : k + 1] * low)
        mine = (lane == k) | (lane == k + 1)
        p = jnp.where(mine, jnp.where(lane == k, 1.0, 0.0), matrix[k : k + 1])
        q = jnp.where(mine, jnp.where(lane == k, 0.0, 1.0), matrix[k + 1 : k + 2])
        q = (q - low * p) * inverse_b
        p = p * inverse_a - (b[k : k + 1] * inverse_a) * q
        rest = jnp.where((col_at == k) | (col_at == k + 1), 0.0, matrix) - a * p - b * q
        matrix = jnp.where(row_at == k, p, jnp.where(row_at == k + 1, q, rest))
    return matrix


def ridged(gram):
    row_at = lax.broadcasted_iota(jnp.int32, gram.shape, 0)
    col_at = lax.broadcasted_iota(jnp.int32, gram.shape, 1)
    return gram + jnp.where(row_at == col_at, ridge_weight, 0.0)


def eliminate_body(start, stop, first, *refs):
    *ins, after_ref, out_ref = refs
    del after_ref
    matrix = ridged(ins[0][...] * ins[1][...]) if first else ins[0][...]
    out_ref[...] = eliminate(matrix, start, stop)


def eliminate_part(operands, start, stop, after):
    return call(
        functools.partial(eliminate_body, start, stop, len(operands) == 2),
        shaped(operands[0].shape),
        [vmem()] * len(operands) + [anywhere()],
        (*operands, after),
        "eliminate",
    )


def halve_first(me_ref, sum_ref, keep_ref, send_ref):
    if keep_ref.shape[0] == 0:
        return
    count, _, width = keep_ref.shape
    bit = me_ref[0] & 1
    for n in range(count):
        keep_ref[n] = sum_ref[:, pl.ds(pl.multiple_of((2 * n + bit) * width, width), width)]
        send = sum_ref[:, pl.ds(pl.multiple_of((2 * n + 1 - bit) * width, width), width)]
        send_ref[n] = send.astype(send_ref.dtype)


def halve_body(shift, me_ref, keep_in, got_in, after_ref, keep_ref, send_ref):
    del after_ref
    bit = (me_ref[0] >> shift) & 1
    for n in range(keep_ref.shape[0]):
        mine, other = 2 * n + bit, 2 * n + 1 - bit
        keep_ref[n] = keep_in[mine] + got_in[mine].astype(F32)
        send_ref[n] = (keep_in[other] + got_in[other].astype(F32)).astype(send_ref.dtype)


def halve(me, keep, got, shift, after):
    shape = (keep.shape[0] // 2,) + keep.shape[1:]
    return call(
        functools.partial(halve_body, shift),
        (shaped(shape), shaped(shape, got.dtype)),
        [smem(), vmem(), vmem(), anywhere()],
        (me, keep, got, after),
        "halve",
        us=0.2,
    )


def shares_out(direct, components, rows, width, send_type):
    if not direct:
        return (shaped((components, rows)),)
    shape = (rows // width // 2, components, width)
    return (shaped(shape), shaped(shape, send_type))


def slab_body(groups, me_ref, inverse_ref, summed_ref, *refs):
    t_refs, wide_refs = refs[:groups], refs[groups : 2 * groups]
    frames_ref, gram_ref, z_ref, *outs, sum_ref = refs[2 * groups :]
    components, rows = sum_ref.shape
    frames = dot(inverse_ref[...], summed_ref[...], ((1,), (0,)), HIGH)
    frames_ref[...] = frames
    gram_ref[...] = dot(frames, frames, ((1,), (1,)), HIGH)
    high = frames.astype(BF16)
    low = (frames - high.astype(F32)).astype(BF16)
    both = jnp.concatenate([high, low], axis=0)
    wide = 256

    def chunk(c, _):
        lanes = pl.ds(pl.multiple_of(c * wide, wide), wide)
        total = jnp.zeros((components, wide), F32)
        for g in range(groups):
            t_ref, wide_ref = t_refs[g], wide_refs[g]

            def step(n, total):
                for s in range(8):
                    j = n * 8 + s
                    product = dot(both, t_ref[j, :, lanes], ((1,), (0,)))
                    z = product[:components] + product[components:]
                    z_ref[g * GROUP + j, :, lanes] = z
                    scale = wide_ref[j]
                    total = total + z * jnp.concatenate([scale, scale], axis=1)
                return total

            total = lax.fori_loop(0, GROUP // 8, step, total)
        sum_ref[:, lanes] = total
        return 0

    lax.fori_loop(0, rows // wide, chunk, 0)
    if len(outs) == 1:
        outs[0][...] = sum_ref[...]
    else:
        halve_first(me_ref, sum_ref, *outs)


def slab(me, inverse_first, frame_sum, turned, wides, width, direct):
    _, frames, rows = turned[0].shape
    components = inverse_first.shape[0]
    groups = len(turned)
    return call(
        functools.partial(slab_body, groups),
        (
            shaped((components, frames)),
            shaped((components, components)),
            VM((groups * GROUP, components, rows), F32),
        )
        + shares_out(direct, components, rows, width, F32),
        [smem()] + [vmem()] * (2 + 2 * groups),
        (me, inverse_first, frame_sum, *turned, *wides),
        "slab",
        [VM((components, rows), F32)],
        us=8,
    )


def update_body(inverse_ref, *refs):
    *parts, out_ref = refs
    for n in range(out_ref.shape[0]):
        summed = parts[0][n]
        for part in parts[1:]:
            summed = summed + part[n]
        out_ref[n] = dot(inverse_ref[...], summed, ((1,), (0,)), HIGH).astype(BF16)


def update(inverse_now, parts):
    return call(
        update_body,
        shaped(parts[0].shape, BF16),
        [vmem()] * (1 + len(parts)),
        (inverse_now, *parts),
        "update",
    )


def second_body(offsets, me_ref, *refs):
    *stacks, z_ref, out_ref, full_ref = refs
    cols, components, rows = z_ref.shape
    blocks = [s[n] for s in stacks for n in range(s.shape[0])]
    place(me_ref[0] & 3, list(zip(offsets, blocks)), blocks[0].shape[1], full_ref)
    lane = lax.broadcasted_iota(jnp.int32, (8, 128), 1)

    def step(n, _):
        at = pl.ds(pl.multiple_of(n * 8, 8), 8)
        mine = full_ref[at, :]
        total = jnp.zeros((8, 128), F32)
        for j in range(cols):
            product = z_ref[j, at, :] * mine
            folded = product[:, :128]
            for c in range(1, rows // 128):
                folded = folded + product[:, c * 128 : c * 128 + 128]
            total = jnp.where(lane == j, jnp.sum(folded, axis=1, keepdims=True), total)
        out_ref[at, :] = total
        return 0

    lax.fori_loop(0, components // 8, step, 0)
    full = full_ref[...].astype(BF16)
    gram = dot(full, full, ((1,), (1,)))
    out_ref[...] = jnp.concatenate([out_ref[:, :components], gram], axis=1)


def second(me, stacks, offsets, z):
    cols, components, rows = z.shape
    return call(
        functools.partial(second_body, offsets),
        shaped((components, 2 * components)),
        [smem()] + [vmem()] * (1 + len(stacks)),
        (me, *stacks, z),
        "second",
        [VM((components, rows), F32)],
        us=2,
    )


def mode_body(me_ref, mine_ref, got_ref, gram_frames_ref, z_ref, *refs):
    *outs, sum_ref, new_ref = refs
    cols, components, rows = z_ref.shape
    summed = mine_ref[...] + got_ref[...]
    solver = eliminate(ridged(summed[:, components:] * gram_frames_ref[...]), 0, components)
    new_ref[...] = dot(solver, summed, ((1,), (0,)), HIGH)

    def step(n, _):
        at = pl.ds(pl.multiple_of(n * 8, 8), 8)
        scale = new_ref[at, :]
        total = jnp.zeros((8, rows), F32)
        for j in range(cols):
            total = total + z_ref[j, at, :] * scale[:, j : j + 1]
        sum_ref[at, :] = total
        return 0

    lax.fori_loop(0, components // 8, step, 0)
    if len(outs) == 1:
        outs[0][...] = sum_ref[...]
    else:
        halve_first(me_ref, sum_ref, *outs)


def mode(me, mine, got, gram_frames, z, width, direct):
    cols, components, rows = z.shape
    return call(
        mode_body,
        shares_out(direct, components, rows, width, BF16),
        [smem()] + [vmem()] * 4,
        (me, mine, got, gram_frames, z),
        "mode",
        [VM((components, rows), F32), VM((components, 2 * components), F32)],
        us=5,
    )


def local(tensor, first_factor, second_factor):
    frame_count, col_count, row_count = tensor.shape
    components = first_factor.shape[0]
    row_size, col_size = lax.axis_size("row"), lax.axis_size("col")
    every = row_size * col_size
    width = row_count // col_size
    direct = width % 128 == 0 and col_size == 8
    me = lax.axis_index("col").astype(jnp.int32).reshape(1)
    col_bits = [1 << b for b in range(col_size.bit_length() - 1)]
    row_bits = [col_size << b for b in range(row_size.bit_length() - 1)]
    tensor = pltpu.with_memory_space_constraint(tensor, pltpu.HBM)
    second_values = second_factor.astype(F32)
    second_turned = second_factor.T
    groups = range(0, col_count, GROUP)

    offsets, turned, wides = [0], [], []
    if direct:
        have = join(first_factor, second_turned)
        for n, bit in enumerate((4, 2, 1)):
            got = swap(have, "col", col_size, bit)
            offsets = offsets + [o ^ bit for o in offsets]
            t, w = prepare(tensor, second_values, groups[n], have)
            turned.append(t)
            wides.append(w)
            if n < 2:
                have = stack(have, got, t)
        first_turned, gram_first, gram_second = assemble_first(me, [have, got], t, offsets, components, row_count)
    else:
        full = lax.all_gather(first_factor, "col", axis=1, tiled=True)
        others = lax.all_gather(second_factor, "col", axis=1, tiled=True)
        first_turned = full.T
        gram_first = jnp.dot(full, full.T, preferred_element_type=F32)
        gram_second = jnp.dot(others, others.T, preferred_element_type=F32)
    for at in groups[len(turned) :]:
        t, w = prepare(tensor, second_values, at, second_values)
        turned.append(t)
        wides.append(w)

    total = jnp.zeros((frame_count, components), F32)
    second_flat = second_turned.astype(F32)
    for n, t in enumerate(turned):
        after = gram_first
        if n < len(row_bits):
            got = swap(gram_first, BOTH, every, row_bits[n])
        rows_now = second_flat[n * GROUP : n * GROUP + GROUP]
        total = project(first_turned, rows_now, t, total, after, n == len(turned) - 1)
        if n < len(row_bits):
            gram_first = add(gram_first, got, total)

    state = (gram_first, gram_second)
    bits = row_bits + col_bits
    cuts = components // 4
    for n, bit in enumerate(bits):
        got = swap(total, BOTH, every, bit)
        if n < 4:
            state = (eliminate_part(state, n * cuts, n * cuts + cuts, total),)
        total = add(total, got, state[0])
    frames, gram_frames, z, *outs = slab(me, state[0], total, turned, wides, width, direct)

    state = (gram_second, gram_frames)
    if direct:
        keep, send = outs
        got = swap(send, "col", col_size, 1)
        state = (eliminate_part(state, 0, 24, send),)
        keep, send = halve(me, keep, got, 1, state[0])
        got = swap(send, "col", col_size, 2)
        state = (eliminate_part(state, 24, 44, send),)
        keep = add(keep, got, state[0])
        got = swap(keep, "col", col_size, 4)
        state = (eliminate_part(state, 44, components, keep),)
        have = update(state[0], [keep, got])
        got = swap(have, "col", col_size, 2)
        have = stack(have, got, state[0])
        got = swap(have, "col", col_size, 1)
        stacks = [have, got]
    else:
        state = (eliminate_part(state, 0, components, outs[0]),)
        summed = lax.psum_scatter(outs[0], "col", scatter_dimension=1, tiled=True)
        new = update(state[0], [summed[None]])[0]
        stacks = [lax.all_gather(new, "col", axis=1, tiled=True)[None]]
    part = second(me, stacks, offsets, z)
    for bit in row_bits[:-1]:
        part = part + swap(part, BOTH, every, bit)
    got = swap(part, BOTH, every, row_bits[-1])
    outs = mode(me, part, got, gram_frames, z, width, direct)
    if not direct:
        return (frames, lax.psum_scatter(outs[0], "col", scatter_dimension=1, tiled=True))
    keep, send = outs
    got = swap(send, "col", col_size, 1)
    keep, send = halve(me, keep, got, 1, keep)
    got = swap(send, "col", col_size, 2)
    keep, send = halve(me, keep, got, 2, keep)
    got = swap(send, "col", col_size, 4)
    return (frames, keep[0] + got[0].astype(F32))


def solution(mesh):
    return jax.shard_map(
        local,
        mesh=mesh,
        in_specs=(P(None, "col", "row"), P(None, ("row", "col")), P(None, "col")),
        out_specs=(P(), P(None, ("row", "col"))),
        check_vma=False,
    )
```

```python
import functools

import jax
import jax.numpy as jnp
from jax import lax
from jax.experimental import pallas as pl
from jax.experimental.pallas import tpu as pltpu
from jax.sharding import PartitionSpec as P

ridge_weight = 0.05
HIGH = lax.Precision.HIGHEST
BOTH = ("row", "col")
F32, BF16 = jnp.float32, jnp.bfloat16
VM = pltpu.VMEM
MIB = 1 << 20
GROUP = 16


def vmem():
    return pl.BlockSpec(memory_space=VM)


def anywhere():
    return pl.BlockSpec(memory_space=pl.ANY)


def smem():
    return pl.BlockSpec(memory_space=pltpu.SMEM)


def shaped(shape, dtype=F32):
    return jax.ShapeDtypeStruct(shape, dtype)


def call(body, outs, ins, operands, name, scratch=(), mib=16, us=1):
    several = isinstance(outs, tuple)
    return pl.pallas_call(
        body,
        out_shape=outs,
        in_specs=ins,
        out_specs=(vmem(),) * len(outs) if several else vmem(),
        scratch_shapes=scratch,
        compiler_params=pltpu.CompilerParams(vmem_limit_bytes=mib * MIB),
        cost_estimate=pl.CostEstimate(flops=0, bytes_accessed=int(us * 3_000_000), transcendentals=0),
        name=name,
    )(*operands)


def dot(a, b, dims, precision=None):
    return lax.dot_general(a, b, (dims, ((), ())), precision=precision, preferred_element_type=F32)


def swaps(x, axes, count, bits):
    offsets = [0]
    for bit in bits:
        offsets = offsets + [o ^ bit for o in offsets]
    return [swap(x, axes, count, o) for o in offsets[1:]]


def swap(x, axes, count, offset):
    return lax.ppermute(x, axes, [(n, n ^ offset) for n in range(count)])


def join_body(a_hbm, b_hbm, out_ref, turned_ref, second_ref, a_ref, b_ref, sems):
    moves = [pltpu.make_async_copy(*pair, sems.at[n]) for n, pair in enumerate(((a_hbm, a_ref), (b_hbm, b_ref)))]
    for move in moves:
        move.start()
    for move in moves:
        move.wait()
    components = a_ref.shape[0]
    half = b_ref.shape[0] // 2
    out_ref[0, :components, :] = a_ref[...]
    b = b_ref[...].astype(F32)
    turned_ref[...] = b
    second_ref[...] = jnp.zeros_like(second_ref)
    second_ref[:, : b.shape[0]] = b.T
    pair = jnp.concatenate([b[:half], b[half:]], axis=1)
    pair = jnp.concatenate([pair, jnp.zeros((-half % 16, 2 * components), F32)], axis=0)
    out_ref[0, components:, :] = pair.astype(BF16)


def join(first, second_turned):
    components, width = first.shape
    cols = second_turned.shape[0]
    height = components + cols // 2 + (-(cols // 2) % 16)
    first = pltpu.with_memory_space_constraint(first, pltpu.HBM)
    second_turned = pltpu.with_memory_space_constraint(second_turned, pltpu.HBM)
    return call(
        join_body,
        (shaped((1, height, width), BF16), shaped((cols, components)), shaped((components, 128))),
        [anywhere()] * 2,
        (first, second_turned),
        "join",
        [VM(first.shape, BF16), VM(second_turned.shape, BF16), pltpu.SemaphoreType.DMA((2,))],
    )


def stack_body(*refs):
    *parts, after_ref, out_ref = refs
    del after_ref
    at = 0
    for part in parts:
        out_ref[at : at + part.shape[0]] = part[...]
        at += part.shape[0]


def stack(parts, after):
    shape = (sum(p.shape[0] for p in parts),) + parts[0].shape[1:]
    specs = [vmem()] * len(parts) + [anywhere()]
    return call(stack_body, shaped(shape, parts[0].dtype), specs, (*parts, after), "stack", us=0.2)


def paired(values):
    while len(values) > 1:
        values = [values[n] + values[n + 1] for n in range(0, len(values), 2)]
    return values[0]


def add_body(*refs):
    *parts, after_ref, out_ref = refs
    del after_ref
    out_ref[...] = paired([p[...] for p in parts])


def add(parts, after):
    specs = [vmem()] * len(parts) + [anywhere()]
    return call(add_body, shaped(parts[0].shape), specs, (*parts, after), "add", us=0.2)


def prepare_body(at, t_ref, b_ref, after_ref, out_ref, wide_ref, token_ref, slab, sems):
    del after_ref
    blocks, _, cols, _ = slab.shape

    def fetch(n):
        return pltpu.make_async_copy(
            t_ref.at[pl.ds(n * GROUP, GROUP), pl.ds(at, cols)], slab.at[n], sems.at[n]
        )

    for n in range(blocks):
        fetch(n).start()
    token_ref[...] = jnp.zeros_like(token_ref)
    for j in range(cols):
        wide_ref[j] = jnp.broadcast_to(b_ref[:, at + j : at + j + 1], wide_ref.shape[1:])
    to = lax.broadcasted_iota(jnp.int32, (256, 256), 0)
    of = lax.broadcasted_iota(jnp.int32, (256, 256), 1)
    turn = jnp.where((to // GROUP) + (to % GROUP) * GROUP == of, 1.0, 0.0).astype(BF16)

    def step(n, _):
        fetch(n).wait()
        for g in range(0, cols, GROUP):
            block = slab[n, :, g : g + GROUP, :].reshape(GROUP * GROUP, -1)
            turned = dot(turn, block, ((1,), (0,))).astype(BF16).reshape(GROUP, GROUP, -1)
            out_ref[g : g + GROUP, pl.ds(pl.multiple_of(n * GROUP, GROUP), GROUP), :] = turned
        return 0

    lax.fori_loop(0, blocks, step, 0)


def prepare(tensor, second, at, cols, after):
    frames, _, rows = tensor.shape
    components = second.shape[0]
    blocks = frames // GROUP
    return call(
        functools.partial(prepare_body, at),
        (VM((cols, frames, rows), BF16), VM((cols, components, 128), F32), shaped((8, 128))),
        [anywhere(), vmem(), anywhere()],
        (tensor, second, after),
        "prepare",
        [VM((blocks, GROUP, cols, rows), BF16), pltpu.SemaphoreType.DMA((blocks,))],
        us=cols / 8,
    )


def place(at, blocks, width, full_ref):
    for offset, block in blocks:
        if len(blocks) == 1:
            full_ref[...] = block.astype(full_ref.dtype)
        else:
            lanes = pl.ds(pl.multiple_of((at ^ offset) * width, width), width)
            full_ref[:, lanes] = block.astype(full_ref.dtype)


def assemble_first_body(offsets, me_ref, *refs):
    stacks, (turned_ref, gram_ref, other_ref), (full_ref, every_ref) = refs[:-6], refs[-5:-2], refs[-2:]
    components = full_ref.shape[0]
    blocks = [s[n] for s in stacks for n in range(s.shape[0])]
    width = blocks[0].shape[1]
    place(me_ref[0], [(o, b[:components]) for o, b in zip(offsets, blocks)], width, full_ref)
    full = full_ref[...]
    gram_ref[...] = dot(full.astype(BF16), full.astype(BF16), ((1,), (1,)))
    turned_ref[...] = full.T.astype(BF16)
    height = blocks[0].shape[0] - components
    for o, b in zip(offsets, blocks):
        every_ref[pl.ds(pl.multiple_of((me_ref[0] ^ o) * height, height), height), :] = b[components:].astype(F32)
    every = every_ref[...].T.astype(BF16)
    both = dot(every, every, ((1,), (1,)))
    other_ref[...] = both[:components, :components] + both[components:, components:]


def assemble_first(me, stacks, after, offsets, components, rows):
    height = stacks[0].shape[1] - components
    square = shaped((components, components))
    return call(
        functools.partial(assemble_first_body, offsets),
        (shaped((rows, components), BF16), square, square),
        [smem()] + [vmem()] * len(stacks) + [anywhere()],
        (me, *stacks, after),
        "assemble_first",
        [VM((components, rows), F32), VM((height * len(offsets), 2 * components), F32)],
    )


def project_body(at, base, cols, last, span, turned_ref, second_ref, t_ref, *refs):
    *sums, after_ref, out_ref = refs
    del after_ref
    components = turned_ref.shape[1]
    _, frames, rows = t_ref.shape
    weights = turned_ref[...]

    def step(n, total):
        block = t_ref[pl.ds(base + n * span, span)].reshape(span * frames, rows)
        product = dot(block, weights, ((1,), (0,))).reshape(span, frames, components)
        scale = second_ref[pl.ds(pl.multiple_of(at + base + n * span, span), span), :]
        for s in range(span):
            total = total + product[s] * scale[s : s + 1, :]
        return total

    start = sums[0][...] if sums else jnp.zeros((frames, components), F32)
    total = lax.fori_loop(0, cols // span, step, start)
    out_ref[...] = total.T if last else total


def project(turned, second_turned, t, at, base, cols, sums, after, last):
    components, frames = turned.shape[1], t.shape[1]
    shape = (components, frames) if last else (frames, components)
    return call(
        functools.partial(project_body, at, base, cols, last, 8),
        shaped(shape),
        [vmem()] * (3 + len(sums)) + [anywhere()],
        (turned, second_turned, t, *sums, after),
        "project",
        us=cols / 10,
    )


def eliminate(matrix, start, stop):
    size = matrix.shape[0]
    row_at = lax.broadcasted_iota(jnp.int32, (size, size), 0)
    col_at = lax.broadcasted_iota(jnp.int32, (size, size), 1)
    lane = col_at[:1]
    for k in range(start, stop, 2):
        a = jnp.broadcast_to(matrix[:, k : k + 1], matrix.shape)
        b = jnp.broadcast_to(matrix[:, k + 1 : k + 2], matrix.shape)
        inverse_a = 1.0 / a[k : k + 1]
        low = a[k + 1 : k + 2] * inverse_a
        inverse_b = 1.0 / (b[k + 1 : k + 2] - b[k : k + 1] * low)
        mine = (lane == k) | (lane == k + 1)
        p = jnp.where(mine, jnp.where(lane == k, 1.0, 0.0), matrix[k : k + 1])
        q = jnp.where(mine, jnp.where(lane == k, 0.0, 1.0), matrix[k + 1 : k + 2])
        q = (q - low * p) * inverse_b
        p = p * inverse_a - (b[k : k + 1] * inverse_a) * q
        rest = jnp.where((col_at == k) | (col_at == k + 1), 0.0, matrix) - a * p - b * q
        matrix = jnp.where(row_at == k, p, jnp.where(row_at == k + 1, q, rest))
    return matrix


def ridged(gram):
    row_at = lax.broadcasted_iota(jnp.int32, gram.shape, 0)
    col_at = lax.broadcasted_iota(jnp.int32, gram.shape, 1)
    return gram + jnp.where(row_at == col_at, ridge_weight, 0.0)


def eliminate_body(start, stop, first, *refs):
    *ins, after_ref, out_ref = refs
    del after_ref
    matrix = ridged(ins[0][...] * ins[1][...]) if first else ins[0][...]
    out_ref[...] = eliminate(matrix, start, stop)


def eliminate_part(operands, start, stop, after):
    return call(
        functools.partial(eliminate_body, start, stop, len(operands) == 2),
        shaped(operands[0].shape),
        [vmem()] * len(operands) + [anywhere()],
        (*operands, after),
        "eliminate",
    )


def halve_first(me_ref, sum_ref, keep_ref, send_ref):
    if keep_ref.shape[0] == 0:
        return
    count, _, width = keep_ref.shape
    bit = me_ref[0] & 1
    for n in range(count):
        keep_ref[n] = sum_ref[:, pl.ds(pl.multiple_of((2 * n + bit) * width, width), width)]
        send = sum_ref[:, pl.ds(pl.multiple_of((2 * n + 1 - bit) * width, width), width)]
        send_ref[n] = send.astype(send_ref.dtype)


def deal_body(me_ref, keep_in, got_in, after_ref, mine_ref, *outs):
    del after_ref
    upper = me_ref[0] >> 1
    mine_ref[...] = keep_in[upper] + got_in[upper].astype(F32)
    for n, out in enumerate(outs):
        at = upper ^ (n + 1)
        out[...] = (keep_in[at] + got_in[at].astype(F32)).astype(out.dtype)


def deal(me, keep, got, after):
    count, shape = keep.shape[0], keep.shape[1:]
    return call(
        deal_body,
        (shaped(shape),) + (shaped(shape, got.dtype),) * (count - 1),
        [smem(), vmem(), vmem(), anywhere()],
        (me, keep, got, after),
        "deal",
        us=0.2,
    )


def shares_out(direct, components, rows, width, send_type):
    if not direct:
        return (shaped((components, rows)),)
    shape = (rows // width // 2, components, width)
    return (shaped(shape), shaped(shape, send_type))


def slab_body(groups, me_ref, inverse_ref, summed_ref, *refs):
    t_refs, wide_refs = refs[:groups], refs[groups : 2 * groups]
    frames_ref, gram_ref, z_ref, *outs, sum_ref = refs[2 * groups :]
    components, rows = sum_ref.shape
    frames = dot(inverse_ref[...], summed_ref[...], ((1,), (0,)), HIGH)
    frames_ref[...] = frames
    gram_ref[...] = dot(frames, frames, ((1,), (1,)), HIGH)
    high = frames.astype(BF16)
    low = (frames - high.astype(F32)).astype(BF16)
    both = jnp.concatenate([high, low], axis=0)
    wide = 256

    def chunk(c, _):
        lanes = pl.ds(pl.multiple_of(c * wide, wide), wide)
        total = jnp.zeros((components, wide), F32)
        base = 0
        for t_ref, wide_ref in zip(t_refs, wide_refs):

            def step(n, total, t_ref=t_ref, wide_ref=wide_ref, base=base):
                for s in range(8):
                    j = n * 8 + s
                    product = dot(both, t_ref[j, :, lanes], ((1,), (0,)))
                    z = product[:components] + product[components:]
                    z_ref[base + j, :, lanes] = z
                    scale = wide_ref[j]
                    total = total + z * jnp.concatenate([scale, scale], axis=1)
                return total

            total = lax.fori_loop(0, t_ref.shape[0] // 8, step, total)
            base += t_ref.shape[0]
        sum_ref[:, lanes] = total
        return 0

    lax.fori_loop(0, rows // wide, chunk, 0)
    if len(outs) == 1:
        outs[0][...] = sum_ref[...]
    else:
        halve_first(me_ref, sum_ref, *outs)


def slab(me, inverse_first, frame_sum, turned, wides, width, direct):
    _, frames, rows = turned[0].shape
    components = inverse_first.shape[0]
    groups = len(turned)
    return call(
        functools.partial(slab_body, groups),
        (
            shaped((components, frames)),
            shaped((components, components)),
            VM((sum(t.shape[0] for t in turned), components, rows), F32),
        )
        + shares_out(direct, components, rows, width, F32),
        [smem()] + [vmem()] * (2 + 2 * groups),
        (me, inverse_first, frame_sum, *turned, *wides),
        "slab",
        [VM((components, rows), F32)],
        us=8,
    )


def update_body(inverse_ref, *refs):
    *parts, out_ref = refs
    summed = paired([p[...] for p in parts])
    out_ref[0] = dot(inverse_ref[...], summed, ((1,), (0,)), HIGH).astype(BF16)


def update(inverse_now, parts):
    return call(
        update_body,
        shaped((1,) + parts[0].shape, BF16),
        [vmem()] * (1 + len(parts)),
        (inverse_now, *parts),
        "update",
    )


def second_body(offsets, me_ref, *refs):
    *stacks, z_ref, out_ref, full_ref = refs
    cols, components, rows = z_ref.shape
    blocks = [s[n] for s in stacks for n in range(s.shape[0])]
    place(me_ref[0], list(zip(offsets, blocks)), blocks[0].shape[1], full_ref)
    lane = lax.broadcasted_iota(jnp.int32, (8, 128), 1)

    def step(n, _):
        at = pl.ds(pl.multiple_of(n * 8, 8), 8)
        mine = full_ref[at, :]
        total = jnp.zeros((8, 128), F32)
        for j in range(cols):
            product = z_ref[j, at, :] * mine
            folded = product[:, :128]
            for c in range(1, rows // 128):
                folded = folded + product[:, c * 128 : c * 128 + 128]
            total = jnp.where(lane == j, jnp.sum(folded, axis=1, keepdims=True), total)
        out_ref[at, :] = total
        return 0

    lax.fori_loop(0, components // 8, step, 0)
    full = full_ref[...].astype(BF16)
    gram = dot(full, full, ((1,), (1,)))
    out_ref[...] = jnp.concatenate([out_ref[:, :components], gram], axis=1)


def second(me, stacks, offsets, z):
    cols, components, rows = z.shape
    return call(
        functools.partial(second_body, offsets),
        shaped((components, 2 * components)),
        [smem()] + [vmem()] * (1 + len(stacks)),
        (me, *stacks, z),
        "second",
        [VM((components, rows), F32)],
        us=2,
    )


def mode_body(me_ref, mine_ref, got_ref, gram_frames_ref, z_ref, *refs):
    *outs, sum_ref, new_ref = refs
    cols, components, rows = z_ref.shape
    summed = mine_ref[...] + got_ref[...]
    solver = eliminate(ridged(summed[:, components:] * gram_frames_ref[...]), 0, components)
    new_ref[...] = dot(solver, summed, ((1,), (0,)), HIGH)

    def step(n, _):
        at = pl.ds(pl.multiple_of(n * 8, 8), 8)
        scale = new_ref[at, :]
        total = jnp.zeros((8, rows), F32)
        for j in range(cols):
            total = total + z_ref[j, at, :] * scale[:, j : j + 1]
        sum_ref[at, :] = total
        return 0

    lax.fori_loop(0, components // 8, step, 0)
    if len(outs) == 1:
        outs[0][...] = sum_ref[...]
    else:
        halve_first(me_ref, sum_ref, *outs)


def mode(me, mine, got, gram_frames, z, width, direct):
    cols, components, rows = z.shape
    return call(
        mode_body,
        shares_out(direct, components, rows, width, BF16),
        [smem()] + [vmem()] * 4,
        (me, mine, got, gram_frames, z),
        "mode",
        [VM((components, rows), F32), VM((components, 2 * components), F32)],
        us=5,
    )


def local(tensor, first_factor, second_factor):
    frame_count, col_count, row_count = tensor.shape
    components = first_factor.shape[0]
    row_size, col_size = lax.axis_size("row"), lax.axis_size("col")
    every = row_size * col_size
    width = row_count // col_size
    direct = width % 128 == 0 and col_size == 8
    me = lax.axis_index("col").astype(jnp.int32).reshape(1)
    col_bits = [1 << b for b in range(col_size.bit_length() - 1)]
    row_bits = [col_size << b for b in range(row_size.bit_length() - 1)]
    tensor = pltpu.with_memory_space_constraint(tensor, pltpu.HBM)
    cuts = [(0, GROUP), (GROUP, col_count - GROUP)]

    turned, wides, gathered = [], [], []
    if direct:
        have, second_turned, second_values = join(first_factor, second_factor.T)
        token = have
        for at, cols in cuts:
            bits = [2, 4] if gathered else [1]
            gathered = [have] + swaps(have, "col", col_size, bits)
            t, w, token = prepare(tensor, second_values, at, cols, have)
            turned.append(t)
            wides.append(w)
            if len(turned) == 1:
                have = stack(gathered, token)
        first_turned, gram_first, gram_second = assemble_first(
            me, gathered, token, list(range(col_size)), components, row_count
        )
    else:
        second_turned = second_factor.T.astype(F32)
        second_values = second_factor.astype(F32)
        for at, cols in cuts:
            t, w, token = prepare(tensor, second_values, at, cols, second_values)
            turned.append(t)
            wides.append(w)
        full = lax.all_gather(first_factor, "col", axis=1, tiled=True)
        others = lax.all_gather(second_factor, "col", axis=1, tiled=True)
        first_turned = full.T
        gram_first = jnp.dot(full, full.T, preferred_element_type=F32)
        gram_second = jnp.dot(others, others.T, preferred_element_type=F32)

    pieces = [(t, at, base) for (at, cols), t in zip(cuts, turned) for base in range(0, cols, GROUP)]
    sums = []
    for n, (t, at, base) in enumerate(pieces):
        got = [swap(gram_first, BOTH, every, bit) for bit in row_bits[n : n + 1]]
        last = n == len(pieces) - 1
        sums = [project(first_turned, second_turned, t, at, base, GROUP, sums, gram_first, last)]
        if got:
            gram_first = add([gram_first, *got], sums[0])
    total = sums[0]

    state = (gram_first, gram_second)
    half = components // 2
    bits = row_bits[1:] + col_bits
    stages = [row_bits[:1]] + [bits[n : n + 2] for n in range(0, len(bits), 2)]
    for n, pair in enumerate(stages):
        got = swaps(total, BOTH, every, pair)
        if n in (1, 2):
            state = (eliminate_part(state, (n - 1) * half, n * half, total),)
        total = add([total, *got], state[0])
    frames, gram_frames, z, *outs = slab(me, state[0], total, turned, wides, width, direct)

    state = (gram_second, gram_frames)
    if direct:
        keep, send = outs
        got = swap(send, "col", col_size, 1)
        state = (eliminate_part(state, 0, half, send),)
        mine, *send = deal(me, keep, got, state[0])
        parts = [mine] + [swap(x, "col", col_size, 2 * n + 2) for n, x in enumerate(send)]
        state = (eliminate_part(state, half, components, mine),)
        new = update(state[0], parts)
        new = stack([new] + swaps(new, "col", col_size, [2, 4]), new)
        stacks = [new, swap(new, "col", col_size, 1)]
    else:
        state = (eliminate_part(state, 0, components, outs[0]),)
        summed = lax.psum_scatter(outs[0], "col", scatter_dimension=1, tiled=True)
        new = update(state[0], [summed])[0]
        stacks = [lax.all_gather(new, "col", axis=1, tiled=True)[None]]
    part = second(me, stacks, [0, 2, 4, 6, 1, 3, 5, 7], z)
    for bit in row_bits[:-1]:
        part = part + swap(part, BOTH, every, bit)
    got = swap(part, BOTH, every, row_bits[-1])
    outs = mode(me, part, got, gram_frames, z, width, direct)
    if not direct:
        return (frames, lax.psum_scatter(outs[0], "col", scatter_dimension=1, tiled=True))
    keep, send = outs
    mine, *send = deal(me, keep, swap(send, "col", col_size, 1), keep)
    parts = [swap(x, "col", col_size, 2 * n + 2) for n, x in enumerate(send)]
    return (frames, paired([mine] + [x.astype(F32) for x in parts]))


def solution(mesh):
    return jax.shard_map(
        local,
        mesh=mesh,
        in_specs=(P(None, "col", "row"), P(None, ("row", "col")), P(None, "col")),
        out_specs=(P(), P(None, ("row", "col"))),
        check_vma=False,
    )
```

```python
import functools

import jax
import jax.numpy as jnp
from jax import lax
from jax.experimental import pallas as pl
from jax.experimental.pallas import tpu as pltpu
from jax.sharding import PartitionSpec as P

ridge_weight = 0.05
HIGH = lax.Precision.HIGHEST
BOTH = ("row", "col")
F32, BF16 = jnp.float32, jnp.bfloat16
VM = pltpu.VMEM
MIB = 1 << 20
GROUP = 16


def vmem():
    return pl.BlockSpec(memory_space=VM)


def anywhere():
    return pl.BlockSpec(memory_space=pl.ANY)


def smem():
    return pl.BlockSpec(memory_space=pltpu.SMEM)


def shaped(shape, dtype=F32):
    return jax.ShapeDtypeStruct(shape, dtype)


def call(body, outs, ins, operands, name, scratch=(), mib=16, us=1):
    several = isinstance(outs, tuple)
    return pl.pallas_call(
        body,
        out_shape=outs,
        in_specs=ins,
        out_specs=(vmem(),) * len(outs) if several else vmem(),
        scratch_shapes=scratch,
        compiler_params=pltpu.CompilerParams(vmem_limit_bytes=mib * MIB),
        cost_estimate=pl.CostEstimate(flops=0, bytes_accessed=int(us * 3_000_000), transcendentals=0),
        name=name,
    )(*operands)


def dot(a, b, dims, precision=None):
    return lax.dot_general(a, b, (dims, ((), ())), precision=precision, preferred_element_type=F32)


def swaps(x, axes, count, bits):
    offsets = [0]
    for bit in bits:
        offsets = offsets + [o ^ bit for o in offsets]
    return [swap(x, axes, count, o) for o in offsets[1:]]


def swap(x, axes, count, offset):
    return lax.ppermute(x, axes, [(n, n ^ offset) for n in range(count)])


def join_body(me_ref, a_hbm, b_hbm, out_ref, turned_ref, second_ref, a_ref, b_ref, sems):
    del me_ref
    moves = [pltpu.make_async_copy(*pair, sems.at[n]) for n, pair in enumerate(((a_hbm, a_ref), (b_hbm, b_ref)))]
    for move in moves:
        move.start()
    for move in moves:
        move.wait()
    components = a_ref.shape[0]
    half = b_ref.shape[0] // 2
    out_ref[0, :components, :] = a_ref[...]
    b = b_ref[...].astype(F32)
    turned_ref[...] = b
    second_ref[...] = jnp.zeros_like(second_ref)
    second_ref[:, : b.shape[0]] = b.T
    pair = jnp.concatenate([b[:half], b[half:]], axis=1)
    pair = jnp.concatenate([pair, jnp.zeros((-half % 16, 2 * components), F32)], axis=0)
    out_ref[0, components:, :] = pair.astype(BF16)


def join(me, first, second_turned):
    components, width = first.shape
    cols = second_turned.shape[0]
    height = components + cols // 2 + (-(cols // 2) % 16)
    first = pltpu.with_memory_space_constraint(first, pltpu.HBM)
    second_turned = pltpu.with_memory_space_constraint(second_turned, pltpu.HBM)
    return call(
        join_body,
        (shaped((1, height, width), BF16), shaped((cols, components)), shaped((components, 128))),
        [smem()] + [anywhere()] * 2,
        (me, first, second_turned),
        "join",
        [VM(first.shape, BF16), VM(second_turned.shape, BF16), pltpu.SemaphoreType.DMA((2,))],
    )


def stack_body(*refs):
    *parts, after_ref, out_ref = refs
    del after_ref
    at = 0
    for part in parts:
        out_ref[at : at + part.shape[0]] = part[...]
        at += part.shape[0]


def stack(parts, after):
    shape = (sum(p.shape[0] for p in parts),) + parts[0].shape[1:]
    specs = [vmem()] * len(parts) + [anywhere()]
    return call(stack_body, shaped(shape, parts[0].dtype), specs, (*parts, after), "stack", us=0.2)


def paired(values):
    while len(values) > 1:
        values = [values[n] + values[n + 1] for n in range(0, len(values), 2)]
    return values[0]


def add_body(*refs):
    *parts, after_ref, out_ref = refs
    del after_ref
    out_ref[...] = paired([p[...] for p in parts])


def add(parts, after):
    specs = [vmem()] * len(parts) + [anywhere()]
    return call(add_body, shaped(parts[0].shape), specs, (*parts, after), "add", us=0.2)


def split_body(a_ref, b_ref, sum_ref, gram_ref):
    components = sum_ref.shape[0]
    sum_ref[...] = a_ref[:components] + b_ref[:components]
    gram_ref[...] = a_ref[components:, :components] + b_ref[components:, :components]


def split_add(a, b):
    half = a.shape[0] // 2
    outs = (shaped((half, a.shape[1])), shaped((half, half)))
    return call(split_body, outs, [vmem()] * 2, (a, b), "split_add", us=0.2)


def prepare_body(at, t_ref, b_ref, after_ref, out_ref, wide_ref, token_ref, slab, sems):
    del after_ref
    blocks, _, cols, _ = slab.shape

    def fetch(n):
        return pltpu.make_async_copy(
            t_ref.at[pl.ds(n * GROUP, GROUP), pl.ds(at, cols)], slab.at[n], sems.at[n]
        )

    for n in range(blocks):
        fetch(n).start()
    token_ref[...] = jnp.zeros_like(token_ref)
    for j in range(cols):
        wide_ref[j] = jnp.broadcast_to(b_ref[:, at + j : at + j + 1], wide_ref.shape[1:])
    to = lax.broadcasted_iota(jnp.int32, (256, 256), 0)
    of = lax.broadcasted_iota(jnp.int32, (256, 256), 1)
    turn = jnp.where((to // GROUP) + (to % GROUP) * GROUP == of, 1.0, 0.0).astype(BF16)

    def step(n, _):
        fetch(n).wait()
        for g in range(0, cols, GROUP):
            block = slab[n, :, g : g + GROUP, :].reshape(GROUP * GROUP, -1)
            turned = dot(turn, block, ((1,), (0,))).astype(BF16).reshape(GROUP, GROUP, -1)
            out_ref[g : g + GROUP, pl.ds(pl.multiple_of(n * GROUP, GROUP), GROUP), :] = turned
        return 0

    lax.fori_loop(0, blocks, step, 0)


def prepare(tensor, second, at, cols, after):
    frames, _, rows = tensor.shape
    components = second.shape[0]
    blocks = frames // GROUP
    return call(
        functools.partial(prepare_body, at),
        (VM((cols, frames, rows), BF16), VM((cols, components, 128), F32), shaped((8, 128))),
        [anywhere(), vmem(), anywhere()],
        (tensor, second, after),
        "prepare",
        [VM((blocks, GROUP, cols, rows), BF16), pltpu.SemaphoreType.DMA((blocks,))],
        us=cols / 8,
    )


def place(at, blocks, width, full_ref):
    for offset, block in blocks:
        if len(blocks) == 1:
            full_ref[...] = block.astype(full_ref.dtype)
        else:
            lanes = pl.ds(pl.multiple_of((at ^ offset) * width, width), width)
            full_ref[:, lanes] = block.astype(full_ref.dtype)


def assemble_first_body(offsets, me_ref, *refs):
    stacks, (turned_ref, gram_ref, other_ref), (full_ref, every_ref) = refs[:-6], refs[-5:-2], refs[-2:]
    components = full_ref.shape[0]
    blocks = [s[n] for s in stacks for n in range(s.shape[0])]
    width = blocks[0].shape[1]
    place(me_ref[0], [(o, b[:components]) for o, b in zip(offsets, blocks)], width, full_ref)
    full = full_ref[...]
    gram_ref[...] = dot(full.astype(BF16), full.astype(BF16), ((1,), (1,)))
    turned_ref[...] = full.T.astype(BF16)
    height = blocks[0].shape[0] - components
    for o, b in zip(offsets, blocks):
        every_ref[pl.ds(pl.multiple_of((me_ref[0] ^ o) * height, height), height), :] = b[components:].astype(F32)
    every = every_ref[...].T.astype(BF16)
    both = dot(every, every, ((1,), (1,)))
    other_ref[...] = both[:components, :components] + both[components:, components:]


def assemble_first(me, stacks, after, offsets, components, rows):
    height = stacks[0].shape[1] - components
    square = shaped((components, components))
    return call(
        functools.partial(assemble_first_body, offsets),
        (shaped((rows, components), BF16), square, square),
        [smem()] + [vmem()] * len(stacks) + [anywhere()],
        (me, *stacks, after),
        "assemble_first",
        [VM((components, rows), F32), VM((height * len(offsets), 2 * components), F32)],
    )


def project_body(span, turned_ref, second_ref, gram_ref, *refs):
    *t_refs, out_ref = refs
    components = turned_ref.shape[1]
    weights = turned_ref[...]
    total, at = 0.0, 0
    for t_ref in t_refs:
        cols, frames, rows = t_ref.shape

        def step(n, total, t_ref=t_ref, at=at):
            block = t_ref[pl.ds(n * span, span)].reshape(span * frames, rows)
            product = dot(block, weights, ((1,), (0,))).reshape(span, frames, components)
            scale = second_ref[pl.ds(pl.multiple_of(at + n * span, span), span), :]
            for s in range(span):
                total = total + product[s] * scale[s : s + 1, :]
            return total

        total = lax.fori_loop(0, cols // span, step, total + jnp.zeros((frames, components), F32))
        at += cols
    out_ref[:components] = total.T
    gram = gram_ref[...]
    out_ref[components:] = jnp.concatenate([gram, gram], axis=1)


def project(first_turned, second_turned, gram, turned):
    components, frames = first_turned.shape[1], turned[0].shape[1]
    return call(
        functools.partial(project_body, 8),
        shaped((2 * components, frames)),
        [vmem()] * (3 + len(turned)),
        (first_turned, second_turned, gram, *turned),
        "project",
        us=5,
    )


def eliminate(matrix, start, stop):
    size = matrix.shape[0]
    row_at = lax.broadcasted_iota(jnp.int32, (size, size), 0)
    col_at = lax.broadcasted_iota(jnp.int32, (size, size), 1)
    lane = col_at[:1]
    for k in range(start, stop, 2):
        a = jnp.broadcast_to(matrix[:, k : k + 1], matrix.shape)
        b = jnp.broadcast_to(matrix[:, k + 1 : k + 2], matrix.shape)
        inverse_a = 1.0 / a[k : k + 1]
        low = a[k + 1 : k + 2] * inverse_a
        inverse_b = 1.0 / (b[k + 1 : k + 2] - b[k : k + 1] * low)
        mine = (lane == k) | (lane == k + 1)
        p = jnp.where(mine, jnp.where(lane == k, 1.0, 0.0), matrix[k : k + 1])
        q = jnp.where(mine, jnp.where(lane == k, 0.0, 1.0), matrix[k + 1 : k + 2])
        q = (q - low * p) * inverse_b
        p = p * inverse_a - (b[k : k + 1] * inverse_a) * q
        rest = jnp.where((col_at == k) | (col_at == k + 1), 0.0, matrix) - a * p - b * q
        matrix = jnp.where(row_at == k, p, jnp.where(row_at == k + 1, q, rest))
    return matrix


def ridged(gram):
    row_at = lax.broadcasted_iota(jnp.int32, gram.shape, 0)
    col_at = lax.broadcasted_iota(jnp.int32, gram.shape, 1)
    return gram + jnp.where(row_at == col_at, ridge_weight, 0.0)


def eliminate_body(start, stop, first, *refs):
    *ins, after_ref, out_ref = refs
    del after_ref
    matrix = ridged(ins[0][...] * ins[1][...]) if first else ins[0][...]
    out_ref[...] = eliminate(matrix, start, stop)


def eliminate_part(operands, start, stop, after):
    return call(
        functools.partial(eliminate_body, start, stop, len(operands) == 2),
        shaped(operands[0].shape),
        [vmem()] * len(operands) + [anywhere()],
        (*operands, after),
        "eliminate",
    )


def halve_first(me_ref, sum_ref, keep_ref, send_ref):
    if keep_ref.shape[0] == 0:
        return
    count, _, width = keep_ref.shape
    bit = me_ref[0] & 1
    for n in range(count):
        keep_ref[n] = sum_ref[:, pl.ds(pl.multiple_of((2 * n + bit) * width, width), width)]
        send = sum_ref[:, pl.ds(pl.multiple_of((2 * n + 1 - bit) * width, width), width)]
        send_ref[n] = send.astype(send_ref.dtype)


def halve_body(shift, me_ref, keep_in, got_in, after_ref, keep_ref, send_ref):
    del after_ref
    bit = (me_ref[0] >> shift) & 1
    for n in range(keep_ref.shape[0]):
        mine, other = 2 * n + bit, 2 * n + 1 - bit
        keep_ref[n] = keep_in[mine] + got_in[mine].astype(F32)
        send_ref[n] = (keep_in[other] + got_in[other].astype(F32)).astype(send_ref.dtype)


def halve(me, keep, got, shift, after):
    shape = (keep.shape[0] // 2,) + keep.shape[1:]
    return call(
        functools.partial(halve_body, shift),
        (shaped(shape), shaped(shape, got.dtype)),
        [smem(), vmem(), vmem(), anywhere()],
        (me, keep, got, after),
        "halve",
        us=0.2,
    )


def deal_body(me_ref, keep_in, got_in, after_ref, mine_ref, *outs):
    del after_ref
    upper = me_ref[0] >> 1
    mine_ref[...] = keep_in[upper] + got_in[upper].astype(F32)
    for n, out in enumerate(outs):
        at = upper ^ (n + 1)
        out[...] = (keep_in[at] + got_in[at].astype(F32)).astype(out.dtype)


def deal(me, keep, got, after):
    count, shape = keep.shape[0], keep.shape[1:]
    return call(
        deal_body,
        (shaped(shape),) + (shaped(shape, got.dtype),) * (count - 1),
        [smem(), vmem(), vmem(), anywhere()],
        (me, keep, got, after),
        "deal",
        us=0.2,
    )


def shares_out(direct, components, rows, width, send_type):
    if not direct:
        return (shaped((components, rows)),)
    shape = (rows // width // 2, components, width)
    return (shaped(shape), shaped(shape, send_type))


def slab_body(groups, me_ref, inverse_ref, summed_ref, *refs):
    t_refs, wide_refs = refs[:groups], refs[groups : 2 * groups]
    frames_ref, gram_ref, z_ref, *outs, sum_ref = refs[2 * groups :]
    components, rows = sum_ref.shape
    frames = dot(inverse_ref[...], summed_ref[...], ((1,), (0,)), HIGH)
    frames_ref[...] = frames
    gram_ref[...] = dot(frames, frames, ((1,), (1,)), HIGH)
    high = frames.astype(BF16)
    low = (frames - high.astype(F32)).astype(BF16)
    none = jnp.zeros_like(high)
    both = jnp.concatenate(
        [jnp.concatenate(pair, axis=1) for pair in ((high, none), (none, high), (low, none), (none, low))], axis=0
    )
    frames_count, wide = frames.shape[1], 256

    def chunk(c, _):
        lanes = pl.ds(pl.multiple_of(c * wide, wide), wide)
        total = jnp.zeros((components, wide), F32)
        base = 0
        for t_ref, wide_ref in zip(t_refs, wide_refs):

            def step(n, total, t_ref=t_ref, wide_ref=wide_ref, base=base):
                for s in range(0, 8, 2):
                    block = t_ref[pl.ds(n * 8 + s, 2), :, lanes].reshape(2 * frames_count, wide)
                    product = dot(both, block, ((1,), (0,)))
                    product = product[: 2 * components] + product[2 * components :]
                    for h in range(2):
                        j = n * 8 + s + h
                        z = product[h * components : h * components + components]
                        z_ref[base + j, :, lanes] = z
                        scale = wide_ref[j]
                        total = total + z * jnp.concatenate([scale, scale], axis=1)
                return total

            total = lax.fori_loop(0, t_ref.shape[0] // 8, step, total)
            base += t_ref.shape[0]
        sum_ref[:, lanes] = total
        return 0

    lax.fori_loop(0, rows // wide, chunk, 0)
    if len(outs) == 1:
        outs[0][...] = sum_ref[...]
    else:
        halve_first(me_ref, sum_ref, *outs)


def slab(me, inverse_first, frame_sum, turned, wides, width, direct):
    _, frames, rows = turned[0].shape
    components = inverse_first.shape[0]
    groups = len(turned)
    return call(
        functools.partial(slab_body, groups),
        (
            shaped((components, frames)),
            shaped((components, components)),
            VM((sum(t.shape[0] for t in turned), components, rows), F32),
        )
        + shares_out(direct, components, rows, width, F32),
        [smem()] + [vmem()] * (2 + 2 * groups),
        (me, inverse_first, frame_sum, *turned, *wides),
        "slab",
        [VM((components, rows), F32)],
        us=8,
    )


def update_body(inverse_ref, *refs):
    *parts, out_ref = refs
    for n in range(out_ref.shape[0]):
        summed = paired([p[n] for p in parts])
        out_ref[n] = dot(inverse_ref[...], summed, ((1,), (0,)), HIGH).astype(BF16)


def update(inverse_now, parts):
    return call(
        update_body,
        shaped(parts[0].shape, BF16),
        [vmem()] * (1 + len(parts)),
        (inverse_now, *parts),
        "update",
    )


def second_body(offsets, me_ref, *refs):
    *stacks, z_ref, out_ref, full_ref = refs
    cols, components, rows = z_ref.shape
    blocks = [s[n] for s in stacks for n in range(s.shape[0])]
    place(me_ref[0] & 3, list(zip(offsets, blocks)), blocks[0].shape[1], full_ref)
    lane = lax.broadcasted_iota(jnp.int32, (8, 128), 1)

    def step(n, _):
        at = pl.ds(pl.multiple_of(n * 8, 8), 8)
        mine = full_ref[at, :]
        total = jnp.zeros((8, 128), F32)
        for j in range(cols):
            product = z_ref[j, at, :] * mine
            folded = product[:, :128]
            for c in range(1, rows // 128):
                folded = folded + product[:, c * 128 : c * 128 + 128]
            total = jnp.where(lane == j, jnp.sum(folded, axis=1, keepdims=True), total)
        out_ref[at, :] = total
        return 0

    lax.fori_loop(0, components // 8, step, 0)
    full = full_ref[...].astype(BF16)
    gram = dot(full, full, ((1,), (1,)))
    out_ref[...] = jnp.concatenate([out_ref[:, :components], gram], axis=1)


def second(me, stacks, offsets, z):
    cols, components, rows = z.shape
    return call(
        functools.partial(second_body, offsets),
        shaped((components, 2 * components)),
        [smem()] + [vmem()] * (1 + len(stacks)),
        (me, *stacks, z),
        "second",
        [VM((components, rows), F32)],
        us=2,
    )


def mode_body(me_ref, mine_ref, got_ref, gram_frames_ref, z_ref, *refs):
    *outs, sum_ref, new_ref = refs
    cols, components, rows = z_ref.shape
    summed = mine_ref[...] + got_ref[...]
    solver = eliminate(ridged(summed[:, components:] * gram_frames_ref[...]), 0, components)
    new_ref[...] = dot(solver, summed, ((1,), (0,)), HIGH)

    def step(n, _):
        at = pl.ds(pl.multiple_of(n * 8, 8), 8)
        scale = new_ref[at, :]
        total = jnp.zeros((8, rows), F32)
        for j in range(cols):
            total = total + z_ref[j, at, :] * scale[:, j : j + 1]
        sum_ref[at, :] = total
        return 0

    lax.fori_loop(0, components // 8, step, 0)
    if len(outs) == 1:
        outs[0][...] = sum_ref[...]
    else:
        halve_first(me_ref, sum_ref, *outs)


def mode(me, mine, got, gram_frames, z, width, direct):
    cols, components, rows = z.shape
    return call(
        mode_body,
        shares_out(direct, components, rows, width, BF16),
        [smem()] + [vmem()] * 4,
        (me, mine, got, gram_frames, z),
        "mode",
        [VM((components, rows), F32), VM((components, 2 * components), F32)],
        us=5,
    )


def local(tensor, first_factor, second_factor):
    frame_count, col_count, row_count = tensor.shape
    components = first_factor.shape[0]
    row_size, col_size = lax.axis_size("row"), lax.axis_size("col")
    every = row_size * col_size
    width = row_count // col_size
    direct = width % 128 == 0 and col_size == 8
    me = lax.axis_index("col").astype(jnp.int32).reshape(1)
    col_bits = [1 << b for b in range(col_size.bit_length() - 1)]
    row_bits = [col_size << b for b in range(row_size.bit_length() - 1)]
    tensor = pltpu.with_memory_space_constraint(tensor, pltpu.HBM)
    cuts = [(0, GROUP), (GROUP, GROUP), (2 * GROUP, col_count - 2 * GROUP)]

    turned, wides = [], []
    order = [0, 4, 2, 6, 1, 5, 3, 7]
    if direct:
        have, second_turned, second_values = join(me, first_factor, second_factor.T)
        for bit, (at, cols) in zip((4, 2, 1), cuts):
            got = swap(have, "col", col_size, bit)
            t, w, token = prepare(tensor, second_values, at, cols, have)
            turned.append(t)
            wides.append(w)
            if bit > 1:
                have = stack([have, got], token)
        first_turned, gram_first, gram_second = assemble_first(
            me, [have, got], token, order, components, row_count
        )
    else:
        second_turned = second_factor.T.astype(F32)
        second_values = second_factor.astype(F32)
        for at, cols in cuts:
            t, w, token = prepare(tensor, second_values, at, cols, second_values)
            turned.append(t)
            wides.append(w)
        full = lax.all_gather(first_factor, "col", axis=1, tiled=True)
        others = lax.all_gather(second_factor, "col", axis=1, tiled=True)
        first_turned = full.T
        gram_first = jnp.dot(full, full.T, preferred_element_type=F32)
        gram_second = jnp.dot(others, others.T, preferred_element_type=F32)

    total = project(first_turned, second_turned, gram_first, turned)
    for bit in row_bits[:-1]:
        total = add([total, swap(total, BOTH, every, bit)], total)
    total, gram_first = split_add(total, swap(total, BOTH, every, row_bits[-1]))
    state = (gram_first, gram_second)
    marks = [0, 24, 44, components]
    for n, bit in enumerate(col_bits):
        got = swap(total, BOTH, every, bit)
        if n < 3:
            state = (eliminate_part(state, marks[n], marks[n + 1], total),)
        total = add([total, got], state[0])
    frames, gram_frames, z, *outs = slab(me, state[0], total, turned, wides, width, direct)

    state = (gram_second, gram_frames)
    if direct:
        keep, send = outs
        got = swap(send, "col", col_size, 1)
        state = (eliminate_part(state, *marks[0:2], send),)
        keep, send = halve(me, keep, got, 1, state[0])
        got = swap(send, "col", col_size, 2)
        state = (eliminate_part(state, *marks[1:3], send),)
        keep = add([keep, got], state[0])
        got = swap(keep, "col", col_size, 4)
        state = (eliminate_part(state, *marks[2:4], keep),)
        new = update(state[0], [keep, got])
        new = stack([new, swap(new, "col", col_size, 2)], new)
        stacks = [new, swap(new, "col", col_size, 1)]
    else:
        state = (eliminate_part(state, 0, components, outs[0]),)
        summed = lax.psum_scatter(outs[0], "col", scatter_dimension=1, tiled=True)
        new = update(state[0], [summed[None]])[0]
        stacks = [lax.all_gather(new, "col", axis=1, tiled=True)[None]]
    part = second(me, stacks, order, z)
    for bit in row_bits[:-1]:
        part = add([part, swap(part, BOTH, every, bit)], part)
    got = swap(part, BOTH, every, row_bits[-1])
    outs = mode(me, part, got, gram_frames, z, width, direct)
    if not direct:
        return (frames, lax.psum_scatter(outs[0], "col", scatter_dimension=1, tiled=True))
    keep, send = outs
    mine, *send = deal(me, keep, swap(send, "col", col_size, 1), keep)
    parts = [swap(x, "col", col_size, 2 * n + 2) for n, x in enumerate(send)]
    return (frames, paired([mine] + [x.astype(F32) for x in parts]))


def solution(mesh):
    return jax.shard_map(
        local,
        mesh=mesh,
        in_specs=(P(None, "col", "row"), P(None, ("row", "col")), P(None, "col")),
        out_specs=(P(), P(None, ("row", "col"))),
        check_vma=False,
    )
```

```python
import functools

import jax
import jax.numpy as jnp
from jax import lax
from jax.experimental import pallas as pl
from jax.experimental.pallas import tpu as pltpu
from jax.sharding import PartitionSpec as P

ridge_weight = 0.05
HIGH = lax.Precision.HIGHEST
BOTH = ("row", "col")
F32, BF16 = jnp.float32, jnp.bfloat16
VM = pltpu.VMEM
MIB = 1 << 20
GROUP = 16


def vmem():
    return pl.BlockSpec(memory_space=VM)


def anywhere():
    return pl.BlockSpec(memory_space=pl.ANY)


def smem():
    return pl.BlockSpec(memory_space=pltpu.SMEM)


def shaped(shape, dtype=F32):
    return jax.ShapeDtypeStruct(shape, dtype)


def call(body, outs, ins, operands, name, scratch=(), mib=16, us=1):
    several = isinstance(outs, tuple)
    return pl.pallas_call(
        body,
        out_shape=outs,
        in_specs=ins,
        out_specs=(vmem(),) * len(outs) if several else vmem(),
        scratch_shapes=scratch,
        compiler_params=pltpu.CompilerParams(vmem_limit_bytes=mib * MIB),
        cost_estimate=pl.CostEstimate(flops=0, bytes_accessed=int(us * 3_000_000), transcendentals=0),
        name=name,
    )(*operands)


def dot(a, b, dims, precision=None):
    return lax.dot_general(a, b, (dims, ((), ())), precision=precision, preferred_element_type=F32)


def swaps(x, axes, count, bits):
    offsets = [0]
    for bit in bits:
        offsets = offsets + [o ^ bit for o in offsets]
    return [swap(x, axes, count, o) for o in offsets[1:]]


def swap(x, axes, count, offset, only=0):
    return lax.ppermute(x, axes, [(n, n ^ offset) for n in range(count) if n & only == only])


def join_body(me_ref, a_hbm, b_hbm, out_ref, turned_ref, second_ref, a_ref, b_ref, sems):
    del me_ref
    moves = [pltpu.make_async_copy(*pair, sems.at[n]) for n, pair in enumerate(((a_hbm, a_ref), (b_hbm, b_ref)))]
    for move in moves:
        move.start()
    for move in moves:
        move.wait()
    components = a_ref.shape[0]
    half = b_ref.shape[0] // 2
    out_ref[0, :components, :] = a_ref[...]
    b = b_ref[...].astype(F32)
    turned_ref[...] = b
    second_ref[...] = jnp.zeros_like(second_ref)
    second_ref[:, : b.shape[0]] = b.T
    pair = jnp.concatenate([b[:half], b[half:]], axis=1)
    pair = jnp.concatenate([pair, jnp.zeros((-half % 16, 2 * components), F32)], axis=0)
    out_ref[0, components:, :] = pair.astype(BF16)


def join(me, first, second_turned):
    components, width = first.shape
    cols = second_turned.shape[0]
    height = components + cols // 2 + (-(cols // 2) % 16)
    first = pltpu.with_memory_space_constraint(first, pltpu.HBM)
    second_turned = pltpu.with_memory_space_constraint(second_turned, pltpu.HBM)
    return call(
        join_body,
        (shaped((1, height, width), BF16), shaped((cols, components)), shaped((components, 128))),
        [smem()] + [anywhere()] * 2,
        (me, first, second_turned),
        "join",
        [VM(first.shape, BF16), VM(second_turned.shape, BF16), pltpu.SemaphoreType.DMA((2,))],
    )


def stack_body(*refs):
    *parts, after_ref, out_ref = refs
    del after_ref
    at = 0
    for part in parts:
        out_ref[at : at + part.shape[0]] = part[...]
        at += part.shape[0]


def stack(parts, after):
    shape = (sum(p.shape[0] for p in parts),) + parts[0].shape[1:]
    specs = [vmem()] * len(parts) + [anywhere()]
    return call(stack_body, shaped(shape, parts[0].dtype), specs, (*parts, after), "stack", us=0.2)


def paired(values):
    while len(values) > 1:
        values = [values[n] + values[n + 1] for n in range(0, len(values), 2)]
    return values[0]


def add_body(*refs):
    *parts, after_ref, out_ref = refs
    del after_ref
    out_ref[...] = paired([p[...] for p in parts])


def add(parts, after):
    specs = [vmem()] * len(parts) + [anywhere()]
    return call(add_body, shaped(parts[0].shape), specs, (*parts, after), "add", us=0.2)


def close_body(a_ref, b_ref, inverse_ref, out_ref):
    components = a_ref.shape[0]
    out_ref[:components] = a_ref[...] + b_ref[...]
    inverse = inverse_ref[...]
    out_ref[components:] = jnp.concatenate([inverse, inverse], axis=1)


def close(a, b, inverse):
    shape = (2 * a.shape[0], a.shape[1])
    return call(close_body, shaped(shape), [vmem()] * 3, (a, b, inverse), "close", us=0.2)


def choose_body(bit, me_ref, mine_ref, got_ref, sum_ref, inverse_ref):
    components = sum_ref.shape[0]
    mine = jnp.full(mine_ref.shape, me_ref[0] & bit) == bit
    chosen = jnp.where(mine, mine_ref[...], got_ref[...])
    sum_ref[...] = chosen[:components]
    inverse_ref[...] = chosen[components:, :components]


def choose(me, bit, mine, got):
    half = mine.shape[0] // 2
    outs = (shaped((half, mine.shape[1])), shaped((half, half)))
    specs = [smem(), vmem(), vmem()]
    return call(functools.partial(choose_body, bit), outs, specs, (me, mine, got), "choose", us=0.2)


def split_body(a_ref, b_ref, sum_ref, gram_ref):
    components = sum_ref.shape[0]
    sum_ref[...] = a_ref[:components] + b_ref[:components]
    gram_ref[...] = a_ref[components:, :components] + b_ref[components:, :components]


def split_add(a, b):
    half = a.shape[0] // 2
    outs = (shaped((half, a.shape[1])), shaped((half, half)))
    return call(split_body, outs, [vmem()] * 2, (a, b), "split_add", us=0.2)


def prepare_body(at, cols, here, ahead, t_ref, b_ref, after_ref, *refs):
    del after_ref
    slab_ref = refs[0] if here else None
    refs = list(refs[1:] if here else refs)
    out_ref, wide_ref, token_ref = refs[:3]
    next_ref = refs.pop(3) if ahead else None
    sems = refs[-1]
    slab_ref = slab_ref if here else refs[3]
    blocks = slab_ref.shape[0]

    def fetch(n, to_ref, start, sem):
        return pltpu.make_async_copy(
            t_ref.at[pl.ds(n * GROUP, GROUP), pl.ds(start, to_ref.shape[2])], to_ref.at[n], sems.at[sem, n]
        )

    if not here:
        for n in range(blocks):
            fetch(n, slab_ref, at, 0).start()
    if ahead:
        for n in range(blocks):
            fetch(n, next_ref, at + cols, 1).start()
    token_ref[...] = jnp.zeros_like(token_ref)
    for j in range(cols):
        wide_ref[j] = jnp.broadcast_to(b_ref[:, at + j : at + j + 1], wide_ref.shape[1:])
    to = lax.broadcasted_iota(jnp.int32, (256, 256), 0)
    of = lax.broadcasted_iota(jnp.int32, (256, 256), 1)
    turn = jnp.where((to // GROUP) + (to % GROUP) * GROUP == of, 1.0, 0.0).astype(BF16)

    def step(n, _):
        if not here:
            fetch(n, slab_ref, at, 0).wait()
        for g in range(0, cols, GROUP):
            block = slab_ref[n, :, g : g + GROUP, :].reshape(GROUP * GROUP, -1)
            turned = dot(turn, block, ((1,), (0,))).astype(BF16).reshape(GROUP, GROUP, -1)
            out_ref[g : g + GROUP, pl.ds(pl.multiple_of(n * GROUP, GROUP), GROUP), :] = turned
        return 0

    lax.fori_loop(0, blocks, step, 0)
    if ahead:
        for n in range(blocks):
            fetch(n, next_ref, at + cols, 1).wait()


def prepare(tensor, second, at, cols, fetched, next_cols, after):
    frames, _, rows = tensor.shape
    components = second.shape[0]
    blocks = frames // GROUP
    outs = (VM((cols, frames, rows), BF16), VM((cols, components, 128), F32), shaped((8, 128)))
    if next_cols:
        outs += (VM((blocks, GROUP, next_cols, rows), BF16),)
    scratch = [] if fetched else [VM((blocks, GROUP, cols, rows), BF16)]
    got = call(
        functools.partial(prepare_body, at, cols, bool(fetched), bool(next_cols)),
        outs,
        [anywhere(), vmem(), anywhere()] + [vmem()] * len(fetched),
        (tensor, second, after, *fetched),
        "prepare",
        scratch + [pltpu.SemaphoreType.DMA((2, blocks))],
        us=cols / 8,
    )
    return got[:3], list(got[3:])


def place(at, blocks, width, full_ref):
    for offset, block in blocks:
        if len(blocks) == 1:
            full_ref[...] = block.astype(full_ref.dtype)
        else:
            lanes = pl.ds(pl.multiple_of((at ^ offset) * width, width), width)
            full_ref[:, lanes] = block.astype(full_ref.dtype)


def assemble_first_body(offsets, me_ref, *refs):
    stacks, (turned_ref, gram_ref, other_ref), (full_ref, every_ref) = refs[:-6], refs[-5:-2], refs[-2:]
    components = full_ref.shape[0]
    blocks = [s[n] for s in stacks for n in range(s.shape[0])]
    width = blocks[0].shape[1]
    place(me_ref[0] & 7, [(o, b[:components]) for o, b in zip(offsets, blocks)], width, full_ref)
    full = full_ref[...]
    gram_ref[...] = dot(full.astype(BF16), full.astype(BF16), ((1,), (1,)))
    turned_ref[...] = full.T.astype(BF16)
    height = blocks[0].shape[0] - components
    for o, b in zip(offsets, blocks):
        every_ref[pl.ds(pl.multiple_of(((me_ref[0] & 7) ^ o) * height, height), height), :] = b[components:].astype(F32)
    every = every_ref[...].T.astype(BF16)
    both = dot(every, every, ((1,), (1,)))
    other_ref[...] = both[:components, :components] + both[components:, components:]


def assemble_first(me, stacks, after, offsets, components, rows):
    height = stacks[0].shape[1] - components
    square = shaped((components, components))
    return call(
        functools.partial(assemble_first_body, offsets),
        (shaped((rows, components), BF16), square, square),
        [smem()] + [vmem()] * len(stacks) + [anywhere()],
        (me, *stacks, after),
        "assemble_first",
        [VM((components, rows), F32), VM((height * len(offsets), 2 * components), F32)],
    )


def project_body(span, turned_ref, second_ref, gram_ref, *refs):
    *t_refs, out_ref = refs
    components = turned_ref.shape[1]
    weights = turned_ref[...]
    total, at = 0.0, 0
    for t_ref in t_refs:
        cols, frames, rows = t_ref.shape

        def step(n, total, t_ref=t_ref, at=at):
            block = t_ref[pl.ds(n * span, span)].reshape(span * frames, rows)
            product = dot(block, weights, ((1,), (0,))).reshape(span, frames, components)
            scale = second_ref[pl.ds(pl.multiple_of(at + n * span, span), span), :]
            for s in range(span):
                total = total + product[s] * scale[s : s + 1, :]
            return total

        total = lax.fori_loop(0, cols // span, step, total + jnp.zeros((frames, components), F32))
        at += cols
    out_ref[:components] = total.T
    gram = gram_ref[...]
    out_ref[components:] = jnp.concatenate([gram, gram], axis=1)


def project(first_turned, second_turned, gram, turned):
    components, frames = first_turned.shape[1], turned[0].shape[1]
    return call(
        functools.partial(project_body, 8),
        shaped((2 * components, frames)),
        [vmem()] * (3 + len(turned)),
        (first_turned, second_turned, gram, *turned),
        "project",
        us=5,
    )


def eliminate(matrix, start, stop):
    size = matrix.shape[0]
    row_at = lax.broadcasted_iota(jnp.int32, (size, size), 0)
    col_at = lax.broadcasted_iota(jnp.int32, (size, size), 1)
    lane = col_at[:1]
    for k in range(start, stop, 2):
        a = jnp.broadcast_to(matrix[:, k : k + 1], matrix.shape)
        b = jnp.broadcast_to(matrix[:, k + 1 : k + 2], matrix.shape)
        inverse_a = 1.0 / a[k : k + 1]
        low = a[k + 1 : k + 2] * inverse_a
        inverse_b = 1.0 / (b[k + 1 : k + 2] - b[k : k + 1] * low)
        mine = (lane == k) | (lane == k + 1)
        p = jnp.where(mine, jnp.where(lane == k, 1.0, 0.0), matrix[k : k + 1])
        q = jnp.where(mine, jnp.where(lane == k, 0.0, 1.0), matrix[k + 1 : k + 2])
        q = (q - low * p) * inverse_b
        p = p * inverse_a - (b[k : k + 1] * inverse_a) * q
        rest = jnp.where((col_at == k) | (col_at == k + 1), 0.0, matrix) - a * p - b * q
        matrix = jnp.where(row_at == k, p, jnp.where(row_at == k + 1, q, rest))
    return matrix


def ridged(gram):
    row_at = lax.broadcasted_iota(jnp.int32, gram.shape, 0)
    col_at = lax.broadcasted_iota(jnp.int32, gram.shape, 1)
    return gram + jnp.where(row_at == col_at, ridge_weight, 0.0)


def eliminate_body(start, stop, first, *refs):
    *ins, after_ref, out_ref = refs
    del after_ref
    matrix = ridged(ins[0][...] * ins[1][...]) if first else ins[0][...]
    out_ref[...] = eliminate(matrix, start, stop)


def eliminate_part(operands, start, stop, after):
    return call(
        functools.partial(eliminate_body, start, stop, len(operands) == 2),
        shaped(operands[0].shape),
        [vmem()] * len(operands) + [anywhere()],
        (*operands, after),
        "eliminate",
    )


def halve_first(me_ref, sum_ref, keep_ref, send_ref):
    if keep_ref.shape[0] == 0:
        return
    count, _, width = keep_ref.shape
    bit = me_ref[0] & 1
    for n in range(count):
        keep_ref[n] = sum_ref[:, pl.ds(pl.multiple_of((2 * n + bit) * width, width), width)]
        send = sum_ref[:, pl.ds(pl.multiple_of((2 * n + 1 - bit) * width, width), width)]
        send_ref[n] = send.astype(send_ref.dtype)


def halve_body(shift, me_ref, keep_in, got_in, after_ref, keep_ref, send_ref):
    del after_ref
    bit = (me_ref[0] >> shift) & 1
    for n in range(keep_ref.shape[0]):
        mine, other = 2 * n + bit, 2 * n + 1 - bit
        keep_ref[n] = keep_in[mine] + got_in[mine].astype(F32)
        send_ref[n] = (keep_in[other] + got_in[other].astype(F32)).astype(send_ref.dtype)


def halve(me, keep, got, shift, after):
    shape = (keep.shape[0] // 2,) + keep.shape[1:]
    return call(
        functools.partial(halve_body, shift),
        (shaped(shape), shaped(shape, got.dtype)),
        [smem(), vmem(), vmem(), anywhere()],
        (me, keep, got, after),
        "halve",
        us=0.2,
    )


def deal_body(me_ref, keep_in, got_in, after_ref, mine_ref, *outs):
    del after_ref
    upper = (me_ref[0] & 7) >> 1
    mine_ref[...] = keep_in[upper] + got_in[upper].astype(F32)
    for n, out in enumerate(outs):
        at = upper ^ (n + 1)
        out[...] = (keep_in[at] + got_in[at].astype(F32)).astype(out.dtype)


def deal(me, keep, got, after):
    count, shape = keep.shape[0], keep.shape[1:]
    return call(
        deal_body,
        (shaped(shape),) + (shaped(shape, got.dtype),) * (count - 1),
        [smem(), vmem(), vmem(), anywhere()],
        (me, keep, got, after),
        "deal",
        us=0.2,
    )


def shares_out(direct, components, rows, width, send_type):
    if not direct:
        return (shaped((components, rows)),)
    shape = (rows // width // 2, components, width)
    return (shaped(shape), shaped(shape, send_type))


def slab_body(groups, me_ref, inverse_ref, summed_ref, *refs):
    t_refs, wide_refs = refs[:groups], refs[groups : 2 * groups]
    frames_ref, gram_ref, z_ref, *outs, sum_ref = refs[2 * groups :]
    components, rows = sum_ref.shape
    frames = dot(inverse_ref[...], summed_ref[...], ((1,), (0,)), HIGH)
    frames_ref[...] = frames
    gram_ref[...] = dot(frames, frames, ((1,), (1,)), HIGH)
    high = frames.astype(BF16)
    low = (frames - high.astype(F32)).astype(BF16)
    both = jnp.concatenate([high, low], axis=1)
    wide = 256

    def chunk(c, _):
        lanes = pl.ds(pl.multiple_of(c * wide, wide), wide)
        total = jnp.zeros((components, wide), F32)
        base = 0
        for t_ref, wide_ref in zip(t_refs, wide_refs):

            def step(n, total, t_ref=t_ref, wide_ref=wide_ref, base=base):
                for s in range(8):
                    j = n * 8 + s
                    block = t_ref[j, :, lanes]
                    z = dot(both, jnp.concatenate([block, block], axis=0), ((1,), (0,)))
                    z_ref[base + j, :, lanes] = z
                    scale = wide_ref[j]
                    total = total + z * jnp.concatenate([scale, scale], axis=1)
                return total

            total = lax.fori_loop(0, t_ref.shape[0] // 8, step, total)
            base += t_ref.shape[0]
        sum_ref[:, lanes] = total
        return 0

    lax.fori_loop(0, rows // wide, chunk, 0)
    if len(outs) == 1:
        outs[0][...] = sum_ref[...]
    else:
        halve_first(me_ref, sum_ref, *outs)


def slab(me, inverse_first, frame_sum, turned, wides, width, direct):
    _, frames, rows = turned[0].shape
    components = inverse_first.shape[0]
    groups = len(turned)
    return call(
        functools.partial(slab_body, groups),
        (
            shaped((components, frames)),
            shaped((components, components)),
            VM((sum(t.shape[0] for t in turned), components, rows), F32),
        )
        + shares_out(direct, components, rows, width, F32),
        [smem()] + [vmem()] * (2 + 2 * groups),
        (me, inverse_first, frame_sum, *turned, *wides),
        "slab",
        [VM((components, rows), F32)],
        us=8,
    )


def update_body(inverse_ref, *refs):
    *parts, out_ref = refs
    for n in range(out_ref.shape[0]):
        summed = paired([p[n] for p in parts])
        out_ref[n] = dot(inverse_ref[...], summed, ((1,), (0,)), HIGH).astype(BF16)


def update(inverse_now, parts):
    return call(
        update_body,
        shaped(parts[0].shape, BF16),
        [vmem()] * (1 + len(parts)),
        (inverse_now, *parts),
        "update",
    )


def second_body(offsets, me_ref, *refs):
    *stacks, z_ref, out_ref, full_ref = refs
    cols, components, rows = z_ref.shape
    blocks = [s[n] for s in stacks for n in range(s.shape[0])]
    place(me_ref[0] & 3, list(zip(offsets, blocks)), blocks[0].shape[1], full_ref)
    lane = lax.broadcasted_iota(jnp.int32, (8, 128), 1)

    def step(n, _):
        at = pl.ds(pl.multiple_of(n * 8, 8), 8)
        mine = full_ref[at, :]
        total = jnp.zeros((8, 128), F32)
        for j in range(cols):
            product = z_ref[j, at, :] * mine
            folded = product[:, :128]
            for c in range(1, rows // 128):
                folded = folded + product[:, c * 128 : c * 128 + 128]
            total = jnp.where(lane == j, jnp.sum(folded, axis=1, keepdims=True), total)
        out_ref[at, :] = total
        return 0

    lax.fori_loop(0, components // 8, step, 0)
    full = full_ref[...].astype(BF16)
    gram = dot(full, full, ((1,), (1,)))
    out_ref[...] = jnp.concatenate([out_ref[:, :components], gram], axis=1)


def second(me, stacks, offsets, z):
    cols, components, rows = z.shape
    return call(
        functools.partial(second_body, offsets),
        shaped((components, 2 * components)),
        [smem()] + [vmem()] * (1 + len(stacks)),
        (me, *stacks, z),
        "second",
        [VM((components, rows), F32)],
        us=2,
    )


def mode_body(me_ref, mine_ref, got_ref, gram_frames_ref, z_ref, *refs):
    *outs, sum_ref, new_ref = refs
    cols, components, rows = z_ref.shape
    summed = mine_ref[...] + got_ref[...]
    solver = eliminate(ridged(summed[:, components:] * gram_frames_ref[...]), 0, components)
    new_ref[...] = dot(solver, summed, ((1,), (0,)), HIGH)

    def step(n, _):
        at = pl.ds(pl.multiple_of(n * 8, 8), 8)
        scale = new_ref[at, :]
        total = jnp.zeros((8, rows), F32)
        for j in range(cols):
            total = total + z_ref[j, at, :] * scale[:, j : j + 1]
        sum_ref[at, :] = total
        return 0

    lax.fori_loop(0, components // 8, step, 0)
    if len(outs) == 1:
        outs[0][...] = sum_ref[...]
    else:
        halve_first(me_ref, sum_ref, *outs)


def mode(me, mine, got, gram_frames, z, width, direct):
    cols, components, rows = z.shape
    return call(
        mode_body,
        shares_out(direct, components, rows, width, BF16),
        [smem()] + [vmem()] * 4,
        (me, mine, got, gram_frames, z),
        "mode",
        [VM((components, rows), F32), VM((components, 2 * components), F32)],
        us=5,
    )


def local(tensor, first_factor, second_factor):
    frame_count, col_count, row_count = tensor.shape
    components = first_factor.shape[0]
    row_size, col_size = lax.axis_size("row"), lax.axis_size("col")
    every = row_size * col_size
    width = row_count // col_size
    direct = width % 128 == 0 and col_size == 8
    me = lax.axis_index(BOTH).astype(jnp.int32).reshape(1)
    col_bits = [1 << b for b in range(col_size.bit_length() - 1)]
    row_bits = [col_size << b for b in range(row_size.bit_length() - 1)]
    tensor = pltpu.with_memory_space_constraint(tensor, pltpu.HBM)
    cuts = [(0, GROUP), (GROUP, GROUP), (2 * GROUP, col_count - 2 * GROUP)]

    turned, wides = [], []
    order = [0, 4, 2, 6, 1, 5, 3, 7]
    ends = [cols for _, cols in cuts[1:]] + [0]
    fetched = []
    if direct:
        have, second_turned, second_values = join(me, first_factor, second_factor.T)
    else:
        have = second_values = second_factor.astype(F32)
        second_turned = second_values.T
    for (at, cols), following, bit in zip(cuts, ends, (4, 2, 1)):
        if direct:
            got = swap(have, "col", col_size, bit)
        (t, w, token), fetched = prepare(tensor, second_values, at, cols, fetched, following, have)
        turned.append(t)
        wides.append(w)
        if direct and bit > 1:
            have = stack([have, got], token)
    if direct:
        first_turned, gram_first, gram_second = assemble_first(
            me, [have, got], token, order, components, row_count
        )
    else:
        full = lax.all_gather(first_factor, "col", axis=1, tiled=True)
        others = lax.all_gather(second_factor, "col", axis=1, tiled=True)
        first_turned = full.T
        gram_first = jnp.dot(full, full.T, preferred_element_type=F32)
        gram_second = jnp.dot(others, others.T, preferred_element_type=F32)

    total = project(first_turned, second_turned, gram_first, turned)
    core, upper = row_bits[0], row_bits[1:]
    total = add([total, swap(total, BOTH, every, core)], total)
    total, gram_first = split_add(total, swap(total, BOTH, every, upper[0], core))
    state = (gram_first, gram_second)
    marks = [0, 24, 44, components]
    bits = upper[1:] + col_bits
    for n, bit in enumerate(bits):
        got = swap(total, BOTH, every, bit, core)
        if n < 3:
            state = (eliminate_part(state, marks[n], marks[n + 1], total),)
        total = add([total, got], state[0]) if n < len(bits) - 1 else close(total, got, state[0])
    handed = lax.ppermute(total, BOTH, [(n, n ^ core) for n in range(every) if n & core])
    total, inverse_first = choose(me, core, total, handed)
    frames, gram_frames, z, *outs = slab(me, inverse_first, total, turned, wides, width, direct)

    state = (gram_second, gram_frames)
    if direct:
        keep, send = outs
        got = swap(send, "col", col_size, 1)
        state = (eliminate_part(state, *marks[0:2], send),)
        keep, send = halve(me, keep, got, 1, state[0])
        got = swap(send, "col", col_size, 2)
        state = (eliminate_part(state, *marks[1:3], send),)
        keep = add([keep, got], state[0])
        got = swap(keep, "col", col_size, 4)
        state = (eliminate_part(state, *marks[2:4], keep),)
        new = update(state[0], [keep, got])
        new = stack([new, swap(new, "col", col_size, 2)], new)
        stacks = [new, swap(new, "col", col_size, 1)]
    else:
        state = (eliminate_part(state, 0, components, outs[0]),)
        summed = lax.psum_scatter(outs[0], "col", scatter_dimension=1, tiled=True)
        new = update(state[0], [summed[None]])[0]
        stacks = [lax.all_gather(new, "col", axis=1, tiled=True)[None]]
    part = second(me, stacks, order, z)
    for bit in row_bits[:-1]:
        part = add([part, swap(part, BOTH, every, bit)], part)
    got = swap(part, BOTH, every, row_bits[-1])
    outs = mode(me, part, got, gram_frames, z, width, direct)
    if not direct:
        return (frames, lax.psum_scatter(outs[0], "col", scatter_dimension=1, tiled=True))
    keep, send = outs
    mine, *send = deal(me, keep, swap(send, "col", col_size, 1), keep)
    parts = [swap(x, "col", col_size, 2 * n + 2) for n, x in enumerate(send)]
    return (frames, paired([mine] + [x.astype(F32) for x in parts]))


def solution(mesh):
    return jax.shard_map(
        local,
        mesh=mesh,
        in_specs=(P(None, "col", "row"), P(None, ("row", "col")), P(None, "col")),
        out_specs=(P(), P(None, ("row", "col"))),
        check_vma=False,
    )
```

```python
import functools

import jax
import jax.numpy as jnp
from jax import lax
from jax.experimental import pallas as pl
from jax.experimental.pallas import tpu as pltpu
from jax.sharding import PartitionSpec as P

ridge_weight = 0.05
HIGH = lax.Precision.HIGHEST
BOTH = ("row", "col")
F32, BF16 = jnp.float32, jnp.bfloat16
VM = pltpu.VMEM
MIB = 1 << 20
GROUP = 16


def vmem():
    return pl.BlockSpec(memory_space=VM)


def anywhere():
    return pl.BlockSpec(memory_space=pl.ANY)


def smem():
    return pl.BlockSpec(memory_space=pltpu.SMEM)


def shaped(shape, dtype=F32):
    return jax.ShapeDtypeStruct(shape, dtype)


def call(body, outs, ins, operands, name, scratch=(), mib=16, us=1):
    several = isinstance(outs, tuple)
    return pl.pallas_call(
        body,
        out_shape=outs,
        in_specs=ins,
        out_specs=(vmem(),) * len(outs) if several else vmem(),
        scratch_shapes=scratch,
        compiler_params=pltpu.CompilerParams(vmem_limit_bytes=mib * MIB),
        cost_estimate=pl.CostEstimate(flops=0, bytes_accessed=int(us * 3_000_000), transcendentals=0),
        name=name,
    )(*operands)


def dot(a, b, dims, precision=None):
    return lax.dot_general(a, b, (dims, ((), ())), precision=precision, preferred_element_type=F32)


def swaps(x, axes, count, bits):
    offsets = [0]
    for bit in bits:
        offsets = offsets + [o ^ bit for o in offsets]
    return [swap(x, axes, count, o) for o in offsets[1:]]


def swap(x, axes, count, offset):
    return lax.ppermute(x, axes, [(n, n ^ offset) for n in range(count)])


def join_body(me_ref, a_hbm, b_hbm, out_ref, turned_ref, second_ref, a_ref, b_ref, sems):
    del me_ref
    moves = [pltpu.make_async_copy(*pair, sems.at[n]) for n, pair in enumerate(((a_hbm, a_ref), (b_hbm, b_ref)))]
    for move in moves:
        move.start()
    for move in moves:
        move.wait()
    components = a_ref.shape[0]
    half = b_ref.shape[0] // 2
    out_ref[0, :components, :] = a_ref[...]
    b = b_ref[...].astype(F32)
    turned_ref[...] = b
    second_ref[...] = jnp.zeros_like(second_ref)
    second_ref[:, : b.shape[0]] = b.T
    pair = jnp.concatenate([b[:half], b[half:]], axis=1)
    pair = jnp.concatenate([pair, jnp.zeros((-half % 16, 2 * components), F32)], axis=0)
    out_ref[0, components:, :] = pair.astype(BF16)


def join(me, first, second_turned):
    components, width = first.shape
    cols = second_turned.shape[0]
    height = components + cols // 2 + (-(cols // 2) % 16)
    first = pltpu.with_memory_space_constraint(first, pltpu.HBM)
    second_turned = pltpu.with_memory_space_constraint(second_turned, pltpu.HBM)
    return call(
        join_body,
        (shaped((1, height, width), BF16), shaped((cols, components)), shaped((components, 128))),
        [smem()] + [anywhere()] * 2,
        (me, first, second_turned),
        "join",
        [VM(first.shape, BF16), VM(second_turned.shape, BF16), pltpu.SemaphoreType.DMA((2,))],
    )


def stack_body(*refs):
    *parts, after_ref, out_ref = refs
    del after_ref
    at = 0
    for part in parts:
        out_ref[at : at + part.shape[0]] = part[...]
        at += part.shape[0]


def stack(parts, after):
    shape = (sum(p.shape[0] for p in parts),) + parts[0].shape[1:]
    specs = [vmem()] * len(parts) + [anywhere()]
    return call(stack_body, shaped(shape, parts[0].dtype), specs, (*parts, after), "stack", us=0.2)


def paired(values):
    while len(values) > 1:
        values = [values[n] + values[n + 1] for n in range(0, len(values), 2)]
    return values[0]


def add_body(*refs):
    *parts, after_ref, out_ref = refs
    del after_ref
    out_ref[...] = paired([p[...] for p in parts])


def add(parts, after):
    specs = [vmem()] * len(parts) + [anywhere()]
    return call(add_body, shaped(parts[0].shape), specs, (*parts, after), "add", us=0.2)


def split_body(a_ref, b_ref, sum_ref, gram_ref):
    components = sum_ref.shape[0]
    sum_ref[...] = a_ref[:components] + b_ref[:components]
    gram_ref[...] = a_ref[components:, :components] + b_ref[components:, :components]


def split_add(a, b):
    half = a.shape[0] // 2
    outs = (shaped((half, a.shape[1])), shaped((half, half)))
    return call(split_body, outs, [vmem()] * 2, (a, b), "split_add", us=0.2)


def prepare_body(at, cols, here, ahead, t_ref, b_ref, after_ref, *refs):
    del after_ref
    slab_ref = refs[0] if here else None
    refs = list(refs[1:] if here else refs)
    out_ref, wide_ref, token_ref = refs[:3]
    next_ref = refs.pop(3) if ahead else None
    sems = refs[-1]
    slab_ref = slab_ref if here else refs[3]
    blocks = slab_ref.shape[0]

    def fetch(n, to_ref, start, sem):
        return pltpu.make_async_copy(
            t_ref.at[pl.ds(n * GROUP, GROUP), pl.ds(start, to_ref.shape[2])], to_ref.at[n], sems.at[sem, n]
        )

    if not here:
        for n in range(blocks):
            fetch(n, slab_ref, at, 0).start()
    if ahead:
        for n in range(blocks):
            fetch(n, next_ref, at + cols, 1).start()
    token_ref[...] = jnp.zeros_like(token_ref)
    for j in range(cols):
        wide_ref[j] = jnp.broadcast_to(b_ref[:, at + j : at + j + 1], wide_ref.shape[1:])
    to = lax.broadcasted_iota(jnp.int32, (256, 256), 0)
    of = lax.broadcasted_iota(jnp.int32, (256, 256), 1)
    turn = jnp.where((to // GROUP) + (to % GROUP) * GROUP == of, 1.0, 0.0).astype(BF16)

    def step(n, _):
        if not here:
            fetch(n, slab_ref, at, 0).wait()
        for g in range(0, cols, GROUP):
            block = slab_ref[n, :, g : g + GROUP, :].reshape(GROUP * GROUP, -1)
            turned = dot(turn, block, ((1,), (0,))).astype(BF16).reshape(GROUP, GROUP, -1)
            out_ref[g : g + GROUP, pl.ds(pl.multiple_of(n * GROUP, GROUP), GROUP), :] = turned
        return 0

    lax.fori_loop(0, blocks, step, 0)
    if ahead:
        for n in range(blocks):
            fetch(n, next_ref, at + cols, 1).wait()


def prepare(tensor, second, at, cols, fetched, next_cols, after):
    frames, _, rows = tensor.shape
    components = second.shape[0]
    blocks = frames // GROUP
    outs = (VM((cols, frames, rows), BF16), VM((cols, components, 128), F32), shaped((8, 128)))
    if next_cols:
        outs += (VM((blocks, GROUP, next_cols, rows), BF16),)
    scratch = [] if fetched else [VM((blocks, GROUP, cols, rows), BF16)]
    got = call(
        functools.partial(prepare_body, at, cols, bool(fetched), bool(next_cols)),
        outs,
        [anywhere(), vmem(), anywhere()] + [vmem()] * len(fetched),
        (tensor, second, after, *fetched),
        "prepare",
        scratch + [pltpu.SemaphoreType.DMA((2, blocks))],
        us=cols / 8,
    )
    return got[:3], list(got[3:])


def place(at, blocks, width, full_ref):
    for offset, block in blocks:
        if len(blocks) == 1:
            full_ref[...] = block.astype(full_ref.dtype)
        else:
            lanes = pl.ds(pl.multiple_of((at ^ offset) * width, width), width)
            full_ref[:, lanes] = block.astype(full_ref.dtype)


def assemble_first_body(offsets, me_ref, *refs):
    stacks, (turned_ref, gram_ref, other_ref), (full_ref, every_ref) = refs[:-6], refs[-5:-2], refs[-2:]
    components = full_ref.shape[0]
    blocks = [s[n] for s in stacks for n in range(s.shape[0])]
    width = blocks[0].shape[1]
    place(me_ref[0] & 7, [(o, b[:components]) for o, b in zip(offsets, blocks)], width, full_ref)
    full = full_ref[...]
    gram_ref[...] = dot(full.astype(BF16), full.astype(BF16), ((1,), (1,)))
    turned_ref[...] = full.T.astype(BF16)
    height = blocks[0].shape[0] - components
    for o, b in zip(offsets, blocks):
        every_ref[pl.ds(pl.multiple_of(((me_ref[0] & 7) ^ o) * height, height), height), :] = b[components:].astype(F32)
    every = every_ref[...].T.astype(BF16)
    both = dot(every, every, ((1,), (1,)))
    other_ref[...] = both[:components, :components] + both[components:, components:]


def assemble_first(me, stacks, after, offsets, components, rows):
    height = stacks[0].shape[1] - components
    square = shaped((components, components))
    return call(
        functools.partial(assemble_first_body, offsets),
        (shaped((rows, components), BF16), square, square),
        [smem()] + [vmem()] * len(stacks) + [anywhere()],
        (me, *stacks, after),
        "assemble_first",
        [VM((components, rows), F32), VM((height * len(offsets), 2 * components), F32)],
    )


def project_body(span, turned_ref, second_ref, gram_ref, *refs):
    *t_refs, out_ref = refs
    components = turned_ref.shape[1]
    weights = turned_ref[...]
    total, at = 0.0, 0
    for t_ref in t_refs:
        cols, frames, rows = t_ref.shape

        def step(n, total, t_ref=t_ref, at=at):
            block = t_ref[pl.ds(n * span, span)].reshape(span * frames, rows)
            product = dot(block, weights, ((1,), (0,))).reshape(span, frames, components)
            scale = second_ref[pl.ds(pl.multiple_of(at + n * span, span), span), :]
            for s in range(span):
                total = total + product[s] * scale[s : s + 1, :]
            return total

        total = lax.fori_loop(0, cols // span, step, total + jnp.zeros((frames, components), F32))
        at += cols
    out_ref[:components] = total.T
    gram = gram_ref[...]
    out_ref[components:] = jnp.concatenate([gram, gram], axis=1)


def project(first_turned, second_turned, gram, turned):
    components, frames = first_turned.shape[1], turned[0].shape[1]
    return call(
        functools.partial(project_body, 8),
        shaped((2 * components, frames)),
        [vmem()] * (3 + len(turned)),
        (first_turned, second_turned, gram, *turned),
        "project",
        us=5,
    )


def eliminate(matrix, start, stop, span=4):
    size = matrix.shape[0]
    row_at = lax.broadcasted_iota(jnp.int32, (size, size), 0)
    col_at = lax.broadcasted_iota(jnp.int32, (size, size), 1)
    lane = col_at[:1]
    for k in range(start, stop, span):
        among = range(span)
        cols = [jnp.broadcast_to(matrix[:, k + n : k + n + 1], matrix.shape) for n in among]
        mine = (lane >= k) & (lane < k + span)
        rows = [
            jnp.where(mine, jnp.where(lane == k + m, 1.0, 0.0), matrix[k + m : k + m + 1]) for m in among
        ]
        block = [[cols[n][k + m : k + m + 1] for n in among] for m in among]
        for m in among:
            pivot = 1.0 / block[m][m]
            rows[m] = rows[m] * pivot
            for n in range(m + 1, span):
                block[m][n] = block[m][n] * pivot
            for other in among:
                if other != m:
                    factor = block[other][m]
                    rows[other] = rows[other] - factor * rows[m]
                    for n in range(m + 1, span):
                        block[other][n] = block[other][n] - factor * block[m][n]
        rest = jnp.where((col_at >= k) & (col_at < k + span), 0.0, matrix)
        taken = cols[0] * rows[0]
        for n in range(1, span):
            taken = taken + cols[n] * rows[n]
        matrix = rest - taken
        for m in among:
            matrix = jnp.where(row_at == k + m, rows[m], matrix)
    return matrix


def ridged(gram):
    row_at = lax.broadcasted_iota(jnp.int32, gram.shape, 0)
    col_at = lax.broadcasted_iota(jnp.int32, gram.shape, 1)
    return gram + jnp.where(row_at == col_at, ridge_weight, 0.0)


def eliminate_body(start, stop, first, *refs):
    *ins, after_ref, out_ref = refs
    del after_ref
    matrix = ridged(ins[0][...] * ins[1][...]) if first else ins[0][...]
    out_ref[...] = eliminate(matrix, start, stop)


def eliminate_part(operands, start, stop, after):
    return call(
        functools.partial(eliminate_body, start, stop, len(operands) == 2),
        shaped(operands[0].shape),
        [vmem()] * len(operands) + [anywhere()],
        (*operands, after),
        "eliminate",
    )


def halve_first(me_ref, sum_ref, keep_ref, send_ref):
    if keep_ref.shape[0] == 0:
        return
    count, _, width = keep_ref.shape
    bit = me_ref[0] & 1
    for n in range(count):
        keep_ref[n] = sum_ref[:, pl.ds(pl.multiple_of((2 * n + bit) * width, width), width)]
        send = sum_ref[:, pl.ds(pl.multiple_of((2 * n + 1 - bit) * width, width), width)]
        send_ref[n] = send.astype(send_ref.dtype)


def halve_body(shift, me_ref, keep_in, got_in, after_ref, keep_ref, send_ref):
    del after_ref
    bit = (me_ref[0] >> shift) & 1
    for n in range(keep_ref.shape[0]):
        mine, other = 2 * n + bit, 2 * n + 1 - bit
        keep_ref[n] = keep_in[mine] + got_in[mine].astype(F32)
        send_ref[n] = (keep_in[other] + got_in[other].astype(F32)).astype(send_ref.dtype)


def halve(me, keep, got, shift, after):
    shape = (keep.shape[0] // 2,) + keep.shape[1:]
    return call(
        functools.partial(halve_body, shift),
        (shaped(shape), shaped(shape, got.dtype)),
        [smem(), vmem(), vmem(), anywhere()],
        (me, keep, got, after),
        "halve",
        us=0.2,
    )


def shares_out(direct, components, rows, width, send_type):
    if not direct:
        return (shaped((components, rows)),)
    shape = (rows // width // 2, components, width)
    return (shaped(shape), shaped(shape, send_type))


def slab_body(groups, me_ref, inverse_ref, summed_ref, *refs):
    t_refs, wide_refs = refs[:groups], refs[groups : 2 * groups]
    frames_ref, gram_ref, z_ref, *outs, sum_ref = refs[2 * groups :]
    components, rows = sum_ref.shape
    frames = dot(inverse_ref[...], summed_ref[...], ((1,), (0,)), HIGH)
    frames_ref[...] = frames
    gram_ref[...] = dot(frames, frames, ((1,), (1,)), HIGH)
    high = frames.astype(BF16)
    none = jnp.zeros_like(high)
    both = jnp.concatenate([jnp.concatenate(pair, axis=1) for pair in ((high, none), (none, high))], axis=0)
    depth = frames.shape[1]
    wide = 256

    def chunk(c, _):
        lanes = pl.ds(pl.multiple_of(c * wide, wide), wide)
        total = jnp.zeros((components, wide), F32)
        base = 0
        for t_ref, wide_ref in zip(t_refs, wide_refs):

            def step(n, total, t_ref=t_ref, wide_ref=wide_ref, base=base):
                for s in range(0, 8, 2):
                    block = t_ref[pl.ds(n * 8 + s, 2), :, lanes].reshape(2 * depth, wide)
                    product = dot(both, block, ((1,), (0,)))
                    for h in range(2):
                        j = n * 8 + s + h
                        z = product[h * components : h * components + components]
                        z_ref[base + j, :, lanes] = z
                        scale = wide_ref[j]
                        total = total + z * jnp.concatenate([scale, scale], axis=1)
                return total

            total = lax.fori_loop(0, t_ref.shape[0] // 8, step, total)
            base += t_ref.shape[0]
        sum_ref[:, lanes] = total
        return 0

    lax.fori_loop(0, rows // wide, chunk, 0)
    if len(outs) == 1:
        outs[0][...] = sum_ref[...]
    else:
        halve_first(me_ref, sum_ref, *outs)


def slab(me, inverse_first, frame_sum, turned, wides, width, direct):
    _, frames, rows = turned[0].shape
    components = inverse_first.shape[0]
    groups = len(turned)
    return call(
        functools.partial(slab_body, groups),
        (
            shaped((components, frames)),
            shaped((components, components)),
            VM((sum(t.shape[0] for t in turned), components, rows), F32),
        )
        + shares_out(direct, components, rows, width, F32),
        [smem()] + [vmem()] * (2 + 2 * groups),
        (me, inverse_first, frame_sum, *turned, *wides),
        "slab",
        [VM((components, rows), F32)],
        us=8,
    )


def update_body(inverse_ref, *refs):
    *parts, out_ref = refs
    for n in range(out_ref.shape[0]):
        summed = paired([p[n] for p in parts])
        out_ref[n] = dot(inverse_ref[...], summed, ((1,), (0,)), HIGH).astype(BF16)


def update(inverse_now, parts):
    return call(
        update_body,
        shaped(parts[0].shape, BF16),
        [vmem()] * (1 + len(parts)),
        (inverse_now, *parts),
        "update",
    )


def second_body(offsets, me_ref, *refs):
    *stacks, z_ref, out_ref, full_ref = refs
    cols, components, rows = z_ref.shape
    blocks = [s[n] for s in stacks for n in range(s.shape[0])]
    place(me_ref[0] & 3, list(zip(offsets, blocks)), blocks[0].shape[1], full_ref)
    lane = lax.broadcasted_iota(jnp.int32, (8, 128), 1)

    def step(n, _):
        at = pl.ds(pl.multiple_of(n * 8, 8), 8)
        mine = full_ref[at, :]
        total = jnp.zeros((8, 128), F32)
        for j in range(cols):
            product = z_ref[j, at, :] * mine
            folded = product[:, :128]
            for c in range(1, rows // 128):
                folded = folded + product[:, c * 128 : c * 128 + 128]
            total = jnp.where(lane == j, jnp.sum(folded, axis=1, keepdims=True), total)
        out_ref[at, :] = total
        return 0

    lax.fori_loop(0, components // 8, step, 0)
    full = full_ref[...].astype(BF16)
    gram = dot(full, full, ((1,), (1,)))
    out_ref[...] = jnp.concatenate([out_ref[:, :components], gram], axis=1)


def second(me, stacks, offsets, z):
    cols, components, rows = z.shape
    return call(
        functools.partial(second_body, offsets),
        shaped((components, 2 * components)),
        [smem()] + [vmem()] * (1 + len(stacks)),
        (me, *stacks, z),
        "second",
        [VM((components, rows), F32)],
        us=2,
    )


def mode_body(mine_ref, got_ref, gram_frames_ref, z_ref, *refs):
    *outs, sum_ref, new_ref = refs
    cols, components, rows = z_ref.shape
    summed = mine_ref[...] + got_ref[...]
    solver = eliminate(ridged(summed[:, components:] * gram_frames_ref[...]), 0, components)
    new_ref[...] = dot(solver, summed, ((1,), (0,)), HIGH)

    def step(n, _):
        at = pl.ds(pl.multiple_of(n * 8, 8), 8)
        scale = new_ref[at, :]
        total = jnp.zeros((8, rows), F32)
        for j in range(cols):
            total = total + z_ref[j, at, :] * scale[:, j : j + 1]
        sum_ref[at, :] = total
        return 0

    lax.fori_loop(0, components // 8, step, 0)
    out_ref = outs[0]
    if out_ref.shape == sum_ref.shape:
        out_ref[...] = sum_ref[...]
    else:
        width = out_ref.shape[2]
        for n in range(out_ref.shape[0]):
            out_ref[n] = sum_ref[:, n * width : n * width + width].astype(out_ref.dtype)


def mode(mine, got, gram_frames, z, width, direct):
    cols, components, rows = z.shape
    out = shaped((rows // width, components, width), BF16) if direct else shaped((components, rows))
    return call(
        mode_body,
        out,
        [vmem()] * 4,
        (mine, got, gram_frames, z),
        "mode",
        [VM((components, rows), F32), VM((components, 2 * components), F32)],
        us=5,
    )


def local(tensor, first_factor, second_factor):
    frame_count, col_count, row_count = tensor.shape
    components = first_factor.shape[0]
    row_size, col_size = lax.axis_size("row"), lax.axis_size("col")
    every = row_size * col_size
    width = row_count // col_size
    direct = width % 128 == 0 and col_size == 8
    me = lax.axis_index(BOTH).astype(jnp.int32).reshape(1)
    col_bits = [1 << b for b in range(col_size.bit_length() - 1)]
    row_bits = [col_size << b for b in range(row_size.bit_length() - 1)]
    tensor = pltpu.with_memory_space_constraint(tensor, pltpu.HBM)
    cuts = [(0, GROUP), (GROUP, GROUP), (2 * GROUP, col_count - 2 * GROUP)]

    turned, wides = [], []
    order = [0, 4, 2, 6, 1, 5, 3, 7]
    ends = [cols for _, cols in cuts[1:]] + [0]
    fetched = []
    if direct:
        have, second_turned, second_values = join(me, first_factor, second_factor.T)
    else:
        have = second_values = second_factor.astype(F32)
        second_turned = second_values.T
    for (at, cols), following, bit in zip(cuts, ends, (4, 2, 1)):
        if direct:
            got = swap(have, "col", col_size, bit)
        (t, w, token), fetched = prepare(tensor, second_values, at, cols, fetched, following, have)
        turned.append(t)
        wides.append(w)
        if direct and bit > 1:
            have = stack([have, got], token)
    if direct:
        first_turned, gram_first, gram_second = assemble_first(
            me, [have, got], token, order, components, row_count
        )
    else:
        full = lax.all_gather(first_factor, "col", axis=1, tiled=True)
        others = lax.all_gather(second_factor, "col", axis=1, tiled=True)
        first_turned = full.T
        gram_first = jnp.dot(full, full.T, preferred_element_type=F32)
        gram_second = jnp.dot(others, others.T, preferred_element_type=F32)

    total = project(first_turned, second_turned, gram_first, turned)
    core, upper = row_bits[0], row_bits[1:]
    total = add([total, swap(total, BOTH, every, core)], total)
    total, gram_first = split_add(total, swap(total, BOTH, every, upper[0] | core))
    state = (gram_first, gram_second)
    marks = [0, 24, 44, components]
    for n, bit in enumerate(upper[1:] + col_bits):
        got = swap(total, BOTH, every, bit | core)
        if n < 3:
            state = (eliminate_part(state, marks[n], marks[n + 1], total),)
        total = add([total, got], state[0])
    frames, gram_frames, z, *outs = slab(me, state[0], total, turned, wides, width, direct)

    state = (gram_second, gram_frames)
    if direct:
        keep, send = outs
        got = swap(send, "col", col_size, 1)
        state = (eliminate_part(state, *marks[0:2], send),)
        keep, send = halve(me, keep, got, 1, state[0])
        got = swap(send, "col", col_size, 2)
        state = (eliminate_part(state, *marks[1:3], send),)
        keep = add([keep, got], state[0])
        got = swap(keep, "col", col_size, 4)
        state = (eliminate_part(state, *marks[2:4], keep),)
        new = update(state[0], [keep, got])
        new = stack([new, swap(new, "col", col_size, 2)], new)
        stacks = [new, swap(new, "col", col_size, 1)]
    else:
        state = (eliminate_part(state, 0, components, outs[0]),)
        summed = lax.psum_scatter(outs[0], "col", scatter_dimension=1, tiled=True)
        new = update(state[0], [summed[None]])[0]
        stacks = [lax.all_gather(new, "col", axis=1, tiled=True)[None]]
    part = second(me, stacks, order, z)
    part = add([part, swap(part, BOTH, every, core)], part)
    got = swap(part, BOTH, every, upper[0] | core)
    out = mode(part, got, gram_frames, z, width, direct)
    if not direct:
        return (frames, lax.psum_scatter(out, "col", scatter_dimension=1, tiled=True))
    shares = lax.all_to_all(out, "col", 0, 0)
    return (frames, paired([shares[n].astype(F32) for n in range(col_size)]))


def solution(mesh):
    return jax.shard_map(
        local,
        mesh=mesh,
        in_specs=(P(None, "col", "row"), P(None, ("row", "col")), P(None, "col")),
        out_specs=(P(), P(None, ("row", "col"))),
        check_vma=False,
    )
```

```python
import functools

import jax
import jax.numpy as jnp
from jax import lax
from jax.experimental import pallas as pl
from jax.experimental.pallas import tpu as pltpu
from jax.sharding import PartitionSpec as P

ridge_weight = 0.05
HIGH = lax.Precision.HIGHEST
BOTH = ("row", "col")
F32, BF16 = jnp.float32, jnp.bfloat16
VM = pltpu.VMEM
MIB = 1 << 20
GROUP = 16


def vmem():
    return pl.BlockSpec(memory_space=VM)


def anywhere():
    return pl.BlockSpec(memory_space=pl.ANY)


def smem():
    return pl.BlockSpec(memory_space=pltpu.SMEM)


def shaped(shape, dtype=F32):
    return jax.ShapeDtypeStruct(shape, dtype)


def call(body, outs, ins, operands, name, scratch=(), mib=16, us=1):
    several = isinstance(outs, tuple)
    return pl.pallas_call(
        body,
        out_shape=outs,
        in_specs=ins,
        out_specs=(vmem(),) * len(outs) if several else vmem(),
        scratch_shapes=scratch,
        compiler_params=pltpu.CompilerParams(vmem_limit_bytes=mib * MIB),
        cost_estimate=pl.CostEstimate(flops=0, bytes_accessed=int(us * 3_000_000), transcendentals=0),
        name=name,
    )(*operands)


def dot(a, b, dims, precision=None):
    return lax.dot_general(a, b, (dims, ((), ())), precision=precision, preferred_element_type=F32)


def swaps(x, axes, count, bits):
    offsets = [0]
    for bit in bits:
        offsets = offsets + [o ^ bit for o in offsets]
    return [swap(x, axes, count, o) for o in offsets[1:]]


def swap(x, axes, count, offset):
    return lax.ppermute(x, axes, [(n, n ^ offset) for n in range(count)])


def join_body(me_ref, a_hbm, b_hbm, out_ref, turned_ref, second_ref, a_ref, b_ref, sems):
    del me_ref
    moves = [pltpu.make_async_copy(*pair, sems.at[n]) for n, pair in enumerate(((a_hbm, a_ref), (b_hbm, b_ref)))]
    for move in moves:
        move.start()
    for move in moves:
        move.wait()
    components = a_ref.shape[0]
    half = b_ref.shape[0] // 2
    out_ref[0, :components, :] = a_ref[...]
    b = b_ref[...].astype(F32)
    turned_ref[...] = b
    second_ref[...] = jnp.zeros_like(second_ref)
    second_ref[:, : b.shape[0]] = b.T
    pair = jnp.concatenate([b[:half], b[half:]], axis=1)
    pair = jnp.concatenate([pair, jnp.zeros((-half % 16, 2 * components), F32)], axis=0)
    out_ref[0, components:, :] = pair.astype(BF16)


def join(me, first, second_turned):
    components, width = first.shape
    cols = second_turned.shape[0]
    height = components + cols // 2 + (-(cols // 2) % 16)
    first = pltpu.with_memory_space_constraint(first, pltpu.HBM)
    second_turned = pltpu.with_memory_space_constraint(second_turned, pltpu.HBM)
    return call(
        join_body,
        (shaped((1, height, width), BF16), shaped((cols, components)), shaped((components, 128))),
        [smem()] + [anywhere()] * 2,
        (me, first, second_turned),
        "join",
        [VM(first.shape, BF16), VM(second_turned.shape, BF16), pltpu.SemaphoreType.DMA((2,))],
    )


def stack_body(*refs):
    *parts, after_ref, out_ref = refs
    del after_ref
    at = 0
    for part in parts:
        out_ref[at : at + part.shape[0]] = part[...]
        at += part.shape[0]


def stack(parts, after):
    shape = (sum(p.shape[0] for p in parts),) + parts[0].shape[1:]
    specs = [vmem()] * len(parts) + [anywhere()]
    return call(stack_body, shaped(shape, parts[0].dtype), specs, (*parts, after), "stack", us=0.2)


def paired(values):
    while len(values) > 1:
        values = [values[n] + values[n + 1] for n in range(0, len(values), 2)]
    return values[0]


def add_body(*refs):
    *parts, after_ref, out_ref = refs
    del after_ref
    out_ref[...] = paired([p[...] for p in parts])


def add(parts, after):
    specs = [vmem()] * len(parts) + [anywhere()]
    return call(add_body, shaped(parts[0].shape), specs, (*parts, after), "add", us=0.2)


def split_body(a_ref, b_ref, sum_ref, gram_ref):
    components = sum_ref.shape[0]
    sum_ref[...] = a_ref[:components] + b_ref[:components]
    gram_ref[...] = a_ref[components:, :components] + b_ref[components:, :components]


def split_add(a, b):
    half = a.shape[0] // 2
    outs = (shaped((half, a.shape[1])), shaped((half, half)))
    return call(split_body, outs, [vmem()] * 2, (a, b), "split_add", us=0.2)


def prepare_body(at, cols, here, ahead, t_ref, b_ref, after_ref, *refs):
    del after_ref
    slab_ref = refs[0] if here else None
    refs = list(refs[1:] if here else refs)
    out_ref, wide_ref, token_ref = refs[:3]
    next_ref = refs.pop(3) if ahead else None
    sems = refs[-1]
    slab_ref = slab_ref if here else refs[3]
    blocks = slab_ref.shape[0]

    def fetch(n, to_ref, start, sem):
        return pltpu.make_async_copy(
            t_ref.at[pl.ds(n * GROUP, GROUP), pl.ds(start, to_ref.shape[2])], to_ref.at[n], sems.at[sem, n]
        )

    if not here:
        for n in range(blocks):
            fetch(n, slab_ref, at, 0).start()
    if ahead:
        for n in range(blocks):
            fetch(n, next_ref, at + cols, 1).start()
    token_ref[...] = jnp.zeros_like(token_ref)
    for j in range(cols):
        wide_ref[j] = jnp.broadcast_to(b_ref[:, at + j : at + j + 1], wide_ref.shape[1:])
    to = lax.broadcasted_iota(jnp.int32, (256, 256), 0)
    of = lax.broadcasted_iota(jnp.int32, (256, 256), 1)
    turn = jnp.where((to // GROUP) + (to % GROUP) * GROUP == of, 1.0, 0.0).astype(BF16)

    def step(n, _):
        if not here:
            fetch(n, slab_ref, at, 0).wait()
        for g in range(0, cols, GROUP):
            block = slab_ref[n, :, g : g + GROUP, :].reshape(GROUP * GROUP, -1)
            turned = dot(turn, block, ((1,), (0,))).astype(BF16).reshape(GROUP, GROUP, -1)
            out_ref[g : g + GROUP, pl.ds(pl.multiple_of(n * GROUP, GROUP), GROUP), :] = turned
        return 0

    lax.fori_loop(0, blocks, step, 0)
    if ahead:
        for n in range(blocks):
            fetch(n, next_ref, at + cols, 1).wait()


def prepare(tensor, second, at, cols, fetched, next_cols, after):
    frames, _, rows = tensor.shape
    components = second.shape[0]
    blocks = frames // GROUP
    outs = (VM((cols, frames, rows), BF16), VM((cols, components, 128), F32), shaped((8, 128)))
    if next_cols:
        outs += (VM((blocks, GROUP, next_cols, rows), BF16),)
    scratch = [] if fetched else [VM((blocks, GROUP, cols, rows), BF16)]
    got = call(
        functools.partial(prepare_body, at, cols, bool(fetched), bool(next_cols)),
        outs,
        [anywhere(), vmem(), anywhere()] + [vmem()] * len(fetched),
        (tensor, second, after, *fetched),
        "prepare",
        scratch + [pltpu.SemaphoreType.DMA((2, blocks))],
        us=cols / 8,
    )
    return got[:3], list(got[3:])


def place(at, blocks, width, full_ref):
    for offset, block in blocks:
        if len(blocks) == 1:
            full_ref[...] = block.astype(full_ref.dtype)
        else:
            lanes = pl.ds(pl.multiple_of((at ^ offset) * width, width), width)
            full_ref[:, lanes] = block.astype(full_ref.dtype)


def assemble_first_body(offsets, me_ref, *refs):
    stacks, (turned_ref, gram_ref, other_ref), (full_ref, every_ref) = refs[:-6], refs[-5:-2], refs[-2:]
    components = full_ref.shape[0]
    blocks = [s[n] for s in stacks for n in range(s.shape[0])]
    width = blocks[0].shape[1]
    place(me_ref[0] & 7, [(o, b[:components]) for o, b in zip(offsets, blocks)], width, full_ref)
    full = full_ref[...]
    gram_ref[...] = dot(full.astype(BF16), full.astype(BF16), ((1,), (1,)))
    turned_ref[...] = full.T.astype(BF16)
    height = blocks[0].shape[0] - components
    for o, b in zip(offsets, blocks):
        every_ref[pl.ds(pl.multiple_of(((me_ref[0] & 7) ^ o) * height, height), height), :] = b[components:].astype(F32)
    every = every_ref[...].T.astype(BF16)
    both = dot(every, every, ((1,), (1,)))
    other_ref[...] = both[:components, :components] + both[components:, components:]


def assemble_first(me, stacks, after, offsets, components, rows):
    height = stacks[0].shape[1] - components
    square = shaped((components, components))
    return call(
        functools.partial(assemble_first_body, offsets),
        (shaped((rows, components), BF16), square, square),
        [smem()] + [vmem()] * len(stacks) + [anywhere()],
        (me, *stacks, after),
        "assemble_first",
        [VM((components, rows), F32), VM((height * len(offsets), 2 * components), F32)],
    )


def project_body(span, turned_ref, second_ref, gram_ref, *refs):
    *t_refs, out_ref = refs
    components = turned_ref.shape[1]
    weights = turned_ref[...]
    total, at = 0.0, 0
    for t_ref in t_refs:
        cols, frames, rows = t_ref.shape

        def step(n, total, t_ref=t_ref, at=at):
            block = t_ref[pl.ds(n * span, span)].reshape(span * frames, rows)
            product = dot(block, weights, ((1,), (0,))).reshape(span, frames, components)
            scale = second_ref[pl.ds(pl.multiple_of(at + n * span, span), span), :]
            for s in range(span):
                total = total + product[s] * scale[s : s + 1, :]
            return total

        total = lax.fori_loop(0, cols // span, step, total + jnp.zeros((frames, components), F32))
        at += cols
    out_ref[:components] = total.T
    gram = gram_ref[...]
    out_ref[components:] = jnp.concatenate([gram, gram], axis=1)


def project(first_turned, second_turned, gram, turned):
    components, frames = first_turned.shape[1], turned[0].shape[1]
    return call(
        functools.partial(project_body, 8),
        shaped((2 * components, frames)),
        [vmem()] * (3 + len(turned)),
        (first_turned, second_turned, gram, *turned),
        "project",
        us=5,
    )


def eliminate(matrix, start, stop, span=4):
    size = matrix.shape[0]
    row_at = lax.broadcasted_iota(jnp.int32, (size, size), 0)
    col_at = lax.broadcasted_iota(jnp.int32, (size, size), 1)
    lane = col_at[:1]
    for k in range(start, stop, span):
        among = range(span)
        cols = [jnp.broadcast_to(matrix[:, k + n : k + n + 1], matrix.shape) for n in among]
        mine = (lane >= k) & (lane < k + span)
        rows = [
            jnp.where(mine, jnp.where(lane == k + m, 1.0, 0.0), matrix[k + m : k + m + 1]) for m in among
        ]
        block = [[cols[n][k + m : k + m + 1] for n in among] for m in among]
        for m in among:
            pivot = 1.0 / block[m][m]
            rows[m] = rows[m] * pivot
            for n in range(m + 1, span):
                block[m][n] = block[m][n] * pivot
            for other in among:
                if other != m:
                    factor = block[other][m]
                    rows[other] = rows[other] - factor * rows[m]
                    for n in range(m + 1, span):
                        block[other][n] = block[other][n] - factor * block[m][n]
        rest = jnp.where((col_at >= k) & (col_at < k + span), 0.0, matrix)
        taken = cols[0] * rows[0]
        for n in range(1, span):
            taken = taken + cols[n] * rows[n]
        matrix = rest - taken
        for m in among:
            matrix = jnp.where(row_at == k + m, rows[m], matrix)
    return matrix


def ridged(gram):
    row_at = lax.broadcasted_iota(jnp.int32, gram.shape, 0)
    col_at = lax.broadcasted_iota(jnp.int32, gram.shape, 1)
    return gram + jnp.where(row_at == col_at, ridge_weight, 0.0)


def eliminate_body(start, stop, first, *refs):
    *ins, after_ref, out_ref = refs
    del after_ref
    matrix = ridged(ins[0][...] * ins[1][...]) if first else ins[0][...]
    out_ref[...] = eliminate(matrix, start, stop)


def eliminate_part(operands, start, stop, after):
    return call(
        functools.partial(eliminate_body, start, stop, len(operands) == 2),
        shaped(operands[0].shape),
        [vmem()] * len(operands) + [anywhere()],
        (*operands, after),
        "eliminate",
    )


def block_lanes(me_ref, offset, upper):
    at = pl.multiple_of((((me_ref[0] & 3) ^ offset) + 4 * upper) * 128, 128)
    return pl.ds(at, 128)


def slab_body(groups, offsets, first, me_ref, *refs):
    heads, refs = refs[: 2 if first else 1], refs[2 if first else 1 :]
    t_refs, wide_refs, refs = refs[:groups], refs[groups : 2 * groups], refs[2 * groups :]
    if first:
        frames_ref, copy_ref, *refs = refs
        frames = dot(heads[0][...], heads[1][...], ((1,), (0,)), HIGH)
        frames_ref[...] = frames
        copy_ref[...] = frames
    else:
        frames = heads[0][...]
    z_ref, *outs = refs
    components, depth = frames.shape
    high = frames.astype(BF16)
    none = jnp.zeros_like(high)
    both = jnp.concatenate([jnp.concatenate(pair, axis=1) for pair in ((high, none), (none, high))], axis=0)
    wide = 256
    for place_at, (offset, out_ref) in enumerate(zip(offsets, outs)):
        lanes = [block_lanes(me_ref, offset, n) for n in range(2)]
        store = pl.ds(place_at * wide, wide)
        total = jnp.zeros((components, wide), F32)
        base = 0
        for t_ref, wide_ref in zip(t_refs, wide_refs):

            def step(n, total, t_ref=t_ref, wide_ref=wide_ref, base=base):
                for s in range(0, 8, 2):
                    rows = pl.ds(n * 8 + s, 2)
                    block = jnp.concatenate([t_ref[rows, :, at].reshape(2 * depth, 128) for at in lanes], axis=1)
                    product = dot(both, block, ((1,), (0,)))
                    for h in range(2):
                        j = n * 8 + s + h
                        z = product[h * components : h * components + components]
                        z_ref[base + j, :, store] = z
                        scale = wide_ref[j]
                        total = total + z * jnp.concatenate([scale, scale], axis=1)
                return total

            total = lax.fori_loop(0, t_ref.shape[0] // 8, step, total)
            base += t_ref.shape[0]
        for n in range(2):
            out_ref[n] = total[:, n * 128 : n * 128 + 128]


def slab(me, heads, turned, wides, offsets):
    _, frames, _ = turned[0].shape
    components = wides[0].shape[1]
    first = len(heads) == 2
    cols = sum(t.shape[0] for t in turned)
    outs = (VM((cols, components, 256 * len(offsets)), F32),) + (shaped((2, components, 128)),) * len(offsets)
    if first:
        outs = (shaped((components, frames)),) * 2 + outs
    return call(
        functools.partial(slab_body, len(turned), offsets, first),
        outs,
        [smem()] + [vmem()] * (len(heads) + 2 * len(turned)),
        (me, *heads, *turned, *wides),
        "slab",
        us=2 * len(offsets),
    )


def frames_gram_body(stop, frames_ref, other_ref, after_ref, gram_ref, out_ref):
    del after_ref
    frames = frames_ref[...]
    gram = dot(frames, frames, ((1,), (1,)), HIGH)
    gram_ref[...] = gram
    out_ref[...] = eliminate(ridged(gram * other_ref[...]), 0, stop)


def frames_gram(frames, other, stop, after):
    square = shaped(other.shape)
    return call(
        functools.partial(frames_gram_body, stop),
        (square, square),
        [vmem(), vmem(), anywhere()],
        (frames, other, after),
        "frames_gram",
        us=2,
    )


def update_body(inverse_ref, *refs):
    *parts, out_ref = refs
    for n in range(out_ref.shape[0]):
        summed = paired([p[n] for p in parts])
        out_ref[n] = dot(inverse_ref[...], summed, ((1,), (0,)), HIGH).astype(BF16)


def update(inverse_now, parts):
    return call(
        update_body,
        shaped(parts[0].shape, BF16),
        [vmem()] * (1 + len(parts)),
        (inverse_now, *parts),
        "update",
    )


def second_body(*refs):
    *stacks, kept_ref, sent_ref, out_ref, full_ref = refs
    cols, components, near = kept_ref.shape
    blocks = [s[n] for s in stacks for n in range(s.shape[0])]
    for n, block in enumerate(blocks):
        full_ref[:, n * 128 : n * 128 + 128] = block.astype(F32)
    lane = lax.broadcasted_iota(jnp.int32, (8, 128), 1)

    def step(n, _):
        at = pl.ds(pl.multiple_of(n * 8, 8), 8)
        mine = full_ref[at, :]
        total = jnp.zeros((8, 128), F32)
        for j in range(cols):
            products = kept_ref[j, at, :] * mine[:, :near], sent_ref[j, at, :] * mine[:, near:]
            folds = [p[:, c : c + 128] for p in products for c in range(0, p.shape[1], 128)]
            folded = paired(folds)
            total = jnp.where(lane == j, jnp.sum(folded, axis=1, keepdims=True), total)
        out_ref[at, :] = total
        return 0

    lax.fori_loop(0, components // 8, step, 0)
    full = full_ref[...].astype(BF16)
    gram = dot(full, full, ((1,), (1,)))
    out_ref[...] = jnp.concatenate([out_ref[:, :components], gram], axis=1)


def second(stacks, kept, sent):
    components = kept.shape[1]
    return call(
        second_body,
        shaped((components, 2 * components)),
        [vmem()] * (2 + len(stacks)),
        (*stacks, kept, sent),
        "second",
        [VM((components, kept.shape[2] + sent.shape[2]), F32)],
        us=2,
    )


def mode_sums(new_ref, parts, out_ref):
    components = new_ref.shape[0]

    def step(n, _):
        at = pl.ds(pl.multiple_of(n * 8, 8), 8)
        scale = new_ref[at, :]
        totals = [jnp.zeros((8, 256), F32) for _ in parts]
        for j in range(parts[0][0].shape[0]):
            factor = scale[:, j : j + 1]
            totals = [t + z[j, at, lane : lane + 256] * factor for t, (z, lane) in zip(totals, parts)]
        for p, total in enumerate(totals):
            for h in range(2):
                out_ref[2 * p + h, at, :] = total[:, h * 128 : h * 128 + 128]
        return 0

    lax.fori_loop(0, components // 8, step, 0)


def mode_send_body(mine_ref, got_ref, gram_frames_ref, sent_ref, new_ref, out_ref, sums_ref):
    components = new_ref.shape[0]
    summed = mine_ref[...] + got_ref[...]
    solver = eliminate(ridged(summed[:, components:] * gram_frames_ref[...]), 0, components)
    new_ref[...] = dot(solver, summed, ((1,), (0,)), HIGH)
    mode_sums(new_ref, [(sent_ref, 0), (sent_ref, 512)], sums_ref)
    out_ref[...] = sums_ref[...].astype(out_ref.dtype)


def mode_send(mine, got, gram_frames, sent, kind):
    components = sent.shape[1]
    shape = (4, components, 128)
    return call(
        mode_send_body,
        (shaped((components, 2 * components)), shaped(shape, kind)),
        [vmem()] * 4,
        (mine, got, gram_frames, sent),
        "mode_send",
        [VM(shape, F32)],
        us=4,
    )


def mode_keep_body(new_ref, kept_ref, sent_ref, after_ref, out_ref):
    del after_ref
    mode_sums(new_ref, [(kept_ref, 0), (sent_ref, 256)], out_ref)


def mode_keep(new, kept, sent, after):
    return call(
        mode_keep_body,
        shaped((4, kept.shape[1], 128)),
        [vmem()] * 3 + [anywhere()],
        (new, kept, sent, after),
        "mode_keep",
    )


def deal_body(me_ref, keep_ref, got_ref, mine_ref, *outs):
    upper = (me_ref[0] >> 2) & 1
    places = [upper, 2 + upper, 1 - upper, 3 - upper]
    values = [keep_ref[at] + got_ref[at].astype(F32) for at in places]
    mine_ref[...] = values[0]
    for out, value in zip(outs, values[1:]):
        out[...] = value.astype(out.dtype)


def deal(me, keep, got):
    shape = keep.shape[1:]
    return call(
        deal_body,
        (shaped(shape),) + (shaped(shape, got.dtype),) * 3,
        [smem(), vmem(), vmem()],
        (me, keep, got),
        "deal",
        us=0.2,
    )


def local(tensor, first_factor, second_factor):
    frame_count, col_count, row_count = tensor.shape
    components = first_factor.shape[0]
    row_size, col_size = lax.axis_size("row"), lax.axis_size("col")
    every = row_size * col_size
    width = row_count // col_size
    direct = width % 128 == 0 and col_size == 8
    me = lax.axis_index(BOTH).astype(jnp.int32).reshape(1)
    col_bits = [1 << b for b in range(col_size.bit_length() - 1)]
    row_bits = [col_size << b for b in range(row_size.bit_length() - 1)]
    tensor = pltpu.with_memory_space_constraint(tensor, pltpu.HBM)
    cuts = [(0, GROUP), (GROUP, GROUP), (2 * GROUP, col_count - 2 * GROUP)]

    turned, wides = [], []
    order = [0, 4, 2, 6, 1, 5, 3, 7]
    ends = [cols for _, cols in cuts[1:]] + [0]
    fetched = []
    if direct:
        have, second_turned, second_values = join(me, first_factor, second_factor.T)
    else:
        have = second_values = second_factor.astype(F32)
        second_turned = second_values.T
    for (at, cols), following, bit in zip(cuts, ends, (4, 2, 1)):
        if direct:
            got = swap(have, "col", col_size, bit)
        (t, w, token), fetched = prepare(tensor, second_values, at, cols, fetched, following, have)
        turned.append(t)
        wides.append(w)
        if direct and bit > 1:
            have = stack([have, got], token)
    if direct:
        first_turned, gram_first, gram_second = assemble_first(
            me, [have, got], token, order, components, row_count
        )
    else:
        full = lax.all_gather(first_factor, "col", axis=1, tiled=True)
        others = lax.all_gather(second_factor, "col", axis=1, tiled=True)
        first_turned = full.T
        gram_first = jnp.dot(full, full.T, preferred_element_type=F32)
        gram_second = jnp.dot(others, others.T, preferred_element_type=F32)

    total = project(first_turned, second_turned, gram_first, turned)
    core, upper = row_bits[0], row_bits[1:]
    total = add([total, swap(total, BOTH, every, core)], total)
    total, gram_first = split_add(total, swap(total, BOTH, every, upper[0] | core))
    state = (gram_first, gram_second)
    marks = [0, 24, 44, components]
    for n, bit in enumerate(upper[1:] + col_bits):
        got = swap(total, BOTH, every, bit | core)
        if n < 3:
            state = (eliminate_part(state, marks[n], marks[n + 1], total),)
        total = add([total, got], state[0])
    at = me if direct else jnp.zeros((1,), jnp.int32)
    near, far = (0,), (1, 2, 3)
    frames, frames_again, sent, *sends = slab(at, (state[0], total), turned, wides, far)
    if direct:
        got = [swap(x, "col", col_size, o) for o, x in zip(far, sends)]
    kept, keep = slab(at, (frames_again,), turned, wides, near)

    gram_frames, state = frames_gram(frames_again, gram_second, 44, keep)
    if direct:
        keep = add([keep, *got], state)
        got = swap(keep, "col", col_size, 4)
        state = eliminate_part((state,), 44, components, keep)
        new = update(state, [keep, got])
        stacks = [new] + [swap(new, "col", col_size, o) for o in far]
    else:
        state = eliminate_part((state,), 44, components, keep)
        blocks = jnp.stack([keep, *sends]).transpose(2, 1, 0, 3).reshape(components, row_count)
        summed = lax.psum_scatter(blocks, "col", scatter_dimension=1, tiled=True)
        new = update(state, [summed[None]])[0]
        new = lax.all_gather(new, "col", axis=1, tiled=True).reshape(components, 2, 4, 128)
        stacks = list(new.transpose(2, 1, 0, 3))
    part = second(stacks, kept, sent)
    part = add([part, swap(part, BOTH, every, core)], part)
    got = swap(part, BOTH, every, upper[0] | core)

    new_second, send = mode_send(part, got, gram_frames, sent, BF16 if direct else F32)
    if not direct:
        keep = mode_keep(new_second, kept, sent, new_second)
        odd, even = send.reshape(2, 2, components, 128), keep.reshape(2, 2, components, 128)
        blocks = jnp.stack([even[0], odd[0], even[1], odd[1]]).transpose(2, 1, 0, 3).reshape(components, row_count)
        return (frames, lax.psum_scatter(blocks, "col", scatter_dimension=1, tiled=True))
    got = swap(send, "col", col_size, 1)
    keep = mode_keep(new_second, kept, sent, send)
    mine, *send = deal(me, keep, got)
    got = [swap(x, "col", col_size, 2 * n + 2).astype(F32) for n, x in enumerate(send)]
    return (frames, paired([mine, *got]))


def solution(mesh):
    return jax.shard_map(
        local,
        mesh=mesh,
        in_specs=(P(None, "col", "row"), P(None, ("row", "col")), P(None, "col")),
        out_specs=(P(), P(None, ("row", "col"))),
        check_vma=False,
    )
```

```python
import functools

import jax
import jax.numpy as jnp
from jax import lax
from jax.experimental import pallas as pl
from jax.experimental.pallas import tpu as pltpu
from jax.sharding import PartitionSpec as P

ridge_weight = 0.05
HIGH = lax.Precision.HIGHEST
BOTH = ("row", "col")
F32, BF16 = jnp.float32, jnp.bfloat16
VM = pltpu.VMEM
MIB = 1 << 20
GROUP = 16


def vmem():
    return pl.BlockSpec(memory_space=VM)


def anywhere():
    return pl.BlockSpec(memory_space=pl.ANY)


def smem():
    return pl.BlockSpec(memory_space=pltpu.SMEM)


def shaped(shape, dtype=F32):
    return jax.ShapeDtypeStruct(shape, dtype)


def call(body, outs, ins, operands, name, scratch=(), mib=16, us=1):
    several = isinstance(outs, tuple)
    return pl.pallas_call(
        body,
        out_shape=outs,
        in_specs=ins,
        out_specs=(vmem(),) * len(outs) if several else vmem(),
        scratch_shapes=scratch,
        compiler_params=pltpu.CompilerParams(vmem_limit_bytes=mib * MIB),
        cost_estimate=pl.CostEstimate(flops=0, bytes_accessed=int(us * 3_000_000), transcendentals=0),
        name=name,
    )(*operands)


def dot(a, b, dims, precision=None):
    return lax.dot_general(a, b, (dims, ((), ())), precision=precision, preferred_element_type=F32)


def swaps(x, axes, count, bits):
    offsets = [0]
    for bit in bits:
        offsets = offsets + [o ^ bit for o in offsets]
    return [swap(x, axes, count, o) for o in offsets[1:]]


def swap(x, axes, count, offset):
    return lax.ppermute(x, axes, [(n, n ^ offset) for n in range(count)])


def join_body(me_ref, a_hbm, b_hbm, out_ref, turned_ref, second_ref, a_ref, b_ref, sems):
    del me_ref
    moves = [pltpu.make_async_copy(*pair, sems.at[n]) for n, pair in enumerate(((a_hbm, a_ref), (b_hbm, b_ref)))]
    for move in moves:
        move.start()
    for move in moves:
        move.wait()
    components = a_ref.shape[0]
    half = b_ref.shape[0] // 2
    out_ref[0, :components, :] = a_ref[...]
    b = b_ref[...].astype(F32)
    turned_ref[...] = b
    second_ref[...] = jnp.zeros_like(second_ref)
    second_ref[:, : b.shape[0]] = b.T
    pair = jnp.concatenate([b[:half], b[half:]], axis=1)
    pair = jnp.concatenate([pair, jnp.zeros((-half % 16, 2 * components), F32)], axis=0)
    out_ref[0, components:, :] = pair.astype(BF16)


def join(me, first, second_turned):
    components, width = first.shape
    cols = second_turned.shape[0]
    height = components + cols // 2 + (-(cols // 2) % 16)
    first = pltpu.with_memory_space_constraint(first, pltpu.HBM)
    second_turned = pltpu.with_memory_space_constraint(second_turned, pltpu.HBM)
    return call(
        join_body,
        (shaped((1, height, width), BF16), shaped((cols, components)), shaped((components, 128))),
        [smem()] + [anywhere()] * 2,
        (me, first, second_turned),
        "join",
        [VM(first.shape, BF16), VM(second_turned.shape, BF16), pltpu.SemaphoreType.DMA((2,))],
    )


def stack_body(*refs):
    *parts, after_ref, out_ref = refs
    del after_ref
    at = 0
    for part in parts:
        out_ref[at : at + part.shape[0]] = part[...]
        at += part.shape[0]


def stack(parts, after):
    shape = (sum(p.shape[0] for p in parts),) + parts[0].shape[1:]
    specs = [vmem()] * len(parts) + [anywhere()]
    return call(stack_body, shaped(shape, parts[0].dtype), specs, (*parts, after), "stack", us=0.2)


def paired(values):
    while len(values) > 1:
        values = [values[n] + values[n + 1] for n in range(0, len(values), 2)]
    return values[0]


def add_body(*refs):
    *parts, after_ref, out_ref = refs
    del after_ref
    out_ref[...] = paired([p[...] for p in parts])


def add(parts, after):
    specs = [vmem()] * len(parts) + [anywhere()]
    return call(add_body, shaped(parts[0].shape), specs, (*parts, after), "add", us=0.2)


def split_body(*refs):
    *parts, sum_ref, gram_ref = refs
    components = sum_ref.shape[0]
    sum_ref[...] = paired([p[:components] for p in parts])
    gram_ref[...] = parts[0][components:, :components] + parts[1][components:, :components]


def split_add(parts):
    half = parts[0].shape[0] // 2
    outs = (shaped((half, parts[0].shape[1])), shaped((half, half)))
    return call(split_body, outs, [vmem()] * len(parts), parts, "split_add", us=0.2)


def core_add_body(a_ref, b_ref, out_ref, sum_ref):
    total = a_ref[...] + b_ref[...]
    out_ref[...] = total
    sum_ref[...] = total[: sum_ref.shape[0]]


def core_add(a, b):
    outs = (shaped(a.shape), shaped((a.shape[0] // 2, a.shape[1])))
    return call(core_add_body, outs, [vmem()] * 2, (a, b), "core_add", us=0.2)


def prepare_body(at, cols, here, ahead, t_ref, b_ref, after_ref, *refs):
    del after_ref
    slab_ref = refs[0] if here else None
    refs = list(refs[1:] if here else refs)
    out_ref, wide_ref, token_ref = refs[:3]
    next_ref = refs.pop(3) if ahead else None
    sems = refs[-1]
    slab_ref = slab_ref if here else refs[3]
    blocks = slab_ref.shape[0]

    def fetch(n, to_ref, start, sem):
        return pltpu.make_async_copy(
            t_ref.at[pl.ds(n * GROUP, GROUP), pl.ds(start, to_ref.shape[2])], to_ref.at[n], sems.at[sem, n]
        )

    if not here:
        for n in range(blocks):
            fetch(n, slab_ref, at, 0).start()
    if ahead:
        for n in range(blocks):
            fetch(n, next_ref, at + cols, 1).start()
    token_ref[...] = jnp.zeros_like(token_ref)
    for j in range(cols):
        wide_ref[j] = jnp.broadcast_to(b_ref[:, at + j : at + j + 1], wide_ref.shape[1:])
    to = lax.broadcasted_iota(jnp.int32, (256, 256), 0)
    of = lax.broadcasted_iota(jnp.int32, (256, 256), 1)
    turn = jnp.where((to // GROUP) + (to % GROUP) * GROUP == of, 1.0, 0.0).astype(BF16)

    def step(n, _):
        if not here:
            fetch(n, slab_ref, at, 0).wait()
        for g in range(0, cols, GROUP):
            block = slab_ref[n, :, g : g + GROUP, :].reshape(GROUP * GROUP, -1)
            turned = dot(turn, block, ((1,), (0,))).astype(BF16).reshape(GROUP, GROUP, -1)
            out_ref[g : g + GROUP, pl.ds(pl.multiple_of(n * GROUP, GROUP), GROUP), :] = turned
        return 0

    lax.fori_loop(0, blocks, step, 0)
    if ahead:
        for n in range(blocks):
            fetch(n, next_ref, at + cols, 1).wait()


def prepare(tensor, second, at, cols, fetched, next_cols, after):
    frames, _, rows = tensor.shape
    components = second.shape[0]
    blocks = frames // GROUP
    outs = (VM((cols, frames, rows), BF16), VM((cols, components, 128), F32), shaped((8, 128)))
    if next_cols:
        outs += (VM((blocks, GROUP, next_cols, rows), BF16),)
    scratch = [] if fetched else [VM((blocks, GROUP, cols, rows), BF16)]
    got = call(
        functools.partial(prepare_body, at, cols, bool(fetched), bool(next_cols)),
        outs,
        [anywhere(), vmem(), anywhere()] + [vmem()] * len(fetched),
        (tensor, second, after, *fetched),
        "prepare",
        scratch + [pltpu.SemaphoreType.DMA((2, blocks))],
        us=cols / 8,
    )
    return got[:3], list(got[3:])


def place(at, blocks, width, full_ref):
    for offset, block in blocks:
        if len(blocks) == 1:
            full_ref[...] = block.astype(full_ref.dtype)
        else:
            lanes = pl.ds(pl.multiple_of((at ^ offset) * width, width), width)
            full_ref[:, lanes] = block.astype(full_ref.dtype)


def assemble_first_body(offsets, me_ref, *refs):
    stacks, (turned_ref, gram_ref, other_ref), (full_ref, every_ref) = refs[:-6], refs[-5:-2], refs[-2:]
    components = full_ref.shape[0]
    blocks = [s[n] for s in stacks for n in range(s.shape[0])]
    width = blocks[0].shape[1]
    place(me_ref[0] & 7, [(o, b[:components]) for o, b in zip(offsets, blocks)], width, full_ref)
    full = full_ref[...]
    gram_ref[...] = dot(full.astype(BF16), full.astype(BF16), ((1,), (1,)))
    turned_ref[...] = full.T.astype(BF16)
    height = blocks[0].shape[0] - components
    for o, b in zip(offsets, blocks):
        every_ref[pl.ds(pl.multiple_of(((me_ref[0] & 7) ^ o) * height, height), height), :] = b[components:].astype(F32)
    every = every_ref[...].T.astype(BF16)
    both = dot(every, every, ((1,), (1,)))
    other_ref[...] = both[:components, :components] + both[components:, components:]


def assemble_first(me, stacks, after, offsets, components, rows):
    height = stacks[0].shape[1] - components
    square = shaped((components, components))
    return call(
        functools.partial(assemble_first_body, offsets),
        (shaped((rows, components), BF16), square, square),
        [smem()] + [vmem()] * len(stacks) + [anywhere()],
        (me, *stacks, after),
        "assemble_first",
        [VM((components, rows), F32), VM((height * len(offsets), 2 * components), F32)],
    )


def project_body(span, turned_ref, second_ref, gram_ref, *refs):
    *t_refs, out_ref = refs
    components = turned_ref.shape[1]
    weights = turned_ref[...]
    total, at = 0.0, 0
    for t_ref in t_refs:
        cols, frames, rows = t_ref.shape

        def step(n, total, t_ref=t_ref, at=at):
            block = t_ref[pl.ds(n * span, span)].reshape(span * frames, rows)
            product = dot(block, weights, ((1,), (0,))).reshape(span, frames, components)
            scale = second_ref[pl.ds(pl.multiple_of(at + n * span, span), span), :]
            for s in range(span):
                total = total + product[s] * scale[s : s + 1, :]
            return total

        total = lax.fori_loop(0, cols // span, step, total + jnp.zeros((frames, components), F32))
        at += cols
    out_ref[:components] = total.T
    gram = gram_ref[...]
    out_ref[components:] = jnp.concatenate([gram, gram], axis=1)


def project(first_turned, second_turned, gram, turned):
    components, frames = first_turned.shape[1], turned[0].shape[1]
    return call(
        functools.partial(project_body, 8),
        shaped((2 * components, frames)),
        [vmem()] * (3 + len(turned)),
        (first_turned, second_turned, gram, *turned),
        "project",
        us=5,
    )


def eliminate(matrix, start, stop, span=4):
    size = matrix.shape[0]
    row_at = lax.broadcasted_iota(jnp.int32, (size, size), 0)
    col_at = lax.broadcasted_iota(jnp.int32, (size, size), 1)
    lane = col_at[:1]
    for k in range(start, stop, span):
        among = range(span)
        cols = [jnp.broadcast_to(matrix[:, k + n : k + n + 1], matrix.shape) for n in among]
        mine = (lane >= k) & (lane < k + span)
        rows = [
            jnp.where(mine, jnp.where(lane == k + m, 1.0, 0.0), matrix[k + m : k + m + 1]) for m in among
        ]
        block = [[cols[n][k + m : k + m + 1] for n in among] for m in among]
        for m in among:
            pivot = 1.0 / block[m][m]
            rows[m] = rows[m] * pivot
            for n in range(m + 1, span):
                block[m][n] = block[m][n] * pivot
            for other in among:
                if other != m:
                    factor = block[other][m]
                    rows[other] = rows[other] - factor * rows[m]
                    for n in range(m + 1, span):
                        block[other][n] = block[other][n] - factor * block[m][n]
        rest = jnp.where((col_at >= k) & (col_at < k + span), 0.0, matrix)
        taken = cols[0] * rows[0]
        for n in range(1, span):
            taken = taken + cols[n] * rows[n]
        matrix = rest - taken
        for m in among:
            matrix = jnp.where(row_at == k + m, rows[m], matrix)
    return matrix


def ridged(gram):
    row_at = lax.broadcasted_iota(jnp.int32, gram.shape, 0)
    col_at = lax.broadcasted_iota(jnp.int32, gram.shape, 1)
    return gram + jnp.where(row_at == col_at, ridge_weight, 0.0)


def eliminate_body(start, stop, first, *refs):
    *ins, after_ref, out_ref = refs
    del after_ref
    matrix = ridged(ins[0][...] * ins[1][...]) if first else ins[0][...]
    out_ref[...] = eliminate(matrix, start, stop)


def eliminate_part(operands, start, stop, after):
    return call(
        functools.partial(eliminate_body, start, stop, len(operands) == 2),
        shaped(operands[0].shape),
        [vmem()] * len(operands) + [anywhere()],
        (*operands, after),
        "eliminate",
    )


def block_lanes(me_ref, offset, upper):
    at = pl.multiple_of((((me_ref[0] & 3) ^ offset) + 4 * upper) * 128, 128)
    return pl.ds(at, 128)


def slab_body(groups, offsets, first, me_ref, *refs):
    heads, refs = refs[: 2 if first else 1], refs[2 if first else 1 :]
    t_refs, wide_refs, refs = refs[:groups], refs[groups : 2 * groups], refs[2 * groups :]
    if first:
        frames_ref, copy_ref, *refs = refs
        frames = dot(heads[0][...], heads[1][...], ((1,), (0,)), HIGH)
        frames_ref[...] = frames
        copy_ref[...] = frames
    else:
        frames = heads[0][...]
    z_ref, *outs = refs
    components, depth = frames.shape
    high = frames.astype(BF16)
    none = jnp.zeros_like(high)
    both = jnp.concatenate([jnp.concatenate(pair, axis=1) for pair in ((high, none), (none, high))], axis=0)
    wide = 256
    for place_at, (offset, out_ref) in enumerate(zip(offsets, outs)):
        lanes = [block_lanes(me_ref, offset, n) for n in range(2)]
        store = pl.ds(place_at * wide, wide)
        total = jnp.zeros((components, wide), F32)
        base = 0
        for t_ref, wide_ref in zip(t_refs, wide_refs):

            def step(n, total, t_ref=t_ref, wide_ref=wide_ref, base=base):
                for s in range(0, 8, 2):
                    rows = pl.ds(n * 8 + s, 2)
                    block = jnp.concatenate([t_ref[rows, :, at].reshape(2 * depth, 128) for at in lanes], axis=1)
                    product = dot(both, block, ((1,), (0,)))
                    for h in range(2):
                        j = n * 8 + s + h
                        z = product[h * components : h * components + components]
                        z_ref[base + j, :, store] = z
                        scale = wide_ref[j]
                        total = total + z * jnp.concatenate([scale, scale], axis=1)
                return total

            total = lax.fori_loop(0, t_ref.shape[0] // 8, step, total)
            base += t_ref.shape[0]
        for n in range(2):
            out_ref[n] = total[:, n * 128 : n * 128 + 128]


def slab(me, heads, turned, wides, offsets):
    _, frames, _ = turned[0].shape
    components = wides[0].shape[1]
    first = len(heads) == 2
    cols = sum(t.shape[0] for t in turned)
    outs = (VM((cols, components, 256 * len(offsets)), F32),) + (shaped((2, components, 128)),) * len(offsets)
    if first:
        outs = (shaped((components, frames)),) * 2 + outs
    return call(
        functools.partial(slab_body, len(turned), offsets, first),
        outs,
        [smem()] + [vmem()] * (len(heads) + 2 * len(turned)),
        (me, *heads, *turned, *wides),
        "slab",
        us=2 * len(offsets),
    )


def frames_gram_body(stop, frames_ref, other_ref, after_ref, gram_ref, out_ref):
    del after_ref
    frames = frames_ref[...]
    gram = dot(frames, frames, ((1,), (1,)), HIGH)
    gram_ref[...] = gram
    out_ref[...] = eliminate(ridged(gram * other_ref[...]), 0, stop)


def frames_gram(frames, other, stop, after):
    square = shaped(other.shape)
    return call(
        functools.partial(frames_gram_body, stop),
        (square, square),
        [vmem(), vmem(), anywhere()],
        (frames, other, after),
        "frames_gram",
        us=2,
    )


def update_body(inverse_ref, *refs):
    *parts, out_ref = refs
    for n in range(out_ref.shape[0]):
        summed = paired([p[n] for p in parts])
        out_ref[n] = dot(inverse_ref[...], summed, ((1,), (0,)), HIGH).astype(BF16)


def update(inverse_now, parts):
    return call(
        update_body,
        shaped(parts[0].shape, BF16),
        [vmem()] * (1 + len(parts)),
        (inverse_now, *parts),
        "update",
    )


def second_body(*refs):
    *stacks, kept_ref, sent_ref, out_ref, full_ref = refs
    cols, components, near = kept_ref.shape
    blocks = [s[n] for s in stacks for n in range(s.shape[0])]
    for n, block in enumerate(blocks):
        full_ref[:, n * 128 : n * 128 + 128] = block.astype(F32)
    lane = lax.broadcasted_iota(jnp.int32, (8, 128), 1)

    def step(n, _):
        at = pl.ds(pl.multiple_of(n * 8, 8), 8)
        mine = full_ref[at, :]
        total = jnp.zeros((8, 128), F32)
        for j in range(cols):
            products = kept_ref[j, at, :] * mine[:, :near], sent_ref[j, at, :] * mine[:, near:]
            folds = [p[:, c : c + 128] for p in products for c in range(0, p.shape[1], 128)]
            folded = paired(folds)
            total = jnp.where(lane == j, jnp.sum(folded, axis=1, keepdims=True), total)
        out_ref[at, :] = total
        return 0

    lax.fori_loop(0, components // 8, step, 0)
    full = full_ref[...].astype(BF16)
    gram = dot(full, full, ((1,), (1,)))
    out_ref[...] = jnp.concatenate([out_ref[:, :components], gram], axis=1)


def second(stacks, kept, sent):
    components = kept.shape[1]
    return call(
        second_body,
        shaped((components, 2 * components)),
        [vmem()] * (2 + len(stacks)),
        (*stacks, kept, sent),
        "second",
        [VM((components, kept.shape[2] + sent.shape[2]), F32)],
        us=2,
    )


def mode_sums(new_ref, z_ref, out_refs):
    components = new_ref.shape[0]

    def step(n, _):
        at = pl.ds(pl.multiple_of(n * 8, 8), 8)
        scale = new_ref[at, :]
        total = jnp.zeros((8, z_ref.shape[2]), F32)
        for j in range(z_ref.shape[0]):
            total = total + z_ref[j, at, :] * scale[:, j : j + 1]
        for p, out_ref in enumerate(out_refs):
            for h in range(2):
                lane = 256 * p + 128 * h
                out_ref[h, at, :] = total[:, lane : lane + 128]
        return 0

    lax.fori_loop(0, components // 8, step, 0)


def mode_send_body(mine_ref, got_ref, gram_frames_ref, sent_ref, new_ref, *refs):
    outs, sums = refs[:3], refs[3:]
    components = new_ref.shape[0]
    summed = mine_ref[...] + got_ref[...]
    solver = eliminate(ridged(summed[:, components:] * gram_frames_ref[...]), 0, components)
    new_ref[...] = dot(solver, summed, ((1,), (0,)), HIGH)
    mode_sums(new_ref, sent_ref, sums)
    for out_ref, sum_ref in zip(outs, sums):
        out_ref[...] = sum_ref[...].astype(out_ref.dtype)


def mode_send(mine, got, gram_frames, sent, kind):
    components = sent.shape[1]
    shape = (2, components, 128)
    return call(
        mode_send_body,
        (shaped((components, 2 * components)),) + (shaped(shape, kind),) * 3,
        [vmem()] * 4,
        (mine, got, gram_frames, sent),
        "mode_send",
        [VM(shape, F32)] * 3,
        us=4,
    )


def mode_keep_body(new_ref, kept_ref, after_ref, out_ref):
    del after_ref
    mode_sums(new_ref, kept_ref, [out_ref])


def mode_keep(new, kept, after):
    return call(
        mode_keep_body,
        shaped((2, kept.shape[1], 128)),
        [vmem()] * 2 + [anywhere()],
        (new, kept, after),
        "mode_keep",
        us=0.5,
    )


def deal_body(me_ref, *refs):
    *parts, mine_ref, out_ref = refs
    upper = (me_ref[0] >> 2) & 1
    own, other = (paired([p[at].astype(F32) for p in parts]) for at in (upper, 1 - upper))
    mine_ref[...] = own
    out_ref[...] = other.astype(out_ref.dtype)


def deal(me, parts, kind):
    shape = parts[0].shape[1:]
    return call(
        deal_body,
        (shaped(shape), shaped(shape, kind)),
        [smem()] + [vmem()] * len(parts),
        (me, *parts),
        "deal",
        us=0.2,
    )


def local(tensor, first_factor, second_factor):
    frame_count, col_count, row_count = tensor.shape
    components = first_factor.shape[0]
    row_size, col_size = lax.axis_size("row"), lax.axis_size("col")
    every = row_size * col_size
    width = row_count // col_size
    direct = width % 128 == 0 and col_size == 8
    me = lax.axis_index(BOTH).astype(jnp.int32).reshape(1)
    col_bits = [1 << b for b in range(col_size.bit_length() - 1)]
    row_bits = [col_size << b for b in range(row_size.bit_length() - 1)]
    tensor = pltpu.with_memory_space_constraint(tensor, pltpu.HBM)
    cuts = [(0, GROUP), (GROUP, GROUP), (2 * GROUP, col_count - 2 * GROUP)]

    turned, wides = [], []
    order = [0, 4, 2, 6, 1, 5, 3, 7]
    ends = [cols for _, cols in cuts[1:]] + [0]
    fetched = []
    if direct:
        have, second_turned, second_values = join(me, first_factor, second_factor.T)
    else:
        have = second_values = second_factor.astype(F32)
        second_turned = second_values.T
    for (at, cols), following, bit in zip(cuts, ends, (4, 2, 1)):
        if direct:
            got = swap(have, "col", col_size, bit)
        (t, w, token), fetched = prepare(tensor, second_values, at, cols, fetched, following, have)
        turned.append(t)
        wides.append(w)
        if direct and bit > 1:
            have = stack([have, got], token)
    if direct:
        first_turned, gram_first, gram_second = assemble_first(
            me, [have, got], token, order, components, row_count
        )
    else:
        full = lax.all_gather(first_factor, "col", axis=1, tiled=True)
        others = lax.all_gather(second_factor, "col", axis=1, tiled=True)
        first_turned = full.T
        gram_first = jnp.dot(full, full.T, preferred_element_type=F32)
        gram_second = jnp.dot(others, others.T, preferred_element_type=F32)

    total = project(first_turned, second_turned, gram_first, turned)
    core, upper = row_bits[0], row_bits[1:]
    total, alone = core_add(total, swap(total, BOTH, every, core))
    row, col = upper[0] | core, col_bits[0]
    got = [swap(total, BOTH, every, row)] + [swap(alone, BOTH, every, o) for o in (col | core, row | col)]
    total, gram_first = split_add([total, *got])
    state = (gram_first, gram_second)
    marks = [0, 44, components]
    for n, bit in enumerate(col_bits[1:]):
        got = swap(total, BOTH, every, bit | core)
        if n < 2:
            state = (eliminate_part(state, marks[n], marks[n + 1], total),)
        total = add([total, got], state[0])

    at = me if direct else jnp.zeros((1,), jnp.int32)
    near, far = (0,), (1, 2, 3)
    frames, frames_again, sent, *sends = slab(at, (state[0], total), turned, wides, far)
    if direct:
        got = [swap(x, "col", col_size, o) for o, x in zip(far, sends)]
    kept, keep = slab(at, (frames_again,), turned, wides, near)

    gram_frames, state = frames_gram(frames_again, gram_second, 44, keep)
    if direct:
        keep = add([keep, *got], state)
        got = swap(keep, "col", col_size, 4)
        state = eliminate_part((state,), 44, components, keep)
        new = update(state, [keep, got])
        stacks = [new] + [swap(new, "col", col_size, o) for o in far]
    else:
        state = eliminate_part((state,), 44, components, keep)
        blocks = jnp.stack([keep, *sends]).transpose(2, 1, 0, 3).reshape(components, row_count)
        summed = lax.psum_scatter(blocks, "col", scatter_dimension=1, tiled=True)
        new = update(state, [summed[None]])[0]
        new = lax.all_gather(new, "col", axis=1, tiled=True).reshape(components, 2, 4, 128)
        stacks = list(new.transpose(2, 1, 0, 3))
    part = second(stacks, kept, sent)
    part = add([part, swap(part, BOTH, every, core)], part)
    got = swap(part, BOTH, every, upper[0] | core)

    new_second, *sends = mode_send(part, got, gram_frames, sent, BF16 if direct else F32)
    if not direct:
        keep = mode_keep(new_second, kept, new_second)
        blocks = jnp.stack([keep, *sends]).transpose(2, 1, 0, 3).reshape(components, row_count)
        return (frames, lax.psum_scatter(blocks, "col", scatter_dimension=1, tiled=True))
    got = [swap(x, "col", col_size, o) for o, x in zip(far, sends)]
    keep = mode_keep(new_second, kept, sends[0])
    mine, send = deal(me, [keep, *got], BF16)
    return (frames, mine + swap(send, "col", col_size, 4).astype(F32))


def solution(mesh):
    return jax.shard_map(
        local,
        mesh=mesh,
        in_specs=(P(None, "col", "row"), P(None, ("row", "col")), P(None, "col")),
        out_specs=(P(), P(None, ("row", "col"))),
        check_vma=False,
    )
```

```python
import functools

import jax
import jax.numpy as jnp
from jax import lax
from jax.experimental import pallas as pl
from jax.experimental.pallas import tpu as pltpu
from jax.sharding import PartitionSpec as P

ridge_weight = 0.05
HIGH = lax.Precision.HIGHEST
BOTH = ("row", "col")
F32, BF16 = jnp.float32, jnp.bfloat16
VM = pltpu.VMEM
MIB = 1 << 20
GROUP = 16


def vmem():
    return pl.BlockSpec(memory_space=VM)


def anywhere():
    return pl.BlockSpec(memory_space=pl.ANY)


def smem():
    return pl.BlockSpec(memory_space=pltpu.SMEM)


def shaped(shape, dtype=F32):
    return jax.ShapeDtypeStruct(shape, dtype)


def call(body, outs, ins, operands, name, scratch=(), mib=16, us=1):
    several = isinstance(outs, tuple)
    return pl.pallas_call(
        body,
        out_shape=outs,
        in_specs=ins,
        out_specs=(vmem(),) * len(outs) if several else vmem(),
        scratch_shapes=scratch,
        compiler_params=pltpu.CompilerParams(vmem_limit_bytes=mib * MIB),
        cost_estimate=pl.CostEstimate(flops=0, bytes_accessed=int(us * 3_000_000), transcendentals=0),
        name=name,
    )(*operands)


def dot(a, b, dims, precision=None):
    return lax.dot_general(a, b, (dims, ((), ())), precision=precision, preferred_element_type=F32)


def swaps(x, axes, count, bits):
    offsets = [0]
    for bit in bits:
        offsets = offsets + [o ^ bit for o in offsets]
    return [swap(x, axes, count, o) for o in offsets[1:]]


def swap(x, axes, count, offset):
    return lax.ppermute(x, axes, [(n, n ^ offset) for n in range(count)])


def join_body(me_ref, a_hbm, b_hbm, out_ref, turned_ref, second_ref, a_ref, b_ref, sems):
    del me_ref
    moves = [pltpu.make_async_copy(*pair, sems.at[n]) for n, pair in enumerate(((a_hbm, a_ref), (b_hbm, b_ref)))]
    for move in moves:
        move.start()
    for move in moves:
        move.wait()
    components = a_ref.shape[0]
    half = b_ref.shape[0] // 2
    out_ref[0, :components, :] = a_ref[...]
    b = b_ref[...].astype(F32)
    turned_ref[...] = b
    second_ref[...] = jnp.zeros_like(second_ref)
    second_ref[:, : b.shape[0]] = b.T
    pair = jnp.concatenate([b[:half], b[half:]], axis=1)
    pair = jnp.concatenate([pair, jnp.zeros((-half % 16, 2 * components), F32)], axis=0)
    out_ref[0, components:, :] = pair.astype(BF16)


def join(me, first, second_turned):
    components, width = first.shape
    cols = second_turned.shape[0]
    height = components + cols // 2 + (-(cols // 2) % 16)
    first = pltpu.with_memory_space_constraint(first, pltpu.HBM)
    second_turned = pltpu.with_memory_space_constraint(second_turned, pltpu.HBM)
    return call(
        join_body,
        (shaped((1, height, width), BF16), shaped((cols, components)), shaped((components, 128))),
        [smem()] + [anywhere()] * 2,
        (me, first, second_turned),
        "join",
        [VM(first.shape, BF16), VM(second_turned.shape, BF16), pltpu.SemaphoreType.DMA((2,))],
    )


def stack_body(*refs):
    *parts, after_ref, out_ref = refs
    del after_ref
    at = 0
    for part in parts:
        out_ref[at : at + part.shape[0]] = part[...]
        at += part.shape[0]


def stack(parts, after):
    shape = (sum(p.shape[0] for p in parts),) + parts[0].shape[1:]
    specs = [vmem()] * len(parts) + [anywhere()]
    return call(stack_body, shaped(shape, parts[0].dtype), specs, (*parts, after), "stack", us=0.2)


def paired(values):
    while len(values) > 1:
        values = [values[n] + values[n + 1] for n in range(0, len(values), 2)]
    return values[0]


def add_body(*refs):
    *parts, after_ref, out_ref = refs
    del after_ref
    out_ref[...] = paired([p[...] for p in parts])


def add(parts, after):
    specs = [vmem()] * len(parts) + [anywhere()]
    return call(add_body, shaped(parts[0].shape), specs, (*parts, after), "add", us=0.2)


def split_body(*refs):
    *parts, after_ref, sum_ref, gram_ref = refs
    del after_ref
    components = sum_ref.shape[0]
    sum_ref[...] = paired([p[:components] for p in parts])
    gram_ref[...] = parts[0][components:, :components] + parts[1][components:, :components]


def split_add(parts, after):
    half = parts[0].shape[0] // 2
    outs = (shaped((half, parts[0].shape[1])), shaped((half, half)))
    specs = [vmem()] * len(parts) + [anywhere()]
    return call(split_body, outs, specs, (*parts, after), "split_add", us=0.2)


def core_add_body(a_ref, b_ref, out_ref, sum_ref):
    total = a_ref[...] + b_ref[...]
    out_ref[...] = total
    sum_ref[...] = total[: sum_ref.shape[0]]


def core_add(a, b):
    outs = (shaped(a.shape), shaped((a.shape[0] // 2, a.shape[1])))
    return call(core_add_body, outs, [vmem()] * 2, (a, b), "core_add", us=0.2)


def prepare_body(at, cols, here, ahead, t_ref, after_ref, *refs):
    del after_ref
    slab_ref = refs[0] if here else None
    refs = list(refs[1:] if here else refs)
    out_ref, token_ref = refs[:2]
    next_ref = refs.pop(2) if ahead else None
    sems = refs[-1]
    slab_ref = slab_ref if here else refs[2]
    blocks = slab_ref.shape[0]

    def fetch(n, to_ref, start, sem):
        return pltpu.make_async_copy(
            t_ref.at[pl.ds(n * GROUP, GROUP), pl.ds(start, to_ref.shape[2])], to_ref.at[n], sems.at[sem, n]
        )

    if not here:
        for n in range(blocks):
            fetch(n, slab_ref, at, 0).start()
    if ahead:
        for n in range(blocks):
            fetch(n, next_ref, at + cols, 1).start()
    token_ref[...] = jnp.zeros_like(token_ref)
    to = lax.broadcasted_iota(jnp.int32, (256, 256), 0)
    of = lax.broadcasted_iota(jnp.int32, (256, 256), 1)
    turn = jnp.where((to // GROUP) + (to % GROUP) * GROUP == of, 1.0, 0.0).astype(BF16)

    def step(n, _):
        if not here:
            fetch(n, slab_ref, at, 0).wait()
        for g in range(0, cols, GROUP):
            block = slab_ref[n, :, g : g + GROUP, :].reshape(GROUP * GROUP, -1)
            turned = dot(turn, block, ((1,), (0,))).astype(BF16).reshape(GROUP, GROUP, -1)
            out_ref[g : g + GROUP, pl.ds(pl.multiple_of(n * GROUP, GROUP), GROUP), :] = turned
        return 0

    lax.fori_loop(0, blocks, step, 0)
    if ahead:
        for n in range(blocks):
            fetch(n, next_ref, at + cols, 1).wait()


def prepare(tensor, at, cols, fetched, next_cols, after):
    frames, _, rows = tensor.shape
    blocks = frames // GROUP
    outs = (VM((cols, frames, rows), BF16), shaped((8, 128)))
    if next_cols:
        outs += (VM((blocks, GROUP, next_cols, rows), BF16),)
    scratch = [] if fetched else [VM((blocks, GROUP, cols, rows), BF16)]
    got = call(
        functools.partial(prepare_body, at, cols, bool(fetched), bool(next_cols)),
        outs,
        [anywhere(), anywhere()] + [vmem()] * len(fetched),
        (tensor, after, *fetched),
        "prepare",
        scratch + [pltpu.SemaphoreType.DMA((2, blocks))],
        us=cols / 8,
    )
    return got[:2], list(got[2:])


def widen_body(b_ref, after_ref, out_ref, token_ref):
    del after_ref
    token_ref[...] = jnp.zeros_like(token_ref)
    for j in range(out_ref.shape[0]):
        out_ref[j] = jnp.broadcast_to(b_ref[:, j : j + 1], out_ref.shape[1:])


def widen(second, cols, after):
    specs = [vmem(), anywhere()]
    outs = (VM((cols, second.shape[0], 128), F32), shaped((8, 128)))
    return call(widen_body, outs, specs, (second, after), "widen")


def place(at, blocks, width, full_ref):
    for offset, block in blocks:
        if len(blocks) == 1:
            full_ref[...] = block.astype(full_ref.dtype)
        else:
            lanes = pl.ds(pl.multiple_of((at ^ offset) * width, width), width)
            full_ref[:, lanes] = block.astype(full_ref.dtype)


def assemble_first_body(offsets, me_ref, *refs):
    stacks, (turned_ref, gram_ref, other_ref), (full_ref, every_ref) = refs[:-6], refs[-5:-2], refs[-2:]
    components = full_ref.shape[0]
    blocks = [s[n] for s in stacks for n in range(s.shape[0])]
    width = blocks[0].shape[1]
    place(me_ref[0] & 7, [(o, b[:components]) for o, b in zip(offsets, blocks)], width, full_ref)
    full = full_ref[...]
    gram_ref[...] = dot(full.astype(BF16), full.astype(BF16), ((1,), (1,)))
    turned_ref[...] = full.T.astype(BF16)
    height = blocks[0].shape[0] - components
    for o, b in zip(offsets, blocks):
        every_ref[pl.ds(pl.multiple_of(((me_ref[0] & 7) ^ o) * height, height), height), :] = b[components:].astype(F32)
    every = every_ref[...].T.astype(BF16)
    both = dot(every, every, ((1,), (1,)))
    other_ref[...] = both[:components, :components] + both[components:, components:]


def assemble_first(me, stacks, after, offsets, components, rows):
    height = stacks[0].shape[1] - components
    square = shaped((components, components))
    return call(
        functools.partial(assemble_first_body, offsets),
        (shaped((rows, components), BF16), square, square),
        [smem()] + [vmem()] * len(stacks) + [anywhere()],
        (me, *stacks, after),
        "assemble_first",
        [VM((components, rows), F32), VM((height * len(offsets), 2 * components), F32)],
    )


def project_body(span, turned_ref, second_ref, gram_ref, *refs):
    *t_refs, out_ref = refs
    components = turned_ref.shape[1]
    weights = turned_ref[...]
    total, at = 0.0, 0
    for t_ref in t_refs:
        cols, frames, rows = t_ref.shape

        def step(n, total, t_ref=t_ref, at=at):
            block = t_ref[pl.ds(n * span, span)].reshape(span * frames, rows)
            product = dot(block, weights, ((1,), (0,))).reshape(span, frames, components)
            scale = second_ref[pl.ds(pl.multiple_of(at + n * span, span), span), :]
            for s in range(span):
                total = total + product[s] * scale[s : s + 1, :]
            return total

        total = lax.fori_loop(0, cols // span, step, total + jnp.zeros((frames, components), F32))
        at += cols
    out_ref[:components] = total.T
    gram = gram_ref[...]
    out_ref[components:] = jnp.concatenate([gram, gram], axis=1)


def project(first_turned, second_turned, gram, turned):
    components, frames = first_turned.shape[1], turned[0].shape[1]
    return call(
        functools.partial(project_body, 8),
        shaped((2 * components, frames)),
        [vmem()] * (3 + len(turned)),
        (first_turned, second_turned, gram, *turned),
        "project",
        us=5,
    )


def eliminate(matrix, start, stop, span=4):
    size = matrix.shape[0]
    row_at = lax.broadcasted_iota(jnp.int32, (size, size), 0)
    col_at = lax.broadcasted_iota(jnp.int32, (size, size), 1)
    lane = col_at[:1]
    for k in range(start, stop, span):
        among = range(span)
        cols = [jnp.broadcast_to(matrix[:, k + n : k + n + 1], matrix.shape) for n in among]
        mine = (lane >= k) & (lane < k + span)
        rows = [
            jnp.where(mine, jnp.where(lane == k + m, 1.0, 0.0), matrix[k + m : k + m + 1]) for m in among
        ]
        block = [[cols[n][k + m : k + m + 1] for n in among] for m in among]
        for m in among:
            pivot = 1.0 / block[m][m]
            rows[m] = rows[m] * pivot
            for n in range(m + 1, span):
                block[m][n] = block[m][n] * pivot
            for other in among:
                if other != m:
                    factor = block[other][m]
                    rows[other] = rows[other] - factor * rows[m]
                    for n in range(m + 1, span):
                        block[other][n] = block[other][n] - factor * block[m][n]
        rest = jnp.where((col_at >= k) & (col_at < k + span), 0.0, matrix)
        taken = cols[0] * rows[0]
        for n in range(1, span):
            taken = taken + cols[n] * rows[n]
        matrix = rest - taken
        for m in among:
            matrix = jnp.where(row_at == k + m, rows[m], matrix)
    return matrix


def ridged(gram):
    row_at = lax.broadcasted_iota(jnp.int32, gram.shape, 0)
    col_at = lax.broadcasted_iota(jnp.int32, gram.shape, 1)
    return gram + jnp.where(row_at == col_at, ridge_weight, 0.0)


def eliminate_body(start, stop, first, *refs):
    *ins, after_ref, out_ref = refs
    del after_ref
    matrix = ridged(ins[0][...] * ins[1][...]) if first else ins[0][...]
    out_ref[...] = eliminate(matrix, start, stop)


def eliminate_part(operands, start, stop, after):
    return call(
        functools.partial(eliminate_body, start, stop, len(operands) == 2),
        shaped(operands[0].shape),
        [vmem()] * len(operands) + [anywhere()],
        (*operands, after),
        "eliminate",
    )


def block_lanes(me_ref, offset, upper):
    at = pl.multiple_of((((me_ref[0] & 3) ^ offset) + 4 * upper) * 128, 128)
    return pl.ds(at, 128)


def slab_body(groups, offsets, head_count, me_ref, wide_ref, *refs):
    heads, t_refs, refs = refs[:head_count], refs[head_count : head_count + groups], refs[head_count + groups :]
    if head_count > 1:
        frames_ref, copy_ref, *refs = refs
        frames = dot(heads[0][...], paired([h[...] for h in heads[1:]]), ((1,), (0,)), HIGH)
        frames_ref[...] = frames
        copy_ref[...] = frames
    else:
        frames = heads[0][...]
    z_ref, *outs = refs
    components, depth = frames.shape
    high = frames.astype(BF16)
    none = jnp.zeros_like(high)
    both = jnp.concatenate([jnp.concatenate(pair, axis=1) for pair in ((high, none), (none, high))], axis=0)
    wide = 256
    for place_at, (offset, out_ref) in enumerate(zip(offsets, outs)):
        lanes = [block_lanes(me_ref, offset, n) for n in range(2)]
        store = pl.ds(place_at * wide, wide)
        total = jnp.zeros((components, wide), F32)
        base = 0
        for t_ref in t_refs:

            def step(n, total, t_ref=t_ref, base=base):
                for s in range(0, 8, 2):
                    rows = pl.ds(n * 8 + s, 2)
                    block = jnp.concatenate([t_ref[rows, :, at].reshape(2 * depth, 128) for at in lanes], axis=1)
                    product = dot(both, block, ((1,), (0,)))
                    for h in range(2):
                        j = n * 8 + s + h
                        z = product[h * components : h * components + components]
                        z_ref[base + j, :, store] = z
                        scale = wide_ref[base + j]
                        total = total + z * jnp.concatenate([scale, scale], axis=1)
                return total

            total = lax.fori_loop(0, t_ref.shape[0] // 8, step, total)
            base += t_ref.shape[0]
        for n in range(2):
            out_ref[n] = total[:, n * 128 : n * 128 + 128]


def slab(me, wide, heads, turned, offsets):
    _, frames, _ = turned[0].shape
    cols, components, _ = wide.shape
    outs = (VM((cols, components, 256 * len(offsets)), F32),) + (shaped((2, components, 128)),) * len(offsets)
    if len(heads) > 1:
        outs = (shaped((components, frames)),) * 2 + outs
    return call(
        functools.partial(slab_body, len(turned), offsets, len(heads)),
        outs,
        [smem()] + [vmem()] * (1 + len(heads) + len(turned)),
        (me, wide, *heads, *turned),
        "slab",
        us=2 * len(offsets),
    )


def frames_gram_body(stop, frames_ref, other_ref, after_ref, gram_ref, out_ref):
    del after_ref
    frames = frames_ref[...]
    gram = dot(frames, frames, ((1,), (1,)), HIGH)
    gram_ref[...] = gram
    out_ref[...] = eliminate(ridged(gram * other_ref[...]), 0, stop)


def frames_gram(frames, other, stop, after):
    square = shaped(other.shape)
    return call(
        functools.partial(frames_gram_body, stop),
        (square, square),
        [vmem(), vmem(), anywhere()],
        (frames, other, after),
        "frames_gram",
        us=2,
    )


def update_body(inverse_ref, *refs):
    *parts, out_ref = refs
    for n in range(out_ref.shape[0]):
        summed = paired([p[n] for p in parts])
        out_ref[n] = dot(inverse_ref[...], summed, ((1,), (0,)), HIGH).astype(BF16)


def update(inverse_now, parts):
    return call(
        update_body,
        shaped(parts[0].shape, BF16),
        [vmem()] * (1 + len(parts)),
        (inverse_now, *parts),
        "update",
    )


def second_body(*refs):
    *stacks, kept_ref, sent_ref, out_ref, full_ref, fold_ref = refs
    cols, components, near = kept_ref.shape
    blocks = [s[n] for s in stacks for n in range(s.shape[0])]
    for n, block in enumerate(blocks):
        full_ref[:, n * 128 : n * 128 + 128] = block.astype(F32)
    lane = lax.broadcasted_iota(jnp.int32, (8, 128), 1)
    ones = jnp.ones((256, 128), BF16)

    def folded(j, at, mine):
        products = kept_ref[j, at, :] * mine[:, :near], sent_ref[j, at, :] * mine[:, near:]
        return paired([p[:, c : c + 128] for p in products for c in range(0, p.shape[1], 128)])

    def step(n, _):
        at = pl.ds(pl.multiple_of(n * 8, 8), 8)
        mine = full_ref[at, :]
        for j in range(0, cols, 2):
            pair = jnp.concatenate([folded(j, at, mine), folded(j + 1, at, mine)], axis=0)
            high = pair.astype(BF16)
            fold_ref[8 * j : 8 * j + 16, :128] = high
            fold_ref[8 * j : 8 * j + 16, 128:] = (pair - high.astype(F32)).astype(BF16)
        sums = dot(fold_ref[...], ones, ((1,), (0,)))
        total = jnp.zeros((8, 128), F32)
        for j in range(cols):
            total = jnp.where(lane == j, sums[8 * j : 8 * j + 8], total)
        out_ref[at, :] = total
        return 0

    lax.fori_loop(0, components // 8, step, 0)
    full = full_ref[...].astype(BF16)
    gram = dot(full, full, ((1,), (1,)))
    out_ref[...] = jnp.concatenate([out_ref[:, :components], gram], axis=1)


def second(stacks, kept, sent):
    components = kept.shape[1]
    return call(
        second_body,
        shaped((components, 2 * components)),
        [vmem()] * (2 + len(stacks)),
        (*stacks, kept, sent),
        "second",
        [VM((components, kept.shape[2] + sent.shape[2]), F32), VM((8 * kept.shape[0], 256), BF16)],
        us=2,
    )


def mode_sums(new_ref, z_ref, out_refs):
    components = new_ref.shape[0]

    def step(n, _):
        at = pl.ds(pl.multiple_of(n * 8, 8), 8)
        scale = new_ref[at, :]
        total = jnp.zeros((8, z_ref.shape[2]), F32)
        for j in range(z_ref.shape[0]):
            total = total + z_ref[j, at, :] * scale[:, j : j + 1]
        for p, out_ref in enumerate(out_refs):
            for h in range(2):
                lane = 256 * p + 128 * h
                out_ref[h, at, :] = total[:, lane : lane + 128]
        return 0

    lax.fori_loop(0, components // 8, step, 0)


def mode_send_body(mine_ref, got_ref, gram_frames_ref, sent_ref, new_ref, *refs):
    outs, sums = refs[:3], refs[3:]
    components = new_ref.shape[0]
    summed = mine_ref[...] + got_ref[...]
    solver = eliminate(ridged(summed[:, components:] * gram_frames_ref[...]), 0, components)
    new_ref[...] = dot(solver, summed, ((1,), (0,)), HIGH)
    mode_sums(new_ref, sent_ref, sums)
    for out_ref, sum_ref in zip(outs, sums):
        out_ref[...] = sum_ref[...].astype(out_ref.dtype)


def mode_send(mine, got, gram_frames, sent, kind):
    components = sent.shape[1]
    shape = (2, components, 128)
    return call(
        mode_send_body,
        (shaped((components, 2 * components)),) + (shaped(shape, kind),) * 3,
        [vmem()] * 4,
        (mine, got, gram_frames, sent),
        "mode_send",
        [VM(shape, F32)] * 3,
        us=4,
    )


def mode_keep_body(new_ref, kept_ref, after_ref, out_ref):
    del after_ref
    mode_sums(new_ref, kept_ref, [out_ref])


def mode_keep(new, kept, after):
    return call(
        mode_keep_body,
        shaped((2, kept.shape[1], 128)),
        [vmem()] * 2 + [anywhere()],
        (new, kept, after),
        "mode_keep",
        us=0.5,
    )


def deal_body(me_ref, *refs):
    *parts, mine_ref, out_ref = refs
    upper = (me_ref[0] >> 2) & 1
    own, other = (paired([p[at].astype(F32) for p in parts]) for at in (upper, 1 - upper))
    mine_ref[...] = own
    out_ref[...] = other.astype(out_ref.dtype)


def deal(me, parts, kind):
    shape = parts[0].shape[1:]
    return call(
        deal_body,
        (shaped(shape), shaped(shape, kind)),
        [smem()] + [vmem()] * len(parts),
        (me, *parts),
        "deal",
        us=0.2,
    )


def local(tensor, first_factor, second_factor):
    frame_count, col_count, row_count = tensor.shape
    components = first_factor.shape[0]
    row_size, col_size = lax.axis_size("row"), lax.axis_size("col")
    every = row_size * col_size
    width = row_count // col_size
    direct = width % 128 == 0 and col_size == 8
    me = lax.axis_index(BOTH).astype(jnp.int32).reshape(1)
    col_bits = [1 << b for b in range(col_size.bit_length() - 1)]
    row_bits = [col_size << b for b in range(row_size.bit_length() - 1)]
    tensor = pltpu.with_memory_space_constraint(tensor, pltpu.HBM)
    cuts = [(0, GROUP), (GROUP, GROUP), (2 * GROUP, col_count - 2 * GROUP)]

    turned = []
    order = [0, 4, 2, 6, 1, 5, 3, 7]
    ends = [cols for _, cols in cuts[1:]] + [0]
    fetched = []
    if direct:
        have, second_turned, second_values = join(me, first_factor, second_factor.T)
    else:
        have = second_values = second_factor.astype(F32)
        second_turned = second_values.T
    for (at, cols), following, bit in zip(cuts, ends, (4, 2, 1)):
        if direct:
            got = swap(have, "col", col_size, bit)
        (t, token), fetched = prepare(tensor, at, cols, fetched, following, have)
        turned.append(t)
        if direct and bit > 1:
            have = stack([have, got], token)
    if direct:
        first_turned, gram_first, gram_second = assemble_first(
            me, [have, got], token, order, components, row_count
        )
    else:
        full = lax.all_gather(first_factor, "col", axis=1, tiled=True)
        others = lax.all_gather(second_factor, "col", axis=1, tiled=True)
        first_turned = full.T
        gram_first = jnp.dot(full, full.T, preferred_element_type=F32)
        gram_second = jnp.dot(others, others.T, preferred_element_type=F32)

    total = project(first_turned, second_turned, gram_first, turned)
    core, upper = row_bits[0], row_bits[1:]
    total, alone = core_add(total, swap(total, BOTH, every, core))
    row, col = upper[0] | core, col_bits[0]
    got = [swap(total, BOTH, every, row)] + [swap(alone, BOTH, every, o) for o in (col | core, row | col)]
    wide, token = widen(second_values, col_count, total)
    total, gram_first = split_add([total, *got], token)
    state = (gram_first, gram_second)
    marks = [0, 44, components]
    sums = [total]
    for n, bit in enumerate(col_bits[1:]):
        if n:
            total = add(sums, state[0])
        sums = [total, swap(total, BOTH, every, bit | core)]
        if n < 2:
            state = (eliminate_part(state, marks[n], marks[n + 1], total),)

    at = me if direct else jnp.zeros((1,), jnp.int32)
    near, far = (0,), (1, 2, 3)
    frames, frames_again, sent, *sends = slab(at, wide, (state[0], *sums), turned, far)
    if direct:
        got = [swap(x, "col", col_size, o) for o, x in zip(far, sends)]
    kept, keep = slab(at, wide, (frames_again,), turned, near)

    gram_frames, state = frames_gram(frames_again, gram_second, 20, keep)
    if direct:
        keep = add([keep, *got], state)
        got = swap(keep, "col", col_size, 4)
        state = eliminate_part((state,), 20, components, keep)
        new = update(state, [keep, got])
        stacks = [new] + [swap(new, "col", col_size, o) for o in far]
    else:
        state = eliminate_part((state,), 20, components, keep)
        blocks = jnp.stack([keep, *sends]).transpose(2, 1, 0, 3).reshape(components, row_count)
        summed = lax.psum_scatter(blocks, "col", scatter_dimension=1, tiled=True)
        new = update(state, [summed[None]])[0]
        new = lax.all_gather(new, "col", axis=1, tiled=True).reshape(components, 2, 4, 128)
        stacks = list(new.transpose(2, 1, 0, 3))
    part = second(stacks, kept, sent)
    part = add([part, swap(part, BOTH, every, core)], part)
    got = swap(part, BOTH, every, upper[0] | core)

    new_second, *sends = mode_send(part, got, gram_frames, sent, BF16 if direct else F32)
    if not direct:
        keep = mode_keep(new_second, kept, new_second)
        blocks = jnp.stack([keep, *sends]).transpose(2, 1, 0, 3).reshape(components, row_count)
        return (frames, lax.psum_scatter(blocks, "col", scatter_dimension=1, tiled=True))
    got = [swap(x, "col", col_size, o) for o, x in zip(far, sends)]
    keep = mode_keep(new_second, kept, sends[0])
    mine, send = deal(me, [keep, *got], BF16)
    return (frames, mine + swap(send, "col", col_size, 4).astype(F32))


def solution(mesh):
    return jax.shard_map(
        local,
        mesh=mesh,
        in_specs=(P(None, "col", "row"), P(None, ("row", "col")), P(None, "col")),
        out_specs=(P(), P(None, ("row", "col"))),
        check_vma=False,
    )
```

```python
import functools

import jax
import jax.numpy as jnp
from jax import lax
from jax.experimental import pallas as pl
from jax.experimental.pallas import tpu as pltpu
from jax.sharding import PartitionSpec as P

ridge_weight = 0.05
HIGH = lax.Precision.HIGHEST
BOTH = ("row", "col")
F32, BF16 = jnp.float32, jnp.bfloat16
VM = pltpu.VMEM
MIB = 1 << 20
GROUP = 16


def vmem():
    return pl.BlockSpec(memory_space=VM)


def anywhere():
    return pl.BlockSpec(memory_space=pl.ANY)


def smem():
    return pl.BlockSpec(memory_space=pltpu.SMEM)


def shaped(shape, dtype=F32):
    return jax.ShapeDtypeStruct(shape, dtype)


def call(body, outs, ins, operands, name, scratch=(), mib=16, us=1):
    several = isinstance(outs, tuple)
    return pl.pallas_call(
        body,
        out_shape=outs,
        in_specs=ins,
        out_specs=(vmem(),) * len(outs) if several else vmem(),
        scratch_shapes=scratch,
        compiler_params=pltpu.CompilerParams(vmem_limit_bytes=mib * MIB),
        cost_estimate=pl.CostEstimate(flops=0, bytes_accessed=int(us * 3_000_000), transcendentals=0),
        name=name,
    )(*operands)


def dot(a, b, dims, precision=None):
    return lax.dot_general(a, b, (dims, ((), ())), precision=precision, preferred_element_type=F32)


def swaps(x, axes, count, bits):
    offsets = [0]
    for bit in bits:
        offsets = offsets + [o ^ bit for o in offsets]
    return [swap(x, axes, count, o) for o in offsets[1:]]


def swap(x, axes, count, offset):
    return lax.ppermute(x, axes, [(n, n ^ offset) for n in range(count)])


def join_body(me_ref, a_hbm, b_hbm, out_ref, turned_ref, second_ref, a_ref, b_ref, sems):
    del me_ref
    moves = [pltpu.make_async_copy(*pair, sems.at[n]) for n, pair in enumerate(((a_hbm, a_ref), (b_hbm, b_ref)))]
    for move in moves:
        move.start()
    for move in moves:
        move.wait()
    components = a_ref.shape[0]
    half = b_ref.shape[0] // 2
    out_ref[0, :components, :] = a_ref[...]
    b = b_ref[...].astype(F32)
    turned_ref[...] = b
    second_ref[...] = jnp.zeros_like(second_ref)
    second_ref[:, : b.shape[0]] = b.T
    pair = jnp.concatenate([b[:half], b[half:]], axis=1)
    pair = jnp.concatenate([pair, jnp.zeros((-half % 16, 2 * components), F32)], axis=0)
    out_ref[0, components:, :] = pair.astype(BF16)


def join(me, first, second_turned):
    components, width = first.shape
    cols = second_turned.shape[0]
    height = components + cols // 2 + (-(cols // 2) % 16)
    first = pltpu.with_memory_space_constraint(first, pltpu.HBM)
    second_turned = pltpu.with_memory_space_constraint(second_turned, pltpu.HBM)
    return call(
        join_body,
        (shaped((1, height, width), BF16), shaped((cols, components)), shaped((components, 128))),
        [smem()] + [anywhere()] * 2,
        (me, first, second_turned),
        "join",
        [VM(first.shape, BF16), VM(second_turned.shape, BF16), pltpu.SemaphoreType.DMA((2,))],
    )


def stack_body(*refs):
    *parts, after_ref, out_ref = refs
    del after_ref
    at = 0
    for part in parts:
        out_ref[at : at + part.shape[0]] = part[...]
        at += part.shape[0]


def stack(parts, after):
    shape = (sum(p.shape[0] for p in parts),) + parts[0].shape[1:]
    specs = [vmem()] * len(parts) + [anywhere()]
    return call(stack_body, shaped(shape, parts[0].dtype), specs, (*parts, after), "stack", us=0.2)


def paired(values):
    while len(values) > 1:
        values = [values[n] + values[n + 1] for n in range(0, len(values), 2)]
    return values[0]


def add_body(*refs):
    *parts, after_ref, out_ref = refs
    del after_ref
    out_ref[...] = paired([p[...] for p in parts])


def add(parts, after):
    specs = [vmem()] * len(parts) + [anywhere()]
    return call(add_body, shaped(parts[0].shape), specs, (*parts, after), "add", us=0.2)


def split_body(*refs):
    *parts, after_ref, sum_ref, gram_ref = refs
    del after_ref
    components = sum_ref.shape[0]
    sum_ref[...] = paired([p[:components] for p in parts])
    gram_ref[...] = parts[0][components:, :components] + parts[1][components:, :components]


def split_add(parts, after):
    half = parts[0].shape[0] // 2
    outs = (shaped((half, parts[0].shape[1])), shaped((half, half)))
    specs = [vmem()] * len(parts) + [anywhere()]
    return call(split_body, outs, specs, (*parts, after), "split_add", us=0.2)


def core_add_body(a_ref, b_ref, out_ref, sum_ref):
    total = a_ref[...] + b_ref[...]
    out_ref[...] = total
    sum_ref[...] = total[: sum_ref.shape[0]]


def core_add(a, b):
    outs = (shaped(a.shape), shaped((a.shape[0] // 2, a.shape[1])))
    return call(core_add_body, outs, [vmem()] * 2, (a, b), "core_add", us=0.2)


def prepare_body(at, cols, here, ahead, t_ref, after_ref, *refs):
    del after_ref
    slab_ref = refs[0] if here else None
    refs = list(refs[1:] if here else refs)
    out_ref, token_ref = refs[:2]
    next_ref = refs.pop(2) if ahead else None
    sems = refs[-1]
    slab_ref = slab_ref if here else refs[2]
    blocks = slab_ref.shape[0]

    def fetch(n, to_ref, start, sem):
        return pltpu.make_async_copy(
            t_ref.at[pl.ds(n * GROUP, GROUP), pl.ds(start, to_ref.shape[2])], to_ref.at[n], sems.at[sem, n]
        )

    if not here:
        for n in range(blocks):
            fetch(n, slab_ref, at, 0).start()
    if ahead:
        for n in range(blocks):
            fetch(n, next_ref, at + cols, 1).start()
    token_ref[...] = jnp.zeros_like(token_ref)
    to = lax.broadcasted_iota(jnp.int32, (256, 256), 0)
    of = lax.broadcasted_iota(jnp.int32, (256, 256), 1)
    turn = jnp.where((to // GROUP) + (to % GROUP) * GROUP == of, 1.0, 0.0).astype(BF16)

    def step(n, _):
        if not here:
            fetch(n, slab_ref, at, 0).wait()
        for g in range(0, cols, GROUP):
            block = slab_ref[n, :, g : g + GROUP, :].reshape(GROUP * GROUP, -1)
            turned = dot(turn, block, ((1,), (0,))).astype(BF16).reshape(GROUP, GROUP, -1)
            out_ref[g : g + GROUP, pl.ds(pl.multiple_of(n * GROUP, GROUP), GROUP), :] = turned
        return 0

    lax.fori_loop(0, blocks, step, 0)
    if ahead:
        for n in range(blocks):
            fetch(n, next_ref, at + cols, 1).wait()


def prepare(tensor, at, cols, fetched, next_cols, after):
    frames, _, rows = tensor.shape
    blocks = frames // GROUP
    outs = (VM((cols, frames, rows), BF16), shaped((8, 128)))
    if next_cols:
        outs += (VM((blocks, GROUP, next_cols, rows), BF16),)
    scratch = [] if fetched else [VM((blocks, GROUP, cols, rows), BF16)]
    got = call(
        functools.partial(prepare_body, at, cols, bool(fetched), bool(next_cols)),
        outs,
        [anywhere(), anywhere()] + [vmem()] * len(fetched),
        (tensor, after, *fetched),
        "prepare",
        scratch + [pltpu.SemaphoreType.DMA((2, blocks))],
        us=cols / 8,
    )
    return got[:2], list(got[2:])


def widen_body(b_ref, after_ref, out_ref, token_ref):
    del after_ref
    token_ref[...] = jnp.zeros_like(token_ref)
    for j in range(out_ref.shape[0]):
        out_ref[j] = jnp.broadcast_to(b_ref[:, j : j + 1], out_ref.shape[1:])


def widen(second, cols, after):
    specs = [vmem(), anywhere()]
    outs = (VM((cols, second.shape[0], 128), F32), shaped((8, 128)))
    return call(widen_body, outs, specs, (second, after), "widen")


def place(at, blocks, width, full_ref):
    for offset, block in blocks:
        if len(blocks) == 1:
            full_ref[...] = block.astype(full_ref.dtype)
        else:
            lanes = pl.ds(pl.multiple_of((at ^ offset) * width, width), width)
            full_ref[:, lanes] = block.astype(full_ref.dtype)


def assemble_first_body(offsets, me_ref, *refs):
    stacks, (turned_ref, gram_ref, other_ref), (full_ref, every_ref) = refs[:-6], refs[-5:-2], refs[-2:]
    components = full_ref.shape[0]
    blocks = [s[n] for s in stacks for n in range(s.shape[0])]
    width = blocks[0].shape[1]
    place(me_ref[0] & 7, [(o, b[:components]) for o, b in zip(offsets, blocks)], width, full_ref)
    full = full_ref[...]
    gram_ref[...] = dot(full.astype(BF16), full.astype(BF16), ((1,), (1,)))
    turned_ref[...] = full.T.astype(BF16)
    height = blocks[0].shape[0] - components
    for o, b in zip(offsets, blocks):
        every_ref[pl.ds(pl.multiple_of(((me_ref[0] & 7) ^ o) * height, height), height), :] = b[components:].astype(F32)
    every = every_ref[...].T.astype(BF16)
    both = dot(every, every, ((1,), (1,)))
    other_ref[...] = both[:components, :components] + both[components:, components:]


def assemble_first(me, stacks, after, offsets, components, rows):
    height = stacks[0].shape[1] - components
    square = shaped((components, components))
    return call(
        functools.partial(assemble_first_body, offsets),
        (shaped((rows, components), BF16), square, square),
        [smem()] + [vmem()] * len(stacks) + [anywhere()],
        (me, *stacks, after),
        "assemble_first",
        [VM((components, rows), F32), VM((height * len(offsets), 2 * components), F32)],
    )


def project_body(span, turned_ref, second_ref, gram_ref, *refs):
    *t_refs, out_ref = refs
    components = turned_ref.shape[1]
    weights = turned_ref[...]
    total, at = 0.0, 0
    for t_ref in t_refs:
        cols, frames, rows = t_ref.shape

        def step(n, total, t_ref=t_ref, at=at):
            block = t_ref[pl.ds(n * span, span)].reshape(span * frames, rows)
            product = dot(block, weights, ((1,), (0,))).reshape(span, frames, components)
            scale = second_ref[pl.ds(pl.multiple_of(at + n * span, span), span), :]
            for s in range(span):
                total = total + product[s] * scale[s : s + 1, :]
            return total

        total = lax.fori_loop(0, cols // span, step, total + jnp.zeros((frames, components), F32))
        at += cols
    out_ref[:components] = total.T
    gram = gram_ref[...]
    out_ref[components:] = jnp.concatenate([gram, gram], axis=1)


def project(first_turned, second_turned, gram, turned):
    components, frames = first_turned.shape[1], turned[0].shape[1]
    return call(
        functools.partial(project_body, 8),
        shaped((2 * components, frames)),
        [vmem()] * (3 + len(turned)),
        (first_turned, second_turned, gram, *turned),
        "project",
        us=5,
    )


def eliminate(matrix, start, stop, span=4):
    size = matrix.shape[0]
    row_at = lax.broadcasted_iota(jnp.int32, (size, size), 0)
    col_at = lax.broadcasted_iota(jnp.int32, (size, size), 1)
    lane = col_at[:1]
    for k in range(start, stop, span):
        among = range(span)
        cols = [jnp.broadcast_to(matrix[:, k + n : k + n + 1], matrix.shape) for n in among]
        mine = (lane >= k) & (lane < k + span)
        rows = [
            jnp.where(mine, jnp.where(lane == k + m, 1.0, 0.0), matrix[k + m : k + m + 1]) for m in among
        ]
        block = [[cols[n][k + m : k + m + 1] for n in among] for m in among]
        for m in among:
            pivot = 1.0 / block[m][m]
            rows[m] = rows[m] * pivot
            for n in range(m + 1, span):
                block[m][n] = block[m][n] * pivot
            for other in among:
                if other != m:
                    factor = block[other][m]
                    rows[other] = rows[other] - factor * rows[m]
                    for n in range(m + 1, span):
                        block[other][n] = block[other][n] - factor * block[m][n]
        rest = jnp.where((col_at >= k) & (col_at < k + span), 0.0, matrix)
        taken = cols[0] * rows[0]
        for n in range(1, span):
            taken = taken + cols[n] * rows[n]
        matrix = rest - taken
        for m in among:
            matrix = jnp.where(row_at == k + m, rows[m], matrix)
    return matrix


def ridged(gram):
    row_at = lax.broadcasted_iota(jnp.int32, gram.shape, 0)
    col_at = lax.broadcasted_iota(jnp.int32, gram.shape, 1)
    return gram + jnp.where(row_at == col_at, ridge_weight, 0.0)


def eliminate_body(start, stop, first, *refs):
    *ins, after_ref, out_ref = refs
    del after_ref
    matrix = ridged(ins[0][...] * ins[1][...]) if first else ins[0][...]
    out_ref[...] = eliminate(matrix, start, stop)


def eliminate_part(operands, start, stop, after):
    return call(
        functools.partial(eliminate_body, start, stop, len(operands) == 2),
        shaped(operands[0].shape),
        [vmem()] * len(operands) + [anywhere()],
        (*operands, after),
        "eliminate",
    )


def block_lanes(me_ref, offset, upper):
    at = pl.multiple_of((((me_ref[0] & 3) ^ offset) + 4 * upper) * 128, 128)
    return pl.ds(at, 128)


def slab_body(groups, offsets, head_count, me_ref, wide_ref, *refs):
    heads, t_refs, refs = refs[:head_count], refs[head_count : head_count + groups], refs[head_count + groups :]
    if head_count > 1:
        frames_ref, copy_ref, *refs = refs
        frames = dot(heads[0][...], paired([h[...] for h in heads[1:]]), ((1,), (0,)), HIGH)
        frames_ref[...] = frames
        copy_ref[...] = frames
    else:
        frames = heads[0][...]
    z_ref, *outs = refs
    components, depth = frames.shape
    high = frames.astype(BF16)
    none = jnp.zeros_like(high)
    both = jnp.concatenate([jnp.concatenate(pair, axis=1) for pair in ((high, none), (none, high))], axis=0)
    wide = 256
    for place_at, (offset, out_ref) in enumerate(zip(offsets, outs)):
        lanes = [block_lanes(me_ref, offset, n) for n in range(2)]
        store = pl.ds(place_at * wide, wide)
        total = jnp.zeros((components, wide), F32)
        base = 0
        for t_ref in t_refs:

            def step(n, total, t_ref=t_ref, base=base):
                for s in range(0, 8, 2):
                    rows = pl.ds(n * 8 + s, 2)
                    block = jnp.concatenate([t_ref[rows, :, at].reshape(2 * depth, 128) for at in lanes], axis=1)
                    product = dot(both, block, ((1,), (0,)))
                    for h in range(2):
                        j = n * 8 + s + h
                        z = product[h * components : h * components + components]
                        z_ref[base + j, :, store] = z
                        scale = wide_ref[base + j]
                        total = total + z * jnp.concatenate([scale, scale], axis=1)
                return total

            total = lax.fori_loop(0, t_ref.shape[0] // 8, step, total)
            base += t_ref.shape[0]
        for n in range(2):
            out_ref[n] = total[:, n * 128 : n * 128 + 128]


def slab(me, wide, heads, turned, offsets):
    _, frames, _ = turned[0].shape
    cols, components, _ = wide.shape
    outs = (VM((cols, components, 256 * len(offsets)), F32),) + (shaped((2, components, 128)),) * len(offsets)
    if len(heads) > 1:
        outs = (shaped((components, frames)),) * 2 + outs
    return call(
        functools.partial(slab_body, len(turned), offsets, len(heads)),
        outs,
        [smem()] + [vmem()] * (1 + len(heads) + len(turned)),
        (me, wide, *heads, *turned),
        "slab",
        us=2 * len(offsets),
    )


def frames_gram_body(stop, frames_ref, other_ref, after_ref, gram_ref, out_ref):
    del after_ref
    frames = frames_ref[...]
    gram = dot(frames, frames, ((1,), (1,)), HIGH)
    gram_ref[...] = gram
    out_ref[...] = eliminate(ridged(gram * other_ref[...]), 0, stop)


def frames_gram(frames, other, stop, after):
    square = shaped(other.shape)
    return call(
        functools.partial(frames_gram_body, stop),
        (square, square),
        [vmem(), vmem(), anywhere()],
        (frames, other, after),
        "frames_gram",
        us=2,
    )


def update_body(inverse_ref, *refs):
    *parts, out_ref = refs
    for n in range(out_ref.shape[0]):
        summed = paired([p[n] for p in parts])
        out_ref[n] = dot(inverse_ref[...], summed, ((1,), (0,)), HIGH).astype(BF16)


def update(inverse_now, parts):
    return call(
        update_body,
        shaped(parts[0].shape, BF16),
        [vmem()] * (1 + len(parts)),
        (inverse_now, *parts),
        "update",
    )


def gather_gram_body(*refs):
    *stacks, full_ref, gram_ref = refs
    blocks = [s[n] for s in stacks for n in range(s.shape[0])]
    for n, block in enumerate(blocks):
        full_ref[:, n * 128 : n * 128 + 128] = block.astype(F32)
    full = full_ref[...].astype(BF16)
    gram_ref[...] = dot(full, full, ((1,), (1,)))


def gather_gram(stacks):
    components = stacks[0].shape[1]
    total = sum(s.shape[0] * s.shape[2] for s in stacks)
    outs = (shaped((components, total)), shaped((components, components)))
    return call(gather_gram_body, outs, [vmem()] * len(stacks), stacks, "gather_gram", us=0.3)


def second_body(full_ref, kept_ref, sent_ref, out_ref):
    cols, components, near = kept_ref.shape
    lane = lax.broadcasted_iota(jnp.int32, (8, 128), 1)

    def step(n, _):
        at = pl.ds(pl.multiple_of(n * 8, 8), 8)
        mine = full_ref[at, :]
        total = jnp.zeros((8, 128), F32)
        for j in range(cols):
            products = kept_ref[j, at, :] * mine[:, :near], sent_ref[j, at, :] * mine[:, near:]
            folded = paired([p[:, c : c + 128] for p in products for c in range(0, p.shape[1], 128)])
            total = jnp.where(lane == j, jnp.sum(folded, axis=1, keepdims=True), total)
        out_ref[at, :] = total
        return 0

    lax.fori_loop(0, components // 8, step, 0)


def second(full, kept, sent):
    components = kept.shape[1]
    return call(second_body, shaped((components, 128)), [vmem()] * 3, (full, kept, sent), "second", us=2)


def third_inverse_body(mine_ref, got_ref, other_ref, after_ref, out_ref):
    del after_ref
    gram = (mine_ref[...] + got_ref[...]) * other_ref[...]
    out_ref[...] = eliminate(ridged(gram), 0, gram.shape[0], 8)


def third_inverse(mine, got, other, after):
    specs = [vmem()] * 3 + [anywhere()]
    return call(third_inverse_body, shaped(other.shape), specs, (mine, got, other, after), "third_inverse", us=3)


def mode_sums(new_ref, z_ref, out_refs):
    components = new_ref.shape[0]

    def step(n, _):
        at = pl.ds(pl.multiple_of(n * 8, 8), 8)
        scale = new_ref[at, :]
        total = jnp.zeros((8, z_ref.shape[2]), F32)
        for j in range(z_ref.shape[0]):
            total = total + z_ref[j, at, :] * scale[:, j : j + 1]
        for p, out_ref in enumerate(out_refs):
            for h in range(2):
                lane = 256 * p + 128 * h
                out_ref[h, at, :] = total[:, lane : lane + 128]
        return 0

    lax.fori_loop(0, components // 8, step, 0)


def mode_send_body(mine_ref, got_ref, inverse_ref, sent_ref, new_ref, *refs):
    outs, sums = refs[:3], refs[3:]
    new_ref[...] = dot(inverse_ref[...], mine_ref[...] + got_ref[...], ((1,), (0,)), HIGH)
    mode_sums(new_ref, sent_ref, sums)
    for out_ref, sum_ref in zip(outs, sums):
        out_ref[...] = sum_ref[...].astype(out_ref.dtype)


def mode_send(mine, got, inverse_now, sent, kind):
    components = sent.shape[1]
    shape = (2, components, 128)
    return call(
        mode_send_body,
        (shaped(mine.shape),) + (shaped(shape, kind),) * 3,
        [vmem()] * 4,
        (mine, got, inverse_now, sent),
        "mode_send",
        [VM(shape, F32)] * 3,
        us=1.5,
    )


def mode_keep_body(new_ref, kept_ref, after_ref, out_ref):
    del after_ref
    mode_sums(new_ref, kept_ref, [out_ref])


def mode_keep(new, kept, after):
    return call(
        mode_keep_body,
        shaped((2, kept.shape[1], 128)),
        [vmem()] * 2 + [anywhere()],
        (new, kept, after),
        "mode_keep",
        us=0.5,
    )


def deal_body(me_ref, *refs):
    *parts, mine_ref, out_ref = refs
    upper = (me_ref[0] >> 2) & 1
    own, other = (paired([p[at].astype(F32) for p in parts]) for at in (upper, 1 - upper))
    mine_ref[...] = own
    out_ref[...] = other.astype(out_ref.dtype)


def deal(me, parts, kind):
    shape = parts[0].shape[1:]
    return call(
        deal_body,
        (shaped(shape), shaped(shape, kind)),
        [smem()] + [vmem()] * len(parts),
        (me, *parts),
        "deal",
        us=0.2,
    )


def local(tensor, first_factor, second_factor):
    frame_count, col_count, row_count = tensor.shape
    components = first_factor.shape[0]
    row_size, col_size = lax.axis_size("row"), lax.axis_size("col")
    every = row_size * col_size
    width = row_count // col_size
    direct = width % 128 == 0 and col_size == 8
    me = lax.axis_index(BOTH).astype(jnp.int32).reshape(1)
    col_bits = [1 << b for b in range(col_size.bit_length() - 1)]
    row_bits = [col_size << b for b in range(row_size.bit_length() - 1)]
    tensor = pltpu.with_memory_space_constraint(tensor, pltpu.HBM)
    cuts = [(0, GROUP), (GROUP, GROUP), (2 * GROUP, col_count - 2 * GROUP)]

    turned = []
    order = [0, 4, 2, 6, 1, 5, 3, 7]
    ends = [cols for _, cols in cuts[1:]] + [0]
    fetched = []
    if direct:
        have, second_turned, second_values = join(me, first_factor, second_factor.T)
    else:
        have = second_values = second_factor.astype(F32)
        second_turned = second_values.T
    for (at, cols), following, bit in zip(cuts, ends, (4, 2, 1)):
        if direct:
            got = swap(have, "col", col_size, bit)
        (t, token), fetched = prepare(tensor, at, cols, fetched, following, have)
        turned.append(t)
        if direct and bit > 1:
            have = stack([have, got], token)
    if direct:
        first_turned, gram_first, gram_second = assemble_first(
            me, [have, got], token, order, components, row_count
        )
    else:
        full = lax.all_gather(first_factor, "col", axis=1, tiled=True)
        others = lax.all_gather(second_factor, "col", axis=1, tiled=True)
        first_turned = full.T
        gram_first = jnp.dot(full, full.T, preferred_element_type=F32)
        gram_second = jnp.dot(others, others.T, preferred_element_type=F32)

    total = project(first_turned, second_turned, gram_first, turned)
    core, upper = row_bits[0], row_bits[1:]
    total, alone = core_add(total, swap(total, BOTH, every, core))
    row, col = upper[0] | core, col_bits[0]
    got = [swap(total, BOTH, every, row)] + [swap(alone, BOTH, every, o) for o in (col | core, row | col)]
    wide, token = widen(second_values, col_count, total)
    total, gram_first = split_add([total, *got], token)
    state = (gram_first, gram_second)
    marks = [0, 44, components]
    sums = [total]
    for n, bit in enumerate(col_bits[1:]):
        if n:
            total = add(sums, state[0])
        sums = [total, swap(total, BOTH, every, bit | core)]
        if n < 2:
            state = (eliminate_part(state, marks[n], marks[n + 1], total),)

    at = me if direct else jnp.zeros((1,), jnp.int32)
    near, far = (0,), (1, 2, 3)
    frames, frames_again, sent, *sends = slab(at, wide, (state[0], *sums), turned, far)
    if direct:
        got = [swap(x, "col", col_size, o) for o, x in zip(far, sends)]
    kept, keep = slab(at, wide, (frames_again,), turned, near)

    gram_frames, state = frames_gram(frames_again, gram_second, 20, keep)
    if direct:
        keep = add([keep, *got], state)
        got = swap(keep, "col", col_size, 4)
        state = eliminate_part((state,), 20, components, keep)
        new = update(state, [keep, got])
        stacks = [new] + [swap(new, "col", col_size, o) for o in far]
    else:
        state = eliminate_part((state,), 20, components, keep)
        blocks = jnp.stack([keep, *sends]).transpose(2, 1, 0, 3).reshape(components, row_count)
        summed = lax.psum_scatter(blocks, "col", scatter_dimension=1, tiled=True)
        new = update(state, [summed[None]])[0]
        new = lax.all_gather(new, "col", axis=1, tiled=True).reshape(components, 2, 4, 128)
        stacks = list(new.transpose(2, 1, 0, 3))
    full, gram_new = gather_gram(stacks)
    got = swap(gram_new, BOTH, every, core)
    part = second(full, kept, sent)
    gram_new = add([gram_new, got], part)
    gram_got = swap(gram_new, BOTH, every, upper[0] | core)
    part = add([part, swap(part, BOTH, every, core)], gram_new)
    got = swap(part, BOTH, every, upper[0] | core)
    inverse_third = third_inverse(gram_new, gram_got, gram_frames, part)

    new_second, *sends = mode_send(part, got, inverse_third, sent, BF16 if direct else F32)
    if not direct:
        keep = mode_keep(new_second, kept, new_second)
        blocks = jnp.stack([keep, *sends]).transpose(2, 1, 0, 3).reshape(components, row_count)
        return (frames, lax.psum_scatter(blocks, "col", scatter_dimension=1, tiled=True))
    got = [swap(x, "col", col_size, o) for o, x in zip(far, sends)]
    keep = mode_keep(new_second, kept, sends[0])
    mine, send = deal(me, [keep, *got], BF16)
    return (frames, mine + swap(send, "col", col_size, 4).astype(F32))


def solution(mesh):
    return jax.shard_map(
        local,
        mesh=mesh,
        in_specs=(P(None, "col", "row"), P(None, ("row", "col")), P(None, "col")),
        out_specs=(P(), P(None, ("row", "col"))),
        check_vma=False,
    )
```

```python
import functools

import jax
import jax.numpy as jnp
from jax import lax
from jax.experimental import pallas as pl
from jax.experimental.pallas import tpu as pltpu
from jax.sharding import PartitionSpec as P

ridge_weight = 0.05
HIGH = lax.Precision.HIGHEST
BOTH = ("row", "col")
F32, BF16 = jnp.float32, jnp.bfloat16
VM = pltpu.VMEM
MIB = 1 << 20
GROUP = 16


def vmem():
    return pl.BlockSpec(memory_space=VM)


def anywhere():
    return pl.BlockSpec(memory_space=pl.ANY)


def smem():
    return pl.BlockSpec(memory_space=pltpu.SMEM)


def shaped(shape, dtype=F32):
    return jax.ShapeDtypeStruct(shape, dtype)


def call(body, outs, ins, operands, name, scratch=(), mib=16, us=1):
    several = isinstance(outs, tuple)
    return pl.pallas_call(
        body,
        out_shape=outs,
        in_specs=ins,
        out_specs=(vmem(),) * len(outs) if several else vmem(),
        scratch_shapes=scratch,
        compiler_params=pltpu.CompilerParams(vmem_limit_bytes=mib * MIB),
        cost_estimate=pl.CostEstimate(flops=0, bytes_accessed=int(us * 3_000_000), transcendentals=0),
        name=name,
    )(*operands)


def dot(a, b, dims, precision=None):
    return lax.dot_general(a, b, (dims, ((), ())), precision=precision, preferred_element_type=F32)


def swaps(x, axes, count, bits):
    offsets = [0]
    for bit in bits:
        offsets = offsets + [o ^ bit for o in offsets]
    return [swap(x, axes, count, o) for o in offsets[1:]]


def swap(x, axes, count, offset):
    return lax.ppermute(x, axes, [(n, n ^ offset) for n in range(count)])


def join_body(me_ref, a_hbm, b_hbm, out_ref, turned_ref, second_ref, a_ref, b_ref, sems):
    del me_ref
    moves = [pltpu.make_async_copy(*pair, sems.at[n]) for n, pair in enumerate(((a_hbm, a_ref), (b_hbm, b_ref)))]
    for move in moves:
        move.start()
    for move in moves:
        move.wait()
    components = a_ref.shape[0]
    half = b_ref.shape[0] // 2
    out_ref[0, :components, :] = a_ref[...]
    b = b_ref[...].astype(F32)
    turned_ref[...] = b
    second_ref[...] = jnp.zeros_like(second_ref)
    second_ref[:, : b.shape[0]] = b.T
    pair = jnp.concatenate([b[:half], b[half:]], axis=1)
    pair = jnp.concatenate([pair, jnp.zeros((-half % 16, 2 * components), F32)], axis=0)
    out_ref[0, components:, :] = pair.astype(BF16)


def join(me, first, second_turned):
    components, width = first.shape
    cols = second_turned.shape[0]
    height = components + cols // 2 + (-(cols // 2) % 16)
    first = pltpu.with_memory_space_constraint(first, pltpu.HBM)
    second_turned = pltpu.with_memory_space_constraint(second_turned, pltpu.HBM)
    return call(
        join_body,
        (shaped((1, height, width), BF16), shaped((cols, components)), shaped((components, 128))),
        [smem()] + [anywhere()] * 2,
        (me, first, second_turned),
        "join",
        [VM(first.shape, BF16), VM(second_turned.shape, BF16), pltpu.SemaphoreType.DMA((2,))],
    )


def stack_body(*refs):
    *parts, after_ref, out_ref = refs
    del after_ref
    at = 0
    for part in parts:
        out_ref[at : at + part.shape[0]] = part[...]
        at += part.shape[0]


def stack(parts, after):
    shape = (sum(p.shape[0] for p in parts),) + parts[0].shape[1:]
    specs = [vmem()] * len(parts) + [anywhere()]
    return call(stack_body, shaped(shape, parts[0].dtype), specs, (*parts, after), "stack", us=0.2)


def paired(values):
    while len(values) > 1:
        values = [values[n] + values[n + 1] for n in range(0, len(values), 2)]
    return values[0]


def add_body(*refs):
    *parts, after_ref, out_ref = refs
    del after_ref
    out_ref[...] = paired([p[...] for p in parts])


def add(parts, after):
    specs = [vmem()] * len(parts) + [anywhere()]
    return call(add_body, shaped(parts[0].shape), specs, (*parts, after), "add", us=0.2)


def split_body(*refs):
    *parts, after_ref, sum_ref, gram_ref = refs
    del after_ref
    components = sum_ref.shape[0]
    sum_ref[...] = paired([p[:components] for p in parts])
    gram_ref[...] = parts[0][components:, :components] + parts[1][components:, :components]


def split_add(parts, after):
    half = parts[0].shape[0] // 2
    outs = (shaped((half, parts[0].shape[1])), shaped((half, half)))
    specs = [vmem()] * len(parts) + [anywhere()]
    return call(split_body, outs, specs, (*parts, after), "split_add", us=0.2)


def core_add_body(a_ref, b_ref, out_ref, sum_ref):
    total = a_ref[...] + b_ref[...]
    out_ref[...] = total
    sum_ref[...] = total[: sum_ref.shape[0]]


def core_add(a, b):
    outs = (shaped(a.shape), shaped((a.shape[0] // 2, a.shape[1])))
    return call(core_add_body, outs, [vmem()] * 2, (a, b), "core_add", us=0.2)


def prepare_body(at, cols, here, ahead, t_ref, after_ref, *refs):
    del after_ref
    slab_ref = refs[0] if here else None
    refs = list(refs[1:] if here else refs)
    out_ref, token_ref = refs[:2]
    next_ref = refs.pop(2) if ahead else None
    sems = refs[-1]
    slab_ref = slab_ref if here else refs[2]
    blocks = slab_ref.shape[0]

    def fetch(n, to_ref, start, sem):
        return pltpu.make_async_copy(
            t_ref.at[pl.ds(n * GROUP, GROUP), pl.ds(start, to_ref.shape[2])], to_ref.at[n], sems.at[sem, n]
        )

    if not here:
        for n in range(blocks):
            fetch(n, slab_ref, at, 0).start()
    if ahead:
        for n in range(blocks):
            fetch(n, next_ref, at + cols, 1).start()
    token_ref[...] = jnp.zeros_like(token_ref)
    to = lax.broadcasted_iota(jnp.int32, (256, 256), 0)
    of = lax.broadcasted_iota(jnp.int32, (256, 256), 1)
    turn = jnp.where((to // GROUP) + (to % GROUP) * GROUP == of, 1.0, 0.0).astype(BF16)

    def step(n, _):
        if not here:
            fetch(n, slab_ref, at, 0).wait()
        for g in range(0, cols, GROUP):
            block = slab_ref[n, :, g : g + GROUP, :].reshape(GROUP * GROUP, -1)
            turned = dot(turn, block, ((1,), (0,))).astype(BF16).reshape(GROUP, GROUP, -1)
            out_ref[g : g + GROUP, pl.ds(pl.multiple_of(n * GROUP, GROUP), GROUP), :] = turned
        return 0

    lax.fori_loop(0, blocks, step, 0)
    if ahead:
        for n in range(blocks):
            fetch(n, next_ref, at + cols, 1).wait()


def prepare(tensor, at, cols, fetched, next_cols, after):
    frames, _, rows = tensor.shape
    blocks = frames // GROUP
    outs = (VM((cols, frames, rows), BF16), shaped((8, 128)))
    if next_cols:
        outs += (VM((blocks, GROUP, next_cols, rows), BF16),)
    scratch = [] if fetched else [VM((blocks, GROUP, cols, rows), BF16)]
    got = call(
        functools.partial(prepare_body, at, cols, bool(fetched), bool(next_cols)),
        outs,
        [anywhere(), anywhere()] + [vmem()] * len(fetched),
        (tensor, after, *fetched),
        "prepare",
        scratch + [pltpu.SemaphoreType.DMA((2, blocks))],
        us=cols / 8,
    )
    return got[:2], list(got[2:])


def widen_body(b_ref, after_ref, out_ref, token_ref):
    del after_ref
    token_ref[...] = jnp.zeros_like(token_ref)
    for j in range(out_ref.shape[0]):
        out_ref[j] = jnp.broadcast_to(b_ref[:, j : j + 1], out_ref.shape[1:])


def widen(second, cols, after):
    specs = [vmem(), anywhere()]
    outs = (VM((cols, second.shape[0], 128), F32), shaped((8, 128)))
    return call(widen_body, outs, specs, (second, after), "widen")


def place(at, blocks, width, full_ref):
    for offset, block in blocks:
        if len(blocks) == 1:
            full_ref[...] = block.astype(full_ref.dtype)
        else:
            lanes = pl.ds(pl.multiple_of((at ^ offset) * width, width), width)
            full_ref[:, lanes] = block.astype(full_ref.dtype)


def assemble_first_body(offsets, me_ref, *refs):
    stacks, (turned_ref, gram_ref, other_ref), (full_ref, every_ref) = refs[:-6], refs[-5:-2], refs[-2:]
    components = full_ref.shape[0]
    blocks = [s[n] for s in stacks for n in range(s.shape[0])]
    width = blocks[0].shape[1]
    place(me_ref[0] & 7, [(o, b[:components]) for o, b in zip(offsets, blocks)], width, full_ref)
    full = full_ref[...]
    gram_ref[...] = dot(full.astype(BF16), full.astype(BF16), ((1,), (1,)))
    turned_ref[...] = full.T.astype(BF16)
    height = blocks[0].shape[0] - components
    for o, b in zip(offsets, blocks):
        every_ref[pl.ds(pl.multiple_of(((me_ref[0] & 7) ^ o) * height, height), height), :] = b[components:].astype(F32)
    every = every_ref[...].T.astype(BF16)
    both = dot(every, every, ((1,), (1,)))
    other_ref[...] = both[:components, :components] + both[components:, components:]


def assemble_first(me, stacks, after, offsets, components, rows):
    height = stacks[0].shape[1] - components
    square = shaped((components, components))
    return call(
        functools.partial(assemble_first_body, offsets),
        (shaped((rows, components), BF16), square, square),
        [smem()] + [vmem()] * len(stacks) + [anywhere()],
        (me, *stacks, after),
        "assemble_first",
        [VM((components, rows), F32), VM((height * len(offsets), 2 * components), F32)],
    )


def project_body(span, turned_ref, second_ref, gram_ref, *refs):
    *t_refs, out_ref = refs
    components = turned_ref.shape[1]
    weights = turned_ref[...]
    total, at = 0.0, 0
    for t_ref in t_refs:
        cols, frames, rows = t_ref.shape

        def step(n, total, t_ref=t_ref, at=at):
            block = t_ref[pl.ds(n * span, span)].reshape(span * frames, rows)
            product = dot(block, weights, ((1,), (0,))).reshape(span, frames, components)
            scale = second_ref[pl.ds(pl.multiple_of(at + n * span, span), span), :]
            for s in range(span):
                total = total + product[s] * scale[s : s + 1, :]
            return total

        total = lax.fori_loop(0, cols // span, step, total + jnp.zeros((frames, components), F32))
        at += cols
    out_ref[:components] = total.T
    gram = gram_ref[...]
    out_ref[components:] = jnp.concatenate([gram, gram], axis=1)


def project(first_turned, second_turned, gram, turned):
    components, frames = first_turned.shape[1], turned[0].shape[1]
    return call(
        functools.partial(project_body, 8),
        shaped((2 * components, frames)),
        [vmem()] * (3 + len(turned)),
        (first_turned, second_turned, gram, *turned),
        "project",
        us=5,
    )


def eliminate(matrix, start, stop, span=8):
    size = matrix.shape[0]
    row_at = lax.broadcasted_iota(jnp.int32, (size, size), 0)
    col_at = lax.broadcasted_iota(jnp.int32, (size, size), 1)
    lane = col_at[:1]
    for k in range(start, stop, span):
        among = range(span)
        cols = [jnp.broadcast_to(matrix[:, k + n : k + n + 1], matrix.shape) for n in among]
        mine = (lane >= k) & (lane < k + span)
        rows = [
            jnp.where(mine, jnp.where(lane == k + m, 1.0, 0.0), matrix[k + m : k + m + 1]) for m in among
        ]
        block = [[cols[n][k + m : k + m + 1] for n in among] for m in among]
        for m in among:
            pivot = 1.0 / block[m][m]
            rows[m] = rows[m] * pivot
            for n in range(m + 1, span):
                block[m][n] = block[m][n] * pivot
            for other in among:
                if other != m:
                    factor = block[other][m]
                    rows[other] = rows[other] - factor * rows[m]
                    for n in range(m + 1, span):
                        block[other][n] = block[other][n] - factor * block[m][n]
        rest = jnp.where((col_at >= k) & (col_at < k + span), 0.0, matrix)
        taken = cols[0] * rows[0]
        for n in range(1, span):
            taken = taken + cols[n] * rows[n]
        matrix = rest - taken
        for m in among:
            matrix = jnp.where(row_at == k + m, rows[m], matrix)
    return matrix


def ridged(gram):
    row_at = lax.broadcasted_iota(jnp.int32, gram.shape, 0)
    col_at = lax.broadcasted_iota(jnp.int32, gram.shape, 1)
    return gram + jnp.where(row_at == col_at, ridge_weight, 0.0)


def eliminate_body(start, stop, first, *refs):
    *ins, after_ref, out_ref = refs
    del after_ref
    matrix = ridged(ins[0][...] * ins[1][...]) if first else ins[0][...]
    out_ref[...] = eliminate(matrix, start, stop)


def eliminate_part(operands, start, stop, after):
    return call(
        functools.partial(eliminate_body, start, stop, len(operands) == 2),
        shaped(operands[0].shape),
        [vmem()] * len(operands) + [anywhere()],
        (*operands, after),
        "eliminate",
    )


def block_lanes(me_ref, offset, upper):
    at = pl.multiple_of((((me_ref[0] & 3) ^ offset) + 4 * upper) * 128, 128)
    return pl.ds(at, 128)


def slab_body(groups, offset, head_count, me_ref, wide_ref, after_ref, *refs):
    del after_ref
    heads, t_refs, refs = refs[:head_count], refs[head_count : head_count + groups], refs[head_count + groups :]
    if head_count > 1:
        frames_ref, copy_ref, *refs = refs
        frames = dot(heads[0][...], paired([h[...] for h in heads[1:]]), ((1,), (0,)), HIGH)
        frames_ref[...] = frames
        copy_ref[...] = frames
    else:
        frames = heads[0][...]
    z_ref, out_ref = refs
    components, depth = frames.shape
    high = frames.astype(BF16)
    none = jnp.zeros_like(high)
    both = jnp.concatenate([jnp.concatenate(pair, axis=1) for pair in ((high, none), (none, high))], axis=0)
    lanes = [block_lanes(me_ref, offset, n) for n in range(2)]
    total = jnp.zeros((components, 256), F32)
    base = 0
    for t_ref in t_refs:

        def step(n, total, t_ref=t_ref, base=base):
            for s in range(0, 8, 2):
                rows = pl.ds(n * 8 + s, 2)
                block = jnp.concatenate([t_ref[rows, :, at].reshape(2 * depth, 128) for at in lanes], axis=1)
                product = dot(both, block, ((1,), (0,)))
                for h in range(2):
                    j = base + n * 8 + s + h
                    z = product[h * components : h * components + components]
                    z_ref[j] = z
                    scale = wide_ref[j]
                    total = total + z * jnp.concatenate([scale, scale], axis=1)
            return total

        total = lax.fori_loop(0, t_ref.shape[0] // 8, step, total)
        base += t_ref.shape[0]
    for n in range(2):
        out_ref[n] = total[:, n * 128 : n * 128 + 128]


def slab(me, wide, heads, turned, offset, after):
    _, frames, _ = turned[0].shape
    cols, components, _ = wide.shape
    outs = (VM((cols, components, 256), F32), shaped((2, components, 128)))
    if len(heads) > 1:
        outs = (shaped((components, frames)),) * 2 + outs
    return call(
        functools.partial(slab_body, len(turned), offset, len(heads)),
        outs,
        [smem(), vmem(), anywhere()] + [vmem()] * (len(heads) + len(turned)),
        (me, wide, after, *heads, *turned),
        "slab",
        us=2,
    )


def frames_gram_body(stop, frames_ref, other_ref, after_ref, gram_ref, out_ref):
    del after_ref
    frames = frames_ref[...]
    gram = dot(frames, frames, ((1,), (1,)), HIGH)
    gram_ref[...] = gram
    out_ref[...] = eliminate(ridged(gram * other_ref[...]), 0, stop)


def frames_gram(frames, other, stop, after):
    square = shaped(other.shape)
    return call(
        functools.partial(frames_gram_body, stop),
        (square, square),
        [vmem(), vmem(), anywhere()],
        (frames, other, after),
        "frames_gram",
        us=2,
    )


def update_body(inverse_ref, *refs):
    *parts, out_ref = refs
    for n in range(out_ref.shape[0]):
        summed = paired([p[n] for p in parts])
        out_ref[n] = dot(inverse_ref[...], summed, ((1,), (0,)), HIGH).astype(BF16)


def update(inverse_now, parts):
    return call(
        update_body,
        shaped(parts[0].shape, BF16),
        [vmem()] * (1 + len(parts)),
        (inverse_now, *parts),
        "update",
    )


def second_body(count, *refs):
    z_refs, stacks, (out_ref, full_ref) = refs[:count], refs[count:-2], refs[-2:]
    cols, components, width = z_refs[0].shape
    blocks = [s[n] for s in stacks for n in range(s.shape[0])]
    for n, block in enumerate(blocks):
        full_ref[:, n * 128 : n * 128 + 128] = block.astype(F32)
    lane = lax.broadcasted_iota(jnp.int32, (8, 128), 1)

    def step(n, _):
        at = pl.ds(pl.multiple_of(n * 8, 8), 8)
        mine = full_ref[at, :]
        total = jnp.zeros((8, 128), F32)
        for j in range(cols):
            products = [z_refs[p][j, at, :] * mine[:, p * width : p * width + width] for p in range(count)]
            folded = paired([p[:, c : c + 128] for p in products for c in range(0, width, 128)])
            total = jnp.where(lane == j, jnp.sum(folded, axis=1, keepdims=True), total)
        out_ref[at, :] = total
        return 0

    lax.fori_loop(0, components // 8, step, 0)
    full = full_ref[...].astype(BF16)
    gram = dot(full, full, ((1,), (1,)))
    out_ref[...] = jnp.concatenate([out_ref[:, :components], gram], axis=1)


def second(zs, stacks):
    components = zs[0].shape[1]
    return call(
        functools.partial(second_body, len(zs)),
        shaped((components, 2 * components)),
        [vmem()] * (len(zs) + len(stacks)),
        (*zs, *stacks),
        "second",
        [VM((components, len(zs) * zs[0].shape[2]), F32)],
        us=2,
    )


def mode_sums(new_ref, z_refs, out_refs):
    components = new_ref.shape[0]

    def step(n, _):
        at = pl.ds(pl.multiple_of(n * 8, 8), 8)
        scale = new_ref[at, :]
        totals = [jnp.zeros((8, z.shape[2]), F32) for z in z_refs]
        for j in range(z_refs[0].shape[0]):
            factor = jnp.broadcast_to(scale[:, j : j + 1], totals[0].shape)
            totals = [t + z[j, at, :] * factor for t, z in zip(totals, z_refs)]
        for total, out_ref in zip(totals, out_refs):
            for h in range(2):
                out_ref[h, at, :] = total[:, h * 128 : h * 128 + 128]
        return 0

    lax.fori_loop(0, components // 8, step, 0)


def mode_send_body(mine_ref, got_ref, gram_frames_ref, *refs):
    z_refs, new_ref, outs, sums = refs[:3], refs[3], refs[4:7], refs[7:]
    components = new_ref.shape[0]
    summed = mine_ref[...] + got_ref[...]
    solver = eliminate(ridged(summed[:, components:] * gram_frames_ref[...]), 0, components)
    new_ref[...] = dot(solver, summed, ((1,), (0,)), HIGH)
    mode_sums(new_ref, z_refs, sums)
    for out_ref, sum_ref in zip(outs, sums):
        out_ref[...] = sum_ref[...].astype(out_ref.dtype)


def mode_send(mine, got, gram_frames, zs, kind):
    components = zs[0].shape[1]
    shape = (2, components, 128)
    return call(
        mode_send_body,
        (shaped(mine.shape),) + (shaped(shape, kind),) * 3,
        [vmem()] * 6,
        (mine, got, gram_frames, *zs),
        "mode_send",
        [VM(shape, F32)] * 3,
        us=3.5,
    )


def mode_keep_body(new_ref, z_ref, after_ref, out_ref):
    del after_ref
    mode_sums(new_ref, [z_ref], [out_ref])


def mode_keep(new, z, after):
    specs = [vmem()] * 2 + [anywhere()]
    return call(mode_keep_body, shaped((2, z.shape[1], 128)), specs, (new, z, after), "mode_keep", us=1)


def deal_body(me_ref, *refs):
    *parts, mine_ref, out_ref = refs
    upper = (me_ref[0] >> 2) & 1
    own, other = (paired([p[at].astype(F32) for p in parts]) for at in (upper, 1 - upper))
    mine_ref[...] = own
    out_ref[...] = other.astype(out_ref.dtype)


def deal(me, parts, kind):
    shape = parts[0].shape[1:]
    return call(
        deal_body,
        (shaped(shape), shaped(shape, kind)),
        [smem()] + [vmem()] * len(parts),
        (me, *parts),
        "deal",
        us=0.2,
    )


def local(tensor, first_factor, second_factor):
    frame_count, col_count, row_count = tensor.shape
    components = first_factor.shape[0]
    row_size, col_size = lax.axis_size("row"), lax.axis_size("col")
    every = row_size * col_size
    width = row_count // col_size
    direct = width % 128 == 0 and col_size == 8
    me = lax.axis_index(BOTH).astype(jnp.int32).reshape(1)
    col_bits = [1 << b for b in range(col_size.bit_length() - 1)]
    row_bits = [col_size << b for b in range(row_size.bit_length() - 1)]
    tensor = pltpu.with_memory_space_constraint(tensor, pltpu.HBM)
    cuts = [(0, GROUP), (GROUP, GROUP), (2 * GROUP, col_count - 2 * GROUP)]

    turned = []
    order = [0, 4, 2, 6, 1, 5, 3, 7]
    ends = [cols for _, cols in cuts[1:]] + [0]
    fetched = []
    if direct:
        have, second_turned, second_values = join(me, first_factor, second_factor.T)
    else:
        have = second_values = second_factor.astype(F32)
        second_turned = second_values.T
    for (at, cols), following, bit in zip(cuts, ends, (4, 2, 1)):
        if direct:
            got = swap(have, "col", col_size, bit)
        (t, token), fetched = prepare(tensor, at, cols, fetched, following, have)
        turned.append(t)
        if direct and bit > 1:
            have = stack([have, got], token)
    if direct:
        first_turned, gram_first, gram_second = assemble_first(
            me, [have, got], token, order, components, row_count
        )
    else:
        full = lax.all_gather(first_factor, "col", axis=1, tiled=True)
        others = lax.all_gather(second_factor, "col", axis=1, tiled=True)
        first_turned = full.T
        gram_first = jnp.dot(full, full.T, preferred_element_type=F32)
        gram_second = jnp.dot(others, others.T, preferred_element_type=F32)

    total = project(first_turned, second_turned, gram_first, turned)
    core, upper = row_bits[0], row_bits[1:]
    total, alone = core_add(total, swap(total, BOTH, every, core))
    row, col = upper[0] | core, col_bits[0]
    got = [swap(total, BOTH, every, row)] + [swap(alone, BOTH, every, o) for o in (col | core, row | col)]
    wide, token = widen(second_values, col_count, total)
    total, gram_first = split_add([total, *got], token)
    state = (gram_first, gram_second)
    marks = [0, 40, components]
    sums = [total]
    for n, bit in enumerate(col_bits[1:]):
        if n:
            total = add(sums, state[0])
        sums = [total, swap(total, BOTH, every, bit | core)]
        if n < 2:
            state = (eliminate_part(state, marks[n], marks[n + 1], total),)

    at = me if direct else jnp.zeros((1,), jnp.int32)
    far = (1, 2, 3)
    heads, zs, sends, got = (state[0], *sums), [], [], []
    for o in far:
        *made, z, send = slab(at, wide, heads, turned, o, sends[-1] if sends else total)
        if made:
            frames, frames_again = made
            heads = (frames_again,)
        zs.append(z)
        sends.append(send)
        if direct:
            got.append(swap(send, "col", col_size, o))
    z, keep = slab(at, wide, heads, turned, 0, send)
    zs = [z] + zs

    gram_frames, state = frames_gram(frames_again, gram_second, 40, keep)
    if direct:
        keep = add([keep, *got], state)
        got = swap(keep, "col", col_size, 4)
        state = eliminate_part((state,), 40, components, keep)
        new = update(state, [keep, got])
        stacks = [new] + [swap(new, "col", col_size, o) for o in far]
    else:
        state = eliminate_part((state,), 40, components, keep)
        blocks = jnp.stack([keep, *sends]).transpose(2, 1, 0, 3).reshape(components, row_count)
        summed = lax.psum_scatter(blocks, "col", scatter_dimension=1, tiled=True)
        new = update(state, [summed[None]])[0]
        new = lax.all_gather(new, "col", axis=1, tiled=True).reshape(components, 2, 4, 128)
        stacks = list(new.transpose(2, 1, 0, 3))
    part = second(zs, stacks)
    part = add([part, swap(part, BOTH, every, core)], part)
    got = swap(part, BOTH, every, upper[0] | core)

    new_second, *sends = mode_send(part, got, gram_frames, zs[1:], BF16 if direct else F32)
    if not direct:
        keep = mode_keep(new_second, zs[0], new_second)
        blocks = jnp.stack([keep, *sends]).transpose(2, 1, 0, 3).reshape(components, row_count)
        return (frames, lax.psum_scatter(blocks, "col", scatter_dimension=1, tiled=True))
    got = [swap(x, "col", col_size, o) for o, x in zip(far, sends)]
    keep = mode_keep(new_second, zs[0], sends[0])
    mine, send = deal(me, [keep, *got], BF16)
    return (frames, mine + swap(send, "col", col_size, 4).astype(F32))


def solution(mesh):
    return jax.shard_map(
        local,
        mesh=mesh,
        in_specs=(P(None, "col", "row"), P(None, ("row", "col")), P(None, "col")),
        out_specs=(P(), P(None, ("row", "col"))),
        check_vma=False,
    )
```

```python
import functools

import jax
import jax.numpy as jnp
from jax import lax
from jax.experimental import pallas as pl
from jax.experimental.pallas import tpu as pltpu
from jax.sharding import PartitionSpec as P

ridge_weight = 0.05
HIGH = lax.Precision.HIGHEST
BOTH = ("row", "col")
F32, BF16 = jnp.float32, jnp.bfloat16
VM = pltpu.VMEM
MIB = 1 << 20
GROUP = 16


def vmem():
    return pl.BlockSpec(memory_space=VM)


def anywhere():
    return pl.BlockSpec(memory_space=pl.ANY)


def smem():
    return pl.BlockSpec(memory_space=pltpu.SMEM)


def shaped(shape, dtype=F32):
    return jax.ShapeDtypeStruct(shape, dtype)


def call(body, outs, ins, operands, name, scratch=(), mib=16, us=1):
    several = isinstance(outs, tuple)
    return pl.pallas_call(
        body,
        out_shape=outs,
        in_specs=ins,
        out_specs=(vmem(),) * len(outs) if several else vmem(),
        scratch_shapes=scratch,
        compiler_params=pltpu.CompilerParams(vmem_limit_bytes=mib * MIB),
        cost_estimate=pl.CostEstimate(flops=0, bytes_accessed=int(us * 3_000_000), transcendentals=0),
        name=name,
    )(*operands)


def dot(a, b, dims, precision=None):
    return lax.dot_general(a, b, (dims, ((), ())), precision=precision, preferred_element_type=F32)


def swaps(x, axes, count, bits):
    offsets = [0]
    for bit in bits:
        offsets = offsets + [o ^ bit for o in offsets]
    return [swap(x, axes, count, o) for o in offsets[1:]]


def swap(x, axes, count, offset):
    return lax.ppermute(x, axes, [(n, n ^ offset) for n in range(count)])


def join_body(me_ref, a_hbm, b_hbm, out_ref, turned_ref, second_ref, a_ref, b_ref, sems):
    del me_ref
    moves = [pltpu.make_async_copy(*pair, sems.at[n]) for n, pair in enumerate(((a_hbm, a_ref), (b_hbm, b_ref)))]
    for move in moves:
        move.start()
    for move in moves:
        move.wait()
    components = a_ref.shape[0]
    half = b_ref.shape[0] // 2
    out_ref[0, :components, :] = a_ref[...]
    b = b_ref[...].astype(F32)
    turned_ref[...] = b
    second_ref[...] = jnp.zeros_like(second_ref)
    second_ref[:, : b.shape[0]] = b.T
    pair = jnp.concatenate([b[:half], b[half:]], axis=1)
    pair = jnp.concatenate([pair, jnp.zeros((-half % 16, 2 * components), F32)], axis=0)
    out_ref[0, components:, :] = pair.astype(BF16)


def join(me, first, second_turned):
    components, width = first.shape
    cols = second_turned.shape[0]
    height = components + cols // 2 + (-(cols // 2) % 16)
    first = pltpu.with_memory_space_constraint(first, pltpu.HBM)
    second_turned = pltpu.with_memory_space_constraint(second_turned, pltpu.HBM)
    return call(
        join_body,
        (shaped((1, height, width), BF16), shaped((cols, components)), shaped((components, 128))),
        [smem()] + [anywhere()] * 2,
        (me, first, second_turned),
        "join",
        [VM(first.shape, BF16), VM(second_turned.shape, BF16), pltpu.SemaphoreType.DMA((2,))],
    )


def stack_body(*refs):
    *parts, after_ref, out_ref = refs
    del after_ref
    at = 0
    for part in parts:
        out_ref[at : at + part.shape[0]] = part[...]
        at += part.shape[0]


def stack(parts, after):
    shape = (sum(p.shape[0] for p in parts),) + parts[0].shape[1:]
    specs = [vmem()] * len(parts) + [anywhere()]
    return call(stack_body, shaped(shape, parts[0].dtype), specs, (*parts, after), "stack", us=0.2)


def paired(values):
    while len(values) > 1:
        values = [values[n] + values[n + 1] for n in range(0, len(values), 2)]
    return values[0]


def add_body(*refs):
    *parts, after_ref, out_ref = refs
    del after_ref
    out_ref[...] = paired([p[...] for p in parts])


def add(parts, after):
    specs = [vmem()] * len(parts) + [anywhere()]
    return call(add_body, shaped(parts[0].shape), specs, (*parts, after), "add", us=0.2)


def split_body(*refs):
    *parts, after_ref, sum_ref, gram_ref = refs
    del after_ref
    components = sum_ref.shape[0]
    sum_ref[...] = paired([p[:components] for p in parts])
    gram_ref[...] = parts[0][components:, :components] + parts[1][components:, :components]


def split_add(parts, after):
    half = parts[0].shape[0] // 2
    outs = (shaped((half, parts[0].shape[1])), shaped((half, half)))
    specs = [vmem()] * len(parts) + [anywhere()]
    return call(split_body, outs, specs, (*parts, after), "split_add", us=0.2)


def core_add_body(a_ref, b_ref, out_ref, sum_ref):
    total = a_ref[...] + b_ref[...]
    out_ref[...] = total
    sum_ref[...] = total[: sum_ref.shape[0]]


def core_add(a, b):
    outs = (shaped(a.shape), shaped((a.shape[0] // 2, a.shape[1])))
    return call(core_add_body, outs, [vmem()] * 2, (a, b), "core_add", us=0.2)


def prepare_body(at, cols, here, ahead, t_ref, after_ref, *refs):
    del after_ref
    slab_ref = refs[0] if here else None
    refs = list(refs[1:] if here else refs)
    out_ref, token_ref = refs[:2]
    next_ref = refs.pop(2) if ahead else None
    sems = refs[-1]
    slab_ref = slab_ref if here else refs[2]
    blocks = slab_ref.shape[0]

    def fetch(n, to_ref, start, sem):
        return pltpu.make_async_copy(
            t_ref.at[pl.ds(n * GROUP, GROUP), pl.ds(start, to_ref.shape[2])], to_ref.at[n], sems.at[sem, n]
        )

    if not here:
        for n in range(blocks):
            fetch(n, slab_ref, at, 0).start()
    if ahead:
        for n in range(blocks):
            fetch(n, next_ref, at + cols, 1).start()
    token_ref[...] = jnp.zeros_like(token_ref)
    to = lax.broadcasted_iota(jnp.int32, (256, 256), 0)
    of = lax.broadcasted_iota(jnp.int32, (256, 256), 1)
    turn = jnp.where((to // GROUP) + (to % GROUP) * GROUP == of, 1.0, 0.0).astype(BF16)

    def step(n, _):
        if not here:
            fetch(n, slab_ref, at, 0).wait()
        for g in range(0, cols, GROUP):
            block = slab_ref[n, :, g : g + GROUP, :].reshape(GROUP * GROUP, -1)
            turned = dot(turn, block, ((1,), (0,))).astype(BF16).reshape(GROUP, GROUP, -1)
            out_ref[g : g + GROUP, pl.ds(pl.multiple_of(n * GROUP, GROUP), GROUP), :] = turned
        return 0

    lax.fori_loop(0, blocks, step, 0)
    if ahead:
        for n in range(blocks):
            fetch(n, next_ref, at + cols, 1).wait()


def prepare(tensor, at, cols, fetched, next_cols, after):
    frames, _, rows = tensor.shape
    blocks = frames // GROUP
    outs = (VM((cols, frames, rows), BF16), shaped((8, 128)))
    if next_cols:
        outs += (VM((blocks, GROUP, next_cols, rows), BF16),)
    scratch = [] if fetched else [VM((blocks, GROUP, cols, rows), BF16)]
    got = call(
        functools.partial(prepare_body, at, cols, bool(fetched), bool(next_cols)),
        outs,
        [anywhere(), anywhere()] + [vmem()] * len(fetched),
        (tensor, after, *fetched),
        "prepare",
        scratch + [pltpu.SemaphoreType.DMA((2, blocks))],
        us=cols / 8,
    )
    return got[:2], list(got[2:])


def widen_body(b_ref, after_ref, out_ref, token_ref):
    del after_ref
    token_ref[...] = jnp.zeros_like(token_ref)
    for j in range(out_ref.shape[0]):
        out_ref[j] = jnp.broadcast_to(b_ref[:, j : j + 1], out_ref.shape[1:])


def widen(second, cols, after):
    specs = [vmem(), anywhere()]
    outs = (VM((cols, second.shape[0], 128), F32), shaped((8, 128)))
    return call(widen_body, outs, specs, (second, after), "widen")


def place(at, blocks, width, full_ref):
    for offset, block in blocks:
        if len(blocks) == 1:
            full_ref[...] = block.astype(full_ref.dtype)
        else:
            lanes = pl.ds(pl.multiple_of((at ^ offset) * width, width), width)
            full_ref[:, lanes] = block.astype(full_ref.dtype)


def assemble_first_body(offsets, me_ref, *refs):
    stacks, (turned_ref, gram_ref, other_ref), (full_ref, every_ref) = refs[:-6], refs[-5:-2], refs[-2:]
    components = full_ref.shape[0]
    blocks = [s[n] for s in stacks for n in range(s.shape[0])]
    width = blocks[0].shape[1]
    place(me_ref[0] & 7, [(o, b[:components]) for o, b in zip(offsets, blocks)], width, full_ref)
    full = full_ref[...]
    gram_ref[...] = dot(full.astype(BF16), full.astype(BF16), ((1,), (1,)))
    turned_ref[...] = full.T.astype(BF16)
    height = blocks[0].shape[0] - components
    for o, b in zip(offsets, blocks):
        every_ref[pl.ds(pl.multiple_of(((me_ref[0] & 7) ^ o) * height, height), height), :] = b[components:].astype(F32)
    every = every_ref[...].T.astype(BF16)
    both = dot(every, every, ((1,), (1,)))
    other_ref[...] = both[:components, :components] + both[components:, components:]


def assemble_first(me, stacks, after, offsets, components, rows):
    height = stacks[0].shape[1] - components
    square = shaped((components, components))
    return call(
        functools.partial(assemble_first_body, offsets),
        (shaped((rows, components), BF16), square, square),
        [smem()] + [vmem()] * len(stacks) + [anywhere()],
        (me, *stacks, after),
        "assemble_first",
        [VM((components, rows), F32), VM((height * len(offsets), 2 * components), F32)],
    )


def project_body(span, turned_ref, second_ref, gram_ref, *refs):
    *t_refs, out_ref = refs
    components = turned_ref.shape[1]
    weights = turned_ref[...]
    total, at = 0.0, 0
    for t_ref in t_refs:
        cols, frames, rows = t_ref.shape

        def step(n, total, t_ref=t_ref, at=at):
            block = t_ref[pl.ds(n * span, span)].reshape(span * frames, rows)
            product = dot(block, weights, ((1,), (0,))).reshape(span, frames, components)
            scale = second_ref[pl.ds(pl.multiple_of(at + n * span, span), span), :]
            for s in range(span):
                total = total + product[s] * scale[s : s + 1, :]
            return total

        total = lax.fori_loop(0, cols // span, step, total + jnp.zeros((frames, components), F32))
        at += cols
    out_ref[:components] = total.T
    gram = gram_ref[...]
    out_ref[components:] = jnp.concatenate([gram, gram], axis=1)


def project(first_turned, second_turned, gram, turned):
    components, frames = first_turned.shape[1], turned[0].shape[1]
    return call(
        functools.partial(project_body, 8),
        shaped((2 * components, frames)),
        [vmem()] * (3 + len(turned)),
        (first_turned, second_turned, gram, *turned),
        "project",
        us=5,
    )


def eliminate(matrix, start, stop, span=8):
    size = matrix.shape[0]
    row_at = lax.broadcasted_iota(jnp.int32, (size, size), 0)
    col_at = lax.broadcasted_iota(jnp.int32, (size, size), 1)
    lane = col_at[:1]
    for k in range(start, stop, span):
        among = range(span)
        cols = [jnp.broadcast_to(matrix[:, k + n : k + n + 1], matrix.shape) for n in among]
        mine = (lane >= k) & (lane < k + span)
        rows = [
            jnp.where(mine, jnp.where(lane == k + m, 1.0, 0.0), matrix[k + m : k + m + 1]) for m in among
        ]
        block = [[cols[n][k + m : k + m + 1] for n in among] for m in among]
        for m in among:
            pivot = 1.0 / block[m][m]
            rows[m] = rows[m] * pivot
            for n in range(m + 1, span):
                block[m][n] = block[m][n] * pivot
            for other in among:
                if other != m:
                    factor = block[other][m]
                    rows[other] = rows[other] - factor * rows[m]
                    for n in range(m + 1, span):
                        block[other][n] = block[other][n] - factor * block[m][n]
        rest = jnp.where((col_at >= k) & (col_at < k + span), 0.0, matrix)
        taken = cols[0] * rows[0]
        for n in range(1, span):
            taken = taken + cols[n] * rows[n]
        matrix = rest - taken
        for m in among:
            matrix = jnp.where(row_at == k + m, rows[m], matrix)
    return matrix


def ridged(gram):
    row_at = lax.broadcasted_iota(jnp.int32, gram.shape, 0)
    col_at = lax.broadcasted_iota(jnp.int32, gram.shape, 1)
    return gram + jnp.where(row_at == col_at, ridge_weight, 0.0)


def eliminate_body(start, stop, first, *refs):
    *ins, after_ref, out_ref = refs
    del after_ref
    matrix = ridged(ins[0][...] * ins[1][...]) if first else ins[0][...]
    out_ref[...] = eliminate(matrix, start, stop)


def eliminate_part(operands, start, stop, after):
    return call(
        functools.partial(eliminate_body, start, stop, len(operands) == 2),
        shaped(operands[0].shape),
        [vmem()] * len(operands) + [anywhere()],
        (*operands, after),
        "eliminate",
    )


def block_lanes(me_ref, offset, upper):
    at = pl.multiple_of((((me_ref[0] & 3) ^ offset) + 4 * upper) * 128, 128)
    return pl.ds(at, 128)


def slab_body(groups, offsets, head_count, me_ref, wide_ref, *refs):
    heads, t_refs, refs = refs[:head_count], refs[head_count : head_count + groups], refs[head_count + groups :]
    if head_count > 1:
        frames_ref, copy_ref, *refs = refs
        frames = dot(heads[0][...], paired([h[...] for h in heads[1:]]), ((1,), (0,)), HIGH)
        frames_ref[...] = frames
        copy_ref[...] = frames
    else:
        frames = heads[0][...]
    z_ref, *outs = refs
    components, depth = frames.shape
    high = frames.astype(BF16)
    none = jnp.zeros_like(high)
    both = jnp.concatenate([jnp.concatenate(pair, axis=1) for pair in ((high, none), (none, high))], axis=0)
    wide = 256
    for place_at, (offset, out_ref) in enumerate(zip(offsets, outs)):
        lanes = [block_lanes(me_ref, offset, n) for n in range(2)]
        store = pl.ds(place_at * wide, wide)
        total = jnp.zeros((components, wide), F32)
        base = 0
        for t_ref in t_refs:

            def step(n, total, t_ref=t_ref, base=base):
                for s in range(0, 8, 2):
                    rows = pl.ds(n * 8 + s, 2)
                    block = jnp.concatenate([t_ref[rows, :, at].reshape(2 * depth, 128) for at in lanes], axis=1)
                    product = dot(both, block, ((1,), (0,)))
                    for h in range(2):
                        j = n * 8 + s + h
                        z = product[h * components : h * components + components]
                        z_ref[base + j, :, store] = z
                        scale = wide_ref[base + j]
                        total = total + z * jnp.concatenate([scale, scale], axis=1)
                return total

            total = lax.fori_loop(0, t_ref.shape[0] // 8, step, total)
            base += t_ref.shape[0]
        for n in range(2):
            out_ref[n] = total[:, n * 128 : n * 128 + 128]


def slab(me, wide, heads, turned, offsets):
    _, frames, _ = turned[0].shape
    cols, components, _ = wide.shape
    outs = (VM((cols, components, 256 * len(offsets)), F32),) + (shaped((2, components, 128)),) * len(offsets)
    if len(heads) > 1:
        outs = (shaped((components, frames)),) * 2 + outs
    return call(
        functools.partial(slab_body, len(turned), offsets, len(heads)),
        outs,
        [smem()] + [vmem()] * (1 + len(heads) + len(turned)),
        (me, wide, *heads, *turned),
        "slab",
        us=2 * len(offsets),
    )


def frames_gram_body(stop, frames_ref, other_ref, after_ref, gram_ref, out_ref):
    del after_ref
    frames = frames_ref[...]
    gram = dot(frames, frames, ((1,), (1,)), HIGH)
    gram_ref[...] = gram
    out_ref[...] = eliminate(ridged(gram * other_ref[...]), 0, stop)


def frames_gram(frames, other, stop, after):
    square = shaped(other.shape)
    return call(
        functools.partial(frames_gram_body, stop),
        (square, square),
        [vmem(), vmem(), anywhere()],
        (frames, other, after),
        "frames_gram",
        us=2,
    )


def update_body(inverse_ref, *refs):
    *parts, out_ref = refs
    for n in range(out_ref.shape[0]):
        summed = paired([p[n] for p in parts])
        out_ref[n] = dot(inverse_ref[...], summed, ((1,), (0,)), HIGH).astype(BF16)


def update(inverse_now, parts):
    return call(
        update_body,
        shaped(parts[0].shape, BF16),
        [vmem()] * (1 + len(parts)),
        (inverse_now, *parts),
        "update",
    )


def second_body(*refs):
    *stacks, kept_ref, sent_ref, out_ref, full_ref = refs
    cols, components, near = kept_ref.shape
    blocks = [s[n] for s in stacks for n in range(s.shape[0])]
    for n, block in enumerate(blocks):
        full_ref[:, n * 128 : n * 128 + 128] = block.astype(F32)
    lane = lax.broadcasted_iota(jnp.int32, (8, 128), 1)

    def step(n, _):
        at = pl.ds(pl.multiple_of(n * 8, 8), 8)
        mine = full_ref[at, :]
        total = jnp.zeros((8, 128), F32)
        for j in range(cols):
            products = kept_ref[j, at, :] * mine[:, :near], sent_ref[j, at, :] * mine[:, near:]
            folds = [p[:, c : c + 128] for p in products for c in range(0, p.shape[1], 128)]
            folded = paired(folds)
            total = jnp.where(lane == j, jnp.sum(folded, axis=1, keepdims=True), total)
        out_ref[at, :] = total
        return 0

    lax.fori_loop(0, components // 8, step, 0)
    full = full_ref[...].astype(BF16)
    gram = dot(full, full, ((1,), (1,)))
    out_ref[...] = jnp.concatenate([out_ref[:, :components], gram], axis=1)


def second(stacks, kept, sent):
    components = kept.shape[1]
    return call(
        second_body,
        shaped((components, 2 * components)),
        [vmem()] * (2 + len(stacks)),
        (*stacks, kept, sent),
        "second",
        [VM((components, kept.shape[2] + sent.shape[2]), F32)],
        us=2,
    )


def mode_sums(new_ref, z_ref, out_refs):
    components = new_ref.shape[0]

    def step(n, _):
        at = pl.ds(pl.multiple_of(n * 8, 8), 8)
        scale = new_ref[at, :]
        total = jnp.zeros((8, z_ref.shape[2]), F32)
        for j in range(z_ref.shape[0]):
            total = total + z_ref[j, at, :] * scale[:, j : j + 1]
        for p, out_ref in enumerate(out_refs):
            for h in range(2):
                lane = 256 * p + 128 * h
                out_ref[h, at, :] = total[:, lane : lane + 128]
        return 0

    lax.fori_loop(0, components // 8, step, 0)


def mode_send_body(mine_ref, got_ref, gram_frames_ref, sent_ref, new_ref, *refs):
    outs, sums = refs[:3], refs[3:]
    components = new_ref.shape[0]
    summed = mine_ref[...] + got_ref[...]
    solver = eliminate(ridged(summed[:, components:] * gram_frames_ref[...]), 0, components)
    new_ref[...] = dot(solver, summed, ((1,), (0,)), HIGH)
    mode_sums(new_ref, sent_ref, sums)
    for out_ref, sum_ref in zip(outs, sums):
        out_ref[...] = sum_ref[...].astype(out_ref.dtype)


def mode_send(mine, got, gram_frames, sent, kind):
    components = sent.shape[1]
    shape = (2, components, 128)
    return call(
        mode_send_body,
        (shaped((components, 2 * components)),) + (shaped(shape, kind),) * 3,
        [vmem()] * 4,
        (mine, got, gram_frames, sent),
        "mode_send",
        [VM(shape, F32)] * 3,
        us=4,
    )


def mode_keep_body(new_ref, kept_ref, after_ref, out_ref):
    del after_ref
    mode_sums(new_ref, kept_ref, [out_ref])


def mode_keep(new, kept, after):
    return call(
        mode_keep_body,
        shaped((2, kept.shape[1], 128)),
        [vmem()] * 2 + [anywhere()],
        (new, kept, after),
        "mode_keep",
        us=0.5,
    )


def deal_body(me_ref, *refs):
    *parts, mine_ref, out_ref = refs
    upper = (me_ref[0] >> 2) & 1
    own, other = (paired([p[at].astype(F32) for p in parts]) for at in (upper, 1 - upper))
    mine_ref[...] = own
    out_ref[...] = other.astype(out_ref.dtype)


def deal(me, parts, kind):
    shape = parts[0].shape[1:]
    return call(
        deal_body,
        (shaped(shape), shaped(shape, kind)),
        [smem()] + [vmem()] * len(parts),
        (me, *parts),
        "deal",
        us=0.2,
    )


def local(tensor, first_factor, second_factor):
    frame_count, col_count, row_count = tensor.shape
    components = first_factor.shape[0]
    row_size, col_size = lax.axis_size("row"), lax.axis_size("col")
    every = row_size * col_size
    width = row_count // col_size
    direct = width % 128 == 0 and col_size == 8
    me = lax.axis_index(BOTH).astype(jnp.int32).reshape(1)
    col_bits = [1 << b for b in range(col_size.bit_length() - 1)]
    row_bits = [col_size << b for b in range(row_size.bit_length() - 1)]
    tensor = pltpu.with_memory_space_constraint(tensor, pltpu.HBM)
    cuts = [(0, GROUP), (GROUP, GROUP), (2 * GROUP, col_count - 2 * GROUP)]

    turned = []
    order = [0, 4, 2, 6, 1, 5, 3, 7]
    ends = [cols for _, cols in cuts[1:]] + [0]
    fetched = []
    if direct:
        have, second_turned, second_values = join(me, first_factor, second_factor.T)
    else:
        have = second_values = second_factor.astype(F32)
        second_turned = second_values.T
    for (at, cols), following, bit in zip(cuts, ends, (4, 2, 1)):
        if direct:
            got = swap(have, "col", col_size, bit)
        (t, token), fetched = prepare(tensor, at, cols, fetched, following, have)
        turned.append(t)
        if direct and bit > 1:
            have = stack([have, got], token)
    if direct:
        first_turned, gram_first, gram_second = assemble_first(
            me, [have, got], token, order, components, row_count
        )
    else:
        full = lax.all_gather(first_factor, "col", axis=1, tiled=True)
        others = lax.all_gather(second_factor, "col", axis=1, tiled=True)
        first_turned = full.T
        gram_first = jnp.dot(full, full.T, preferred_element_type=F32)
        gram_second = jnp.dot(others, others.T, preferred_element_type=F32)

    total = project(first_turned, second_turned, gram_first, turned)
    core, upper = row_bits[0], row_bits[1:]
    total, alone = core_add(total, swap(total, BOTH, every, core))
    row, col = upper[0] | core, col_bits[0]
    got = [swap(total, BOTH, every, row)] + [swap(alone, BOTH, every, o) for o in (col | core, row | col)]
    wide, token = widen(second_values, col_count, total)
    total, gram_first = split_add([total, *got], token)
    state = (gram_first, gram_second)
    marks = [0, 40, components]
    sums = [total]
    for n, bit in enumerate(col_bits[1:]):
        if n:
            total = add(sums, state[0])
        sums = [total, swap(total, BOTH, every, bit | core)]
        if n < 2:
            state = (eliminate_part(state, marks[n], marks[n + 1], total),)

    at = me if direct else jnp.zeros((1,), jnp.int32)
    near, far = (0,), (1, 2, 3)
    frames, frames_again, sent, *sends = slab(at, wide, (state[0], *sums), turned, far)
    if direct:
        got = [swap(x, "col", col_size, o) for o, x in zip(far, sends)]
    kept, keep = slab(at, wide, (frames_again,), turned, near)

    gram_frames, state = frames_gram(frames_again, gram_second, 40, keep)
    if direct:
        keep = add([keep, *got], state)
        got = swap(keep, "col", col_size, 4)
        state = eliminate_part((state,), 40, components, keep)
        new = update(state, [keep, got])
        stacks = [new] + [swap(new, "col", col_size, o) for o in far]
    else:
        state = eliminate_part((state,), 40, components, keep)
        blocks = jnp.stack([keep, *sends]).transpose(2, 1, 0, 3).reshape(components, row_count)
        summed = lax.psum_scatter(blocks, "col", scatter_dimension=1, tiled=True)
        new = update(state, [summed[None]])[0]
        new = lax.all_gather(new, "col", axis=1, tiled=True).reshape(components, 2, 4, 128)
        stacks = list(new.transpose(2, 1, 0, 3))
    part = second(stacks, kept, sent)
    part = add([part, swap(part, BOTH, every, core)], part)
    got = swap(part, BOTH, every, upper[0] | core)

    new_second, *sends = mode_send(part, got, gram_frames, sent, BF16 if direct else F32)
    if not direct:
        keep = mode_keep(new_second, kept, new_second)
        blocks = jnp.stack([keep, *sends]).transpose(2, 1, 0, 3).reshape(components, row_count)
        return (frames, lax.psum_scatter(blocks, "col", scatter_dimension=1, tiled=True))
    got = [swap(x, "col", col_size, o) for o, x in zip(far, sends)]
    keep = mode_keep(new_second, kept, sends[0])
    mine, send = deal(me, [keep, *got], BF16)
    return (frames, mine + swap(send, "col", col_size, 4).astype(F32))


def solution(mesh):
    return jax.shard_map(
        local,
        mesh=mesh,
        in_specs=(P(None, "col", "row"), P(None, ("row", "col")), P(None, "col")),
        out_specs=(P(), P(None, ("row", "col"))),
        check_vma=False,
    )
```

```python
import functools

import jax
import jax.numpy as jnp
from jax import lax
from jax.experimental import pallas as pl
from jax.experimental.pallas import tpu as pltpu
from jax.sharding import PartitionSpec as P

ridge_weight = 0.05
HIGH = lax.Precision.HIGHEST
BOTH = ("row", "col")
F32, BF16 = jnp.float32, jnp.bfloat16
VM = pltpu.VMEM
MIB = 1 << 20
GROUP = 16


def vmem():
    return pl.BlockSpec(memory_space=VM)


def anywhere():
    return pl.BlockSpec(memory_space=pl.ANY)


def smem():
    return pl.BlockSpec(memory_space=pltpu.SMEM)


def shaped(shape, dtype=F32):
    return jax.ShapeDtypeStruct(shape, dtype)


def call(body, outs, ins, operands, name, scratch=(), mib=16, us=1):
    several = isinstance(outs, tuple)
    return pl.pallas_call(
        body,
        out_shape=outs,
        in_specs=ins,
        out_specs=(vmem(),) * len(outs) if several else vmem(),
        scratch_shapes=scratch,
        compiler_params=pltpu.CompilerParams(vmem_limit_bytes=mib * MIB),
        cost_estimate=pl.CostEstimate(flops=0, bytes_accessed=int(us * 3_000_000), transcendentals=0),
        name=name,
    )(*operands)


def dot(a, b, dims, precision=None):
    return lax.dot_general(a, b, (dims, ((), ())), precision=precision, preferred_element_type=F32)


def swaps(x, axes, count, bits):
    offsets = [0]
    for bit in bits:
        offsets = offsets + [o ^ bit for o in offsets]
    return [swap(x, axes, count, o) for o in offsets[1:]]


def swap(x, axes, count, offset):
    return lax.ppermute(x, axes, [(n, n ^ offset) for n in range(count)])


def join_body(me_ref, a_hbm, b_hbm, out_ref, turned_ref, second_ref, a_ref, b_ref, sems):
    del me_ref
    moves = [pltpu.make_async_copy(*pair, sems.at[n]) for n, pair in enumerate(((a_hbm, a_ref), (b_hbm, b_ref)))]
    for move in moves:
        move.start()
    for move in moves:
        move.wait()
    components = a_ref.shape[0]
    half = b_ref.shape[0] // 2
    out_ref[0, :components, :] = a_ref[...]
    b = b_ref[...].astype(F32)
    turned_ref[...] = b
    second_ref[...] = jnp.zeros_like(second_ref)
    second_ref[:, : b.shape[0]] = b.T
    pair = jnp.concatenate([b[:half], b[half:]], axis=1)
    pair = jnp.concatenate([pair, jnp.zeros((-half % 16, 2 * components), F32)], axis=0)
    out_ref[0, components:, :] = pair.astype(BF16)


def join(me, first, second_turned):
    components, width = first.shape
    cols = second_turned.shape[0]
    height = components + cols // 2 + (-(cols // 2) % 16)
    first = pltpu.with_memory_space_constraint(first, pltpu.HBM)
    second_turned = pltpu.with_memory_space_constraint(second_turned, pltpu.HBM)
    return call(
        join_body,
        (shaped((1, height, width), BF16), shaped((cols, components)), shaped((components, 128))),
        [smem()] + [anywhere()] * 2,
        (me, first, second_turned),
        "join",
        [VM(first.shape, BF16), VM(second_turned.shape, BF16), pltpu.SemaphoreType.DMA((2,))],
    )


def stack_body(*refs):
    *parts, after_ref, out_ref = refs
    del after_ref
    at = 0
    for part in parts:
        out_ref[at : at + part.shape[0]] = part[...]
        at += part.shape[0]


def stack(parts, after):
    shape = (sum(p.shape[0] for p in parts),) + parts[0].shape[1:]
    specs = [vmem()] * len(parts) + [anywhere()]
    return call(stack_body, shaped(shape, parts[0].dtype), specs, (*parts, after), "stack", us=0.2)


def paired(values):
    while len(values) > 1:
        values = [values[n] + values[n + 1] for n in range(0, len(values), 2)]
    return values[0]


def add_body(*refs):
    *parts, after_ref, out_ref = refs
    del after_ref
    out_ref[...] = paired([p[...] for p in parts])


def add(parts, after):
    specs = [vmem()] * len(parts) + [anywhere()]
    return call(add_body, shaped(parts[0].shape), specs, (*parts, after), "add", us=0.2)


def split_body(*refs):
    *parts, sum_ref, gram_ref = refs
    components = sum_ref.shape[0]
    sum_ref[...] = paired([p[:components] for p in parts])
    gram_ref[...] = parts[0][components:, :components] + parts[1][components:, :components]


def split_add(parts):
    half = parts[0].shape[0] // 2
    outs = (shaped((half, parts[0].shape[1])), shaped((half, half)))
    return call(split_body, outs, [vmem()] * len(parts), parts, "split_add", us=0.2)


def core_add_body(a_ref, b_ref, out_ref, sum_ref):
    total = a_ref[...] + b_ref[...]
    out_ref[...] = total
    sum_ref[...] = total[: sum_ref.shape[0]]


def core_add(a, b):
    outs = (shaped(a.shape), shaped((a.shape[0] // 2, a.shape[1])))
    return call(core_add_body, outs, [vmem()] * 2, (a, b), "core_add", us=0.2)


def prepare_body(at, cols, here, ahead, t_ref, b_ref, after_ref, *refs):
    del after_ref
    slab_ref = refs[0] if here else None
    refs = list(refs[1:] if here else refs)
    out_ref, wide_ref, token_ref = refs[:3]
    next_ref = refs.pop(3) if ahead else None
    sems = refs[-1]
    slab_ref = slab_ref if here else refs[3]
    blocks = slab_ref.shape[0]

    def fetch(n, to_ref, start, sem):
        return pltpu.make_async_copy(
            t_ref.at[pl.ds(n * GROUP, GROUP), pl.ds(start, to_ref.shape[2])], to_ref.at[n], sems.at[sem, n]
        )

    if not here:
        for n in range(blocks):
            fetch(n, slab_ref, at, 0).start()
    if ahead:
        for n in range(blocks):
            fetch(n, next_ref, at + cols, 1).start()
    token_ref[...] = jnp.zeros_like(token_ref)
    for j in range(cols):
        wide_ref[j] = jnp.broadcast_to(b_ref[:, at + j : at + j + 1], wide_ref.shape[1:])
    to = lax.broadcasted_iota(jnp.int32, (256, 256), 0)
    of = lax.broadcasted_iota(jnp.int32, (256, 256), 1)
    turn = jnp.where((to // GROUP) + (to % GROUP) * GROUP == of, 1.0, 0.0).astype(BF16)

    def step(n, _):
        if not here:
            fetch(n, slab_ref, at, 0).wait()
        for g in range(0, cols, GROUP):
            block = slab_ref[n, :, g : g + GROUP, :].reshape(GROUP * GROUP, -1)
            turned = dot(turn, block, ((1,), (0,))).astype(BF16).reshape(GROUP, GROUP, -1)
            out_ref[g : g + GROUP, pl.ds(pl.multiple_of(n * GROUP, GROUP), GROUP), :] = turned
        return 0

    lax.fori_loop(0, blocks, step, 0)
    if ahead:
        for n in range(blocks):
            fetch(n, next_ref, at + cols, 1).wait()


def prepare(tensor, second, at, cols, fetched, next_cols, after):
    frames, _, rows = tensor.shape
    components = second.shape[0]
    blocks = frames // GROUP
    outs = (VM((cols, frames, rows), BF16), VM((cols, components, 128), F32), shaped((8, 128)))
    if next_cols:
        outs += (VM((blocks, GROUP, next_cols, rows), BF16),)
    scratch = [] if fetched else [VM((blocks, GROUP, cols, rows), BF16)]
    got = call(
        functools.partial(prepare_body, at, cols, bool(fetched), bool(next_cols)),
        outs,
        [anywhere(), vmem(), anywhere()] + [vmem()] * len(fetched),
        (tensor, second, after, *fetched),
        "prepare",
        scratch + [pltpu.SemaphoreType.DMA((2, blocks))],
        us=cols / 8,
    )
    return got[:3], list(got[3:])


def place(at, blocks, width, full_ref):
    for offset, block in blocks:
        if len(blocks) == 1:
            full_ref[...] = block.astype(full_ref.dtype)
        else:
            lanes = pl.ds(pl.multiple_of((at ^ offset) * width, width), width)
            full_ref[:, lanes] = block.astype(full_ref.dtype)


def assemble_first_body(offsets, me_ref, *refs):
    stacks, (turned_ref, gram_ref, other_ref), (full_ref, every_ref) = refs[:-6], refs[-5:-2], refs[-2:]
    components = full_ref.shape[0]
    blocks = [s[n] for s in stacks for n in range(s.shape[0])]
    width = blocks[0].shape[1]
    place(me_ref[0] & 7, [(o, b[:components]) for o, b in zip(offsets, blocks)], width, full_ref)
    full = full_ref[...]
    gram_ref[...] = dot(full.astype(BF16), full.astype(BF16), ((1,), (1,)))
    turned_ref[...] = full.T.astype(BF16)
    height = blocks[0].shape[0] - components
    for o, b in zip(offsets, blocks):
        every_ref[pl.ds(pl.multiple_of(((me_ref[0] & 7) ^ o) * height, height), height), :] = b[components:].astype(F32)
    every = every_ref[...].T.astype(BF16)
    both = dot(every, every, ((1,), (1,)))
    other_ref[...] = both[:components, :components] + both[components:, components:]


def assemble_first(me, stacks, after, offsets, components, rows):
    height = stacks[0].shape[1] - components
    square = shaped((components, components))
    return call(
        functools.partial(assemble_first_body, offsets),
        (shaped((rows, components), BF16), square, square),
        [smem()] + [vmem()] * len(stacks) + [anywhere()],
        (me, *stacks, after),
        "assemble_first",
        [VM((components, rows), F32), VM((height * len(offsets), 2 * components), F32)],
    )


def project_body(span, turned_ref, second_ref, gram_ref, *refs):
    *t_refs, out_ref = refs
    components = turned_ref.shape[1]
    weights = turned_ref[...]
    total, at = 0.0, 0
    for t_ref in t_refs:
        cols, frames, rows = t_ref.shape

        def step(n, total, t_ref=t_ref, at=at):
            block = t_ref[pl.ds(n * span, span)].reshape(span * frames, rows)
            product = dot(block, weights, ((1,), (0,))).reshape(span, frames, components)
            scale = second_ref[pl.ds(pl.multiple_of(at + n * span, span), span), :]
            for s in range(span):
                total = total + product[s] * scale[s : s + 1, :]
            return total

        total = lax.fori_loop(0, cols // span, step, total + jnp.zeros((frames, components), F32))
        at += cols
    out_ref[:components] = total.T
    gram = gram_ref[...]
    out_ref[components:] = jnp.concatenate([gram, gram], axis=1)


def project(first_turned, second_turned, gram, turned):
    components, frames = first_turned.shape[1], turned[0].shape[1]
    return call(
        functools.partial(project_body, 8),
        shaped((2 * components, frames)),
        [vmem()] * (3 + len(turned)),
        (first_turned, second_turned, gram, *turned),
        "project",
        us=5,
    )


def eliminate(matrix, start, stop, span=4):
    size = matrix.shape[0]
    row_at = lax.broadcasted_iota(jnp.int32, (size, size), 0)
    col_at = lax.broadcasted_iota(jnp.int32, (size, size), 1)
    lane = col_at[:1]
    for k in range(start, stop, span):
        among = range(span)
        cols = [jnp.broadcast_to(matrix[:, k + n : k + n + 1], matrix.shape) for n in among]
        mine = (lane >= k) & (lane < k + span)
        rows = [
            jnp.where(mine, jnp.where(lane == k + m, 1.0, 0.0), matrix[k + m : k + m + 1]) for m in among
        ]
        block = [[cols[n][k + m : k + m + 1] for n in among] for m in among]
        for m in among:
            pivot = 1.0 / block[m][m]
            rows[m] = rows[m] * pivot
            for n in range(m + 1, span):
                block[m][n] = block[m][n] * pivot
            for other in among:
                if other != m:
                    factor = block[other][m]
                    rows[other] = rows[other] - factor * rows[m]
                    for n in range(m + 1, span):
                        block[other][n] = block[other][n] - factor * block[m][n]
        rest = jnp.where((col_at >= k) & (col_at < k + span), 0.0, matrix)
        taken = cols[0] * rows[0]
        for n in range(1, span):
            taken = taken + cols[n] * rows[n]
        matrix = rest - taken
        for m in among:
            matrix = jnp.where(row_at == k + m, rows[m], matrix)
    return matrix


def ridged(gram):
    row_at = lax.broadcasted_iota(jnp.int32, gram.shape, 0)
    col_at = lax.broadcasted_iota(jnp.int32, gram.shape, 1)
    return gram + jnp.where(row_at == col_at, ridge_weight, 0.0)


def eliminate_body(start, stop, first, *refs):
    *ins, after_ref, out_ref = refs
    del after_ref
    matrix = ridged(ins[0][...] * ins[1][...]) if first else ins[0][...]
    out_ref[...] = eliminate(matrix, start, stop)


def eliminate_part(operands, start, stop, after):
    return call(
        functools.partial(eliminate_body, start, stop, len(operands) == 2),
        shaped(operands[0].shape),
        [vmem()] * len(operands) + [anywhere()],
        (*operands, after),
        "eliminate",
    )


def block_lanes(me_ref, offset, upper):
    at = pl.multiple_of((((me_ref[0] & 3) ^ offset) + 4 * upper) * 128, 128)
    return pl.ds(at, 128)


def slab_body(groups, offsets, first, me_ref, *refs):
    heads, refs = refs[: 2 if first else 1], refs[2 if first else 1 :]
    t_refs, wide_refs, refs = refs[:groups], refs[groups : 2 * groups], refs[2 * groups :]
    if first:
        frames_ref, copy_ref, *refs = refs
        frames = dot(heads[0][...], heads[1][...], ((1,), (0,)), HIGH)
        frames_ref[...] = frames
        copy_ref[...] = frames
    else:
        frames = heads[0][...]
    z_ref, *outs = refs
    components, depth = frames.shape
    high = frames.astype(BF16)
    none = jnp.zeros_like(high)
    both = jnp.concatenate([jnp.concatenate(pair, axis=1) for pair in ((high, none), (none, high))], axis=0)
    wide = 256
    for place_at, (offset, out_ref) in enumerate(zip(offsets, outs)):
        lanes = [block_lanes(me_ref, offset, n) for n in range(2)]
        store = pl.ds(place_at * wide, wide)
        total = jnp.zeros((components, wide), F32)
        base = 0
        for t_ref, wide_ref in zip(t_refs, wide_refs):

            def step(n, total, t_ref=t_ref, wide_ref=wide_ref, base=base):
                for s in range(0, 8, 2):
                    rows = pl.ds(n * 8 + s, 2)
                    block = jnp.concatenate([t_ref[rows, :, at].reshape(2 * depth, 128) for at in lanes], axis=1)
                    product = dot(both, block, ((1,), (0,)))
                    for h in range(2):
                        j = n * 8 + s + h
                        z = product[h * components : h * components + components]
                        z_ref[base + j, :, store] = z
                        scale = wide_ref[j]
                        total = total + z * jnp.concatenate([scale, scale], axis=1)
                return total

            total = lax.fori_loop(0, t_ref.shape[0] // 8, step, total)
            base += t_ref.shape[0]
        for n in range(2):
            out_ref[n] = total[:, n * 128 : n * 128 + 128]


def slab(me, heads, turned, wides, offsets):
    _, frames, _ = turned[0].shape
    components = wides[0].shape[1]
    first = len(heads) == 2
    cols = sum(t.shape[0] for t in turned)
    outs = (VM((cols, components, 256 * len(offsets)), F32),) + (shaped((2, components, 128)),) * len(offsets)
    if first:
        outs = (shaped((components, frames)),) * 2 + outs
    return call(
        functools.partial(slab_body, len(turned), offsets, first),
        outs,
        [smem()] + [vmem()] * (len(heads) + 2 * len(turned)),
        (me, *heads, *turned, *wides),
        "slab",
        us=2 * len(offsets),
    )


def frames_gram_body(stop, frames_ref, other_ref, after_ref, gram_ref, out_ref):
    del after_ref
    frames = frames_ref[...]
    gram = dot(frames, frames, ((1,), (1,)), HIGH)
    gram_ref[...] = gram
    out_ref[...] = eliminate(ridged(gram * other_ref[...]), 0, stop)


def frames_gram(frames, other, stop, after):
    square = shaped(other.shape)
    return call(
        functools.partial(frames_gram_body, stop),
        (square, square),
        [vmem(), vmem(), anywhere()],
        (frames, other, after),
        "frames_gram",
        us=2,
    )


def update_body(inverse_ref, *refs):
    *parts, out_ref = refs
    for n in range(out_ref.shape[0]):
        summed = paired([p[n] for p in parts])
        out_ref[n] = dot(inverse_ref[...], summed, ((1,), (0,)), HIGH).astype(BF16)


def update(inverse_now, parts):
    return call(
        update_body,
        shaped(parts[0].shape, BF16),
        [vmem()] * (1 + len(parts)),
        (inverse_now, *parts),
        "update",
    )


def second_body(*refs):
    *stacks, kept_ref, sent_ref, out_ref, full_ref = refs
    cols, components, near = kept_ref.shape
    blocks = [s[n] for s in stacks for n in range(s.shape[0])]
    for n, block in enumerate(blocks):
        full_ref[:, n * 128 : n * 128 + 128] = block.astype(F32)
    lane = lax.broadcasted_iota(jnp.int32, (8, 128), 1)

    def step(n, _):
        at = pl.ds(pl.multiple_of(n * 8, 8), 8)
        mine = full_ref[at, :]
        total = jnp.zeros((8, 128), F32)
        for j in range(cols):
            products = kept_ref[j, at, :] * mine[:, :near], sent_ref[j, at, :] * mine[:, near:]
            folds = [p[:, c : c + 128] for p in products for c in range(0, p.shape[1], 128)]
            folded = paired(folds)
            total = jnp.where(lane == j, jnp.sum(folded, axis=1, keepdims=True), total)
        out_ref[at, :] = total
        return 0

    lax.fori_loop(0, components // 8, step, 0)
    full = full_ref[...].astype(BF16)
    gram = dot(full, full, ((1,), (1,)))
    out_ref[...] = jnp.concatenate([out_ref[:, :components], gram], axis=1)


def second(stacks, kept, sent):
    components = kept.shape[1]
    return call(
        second_body,
        shaped((components, 2 * components)),
        [vmem()] * (2 + len(stacks)),
        (*stacks, kept, sent),
        "second",
        [VM((components, kept.shape[2] + sent.shape[2]), F32)],
        us=2,
    )


def mode_sums(new_ref, z_ref, out_refs):
    components = new_ref.shape[0]

    def step(n, _):
        at = pl.ds(pl.multiple_of(n * 8, 8), 8)
        scale = new_ref[at, :]
        total = jnp.zeros((8, z_ref.shape[2]), F32)
        for j in range(z_ref.shape[0]):
            total = total + z_ref[j, at, :] * scale[:, j : j + 1]
        for p, out_ref in enumerate(out_refs):
            for h in range(2):
                lane = 256 * p + 128 * h
                out_ref[h, at, :] = total[:, lane : lane + 128]
        return 0

    lax.fori_loop(0, components // 8, step, 0)


def mode_send_body(mine_ref, got_ref, gram_frames_ref, sent_ref, new_ref, *refs):
    outs, sums = refs[:3], refs[3:]
    components = new_ref.shape[0]
    summed = mine_ref[...] + got_ref[...]
    solver = eliminate(ridged(summed[:, components:] * gram_frames_ref[...]), 0, components, 8)
    new_ref[...] = dot(solver, summed, ((1,), (0,)), HIGH)
    mode_sums(new_ref, sent_ref, sums)
    for out_ref, sum_ref in zip(outs, sums):
        out_ref[...] = sum_ref[...].astype(out_ref.dtype)


def mode_send(mine, got, gram_frames, sent, kind):
    components = sent.shape[1]
    shape = (2, components, 128)
    return call(
        mode_send_body,
        (shaped((components, 2 * components)),) + (shaped(shape, kind),) * 3,
        [vmem()] * 4,
        (mine, got, gram_frames, sent),
        "mode_send",
        [VM(shape, F32)] * 3,
        us=4,
    )


def mode_keep_body(new_ref, kept_ref, after_ref, out_ref):
    del after_ref
    mode_sums(new_ref, kept_ref, [out_ref])


def mode_keep(new, kept, after):
    return call(
        mode_keep_body,
        shaped((2, kept.shape[1], 128)),
        [vmem()] * 2 + [anywhere()],
        (new, kept, after),
        "mode_keep",
        us=0.5,
    )


def deal_body(me_ref, *refs):
    *parts, mine_ref, out_ref = refs
    upper = (me_ref[0] >> 2) & 1
    own, other = (paired([p[at].astype(F32) for p in parts]) for at in (upper, 1 - upper))
    mine_ref[...] = own
    out_ref[...] = other.astype(out_ref.dtype)


def deal(me, parts, kind):
    shape = parts[0].shape[1:]
    return call(
        deal_body,
        (shaped(shape), shaped(shape, kind)),
        [smem()] + [vmem()] * len(parts),
        (me, *parts),
        "deal",
        us=0.2,
    )


def local(tensor, first_factor, second_factor):
    frame_count, col_count, row_count = tensor.shape
    components = first_factor.shape[0]
    row_size, col_size = lax.axis_size("row"), lax.axis_size("col")
    every = row_size * col_size
    width = row_count // col_size
    direct = width % 128 == 0 and col_size == 8
    me = lax.axis_index(BOTH).astype(jnp.int32).reshape(1)
    col_bits = [1 << b for b in range(col_size.bit_length() - 1)]
    row_bits = [col_size << b for b in range(row_size.bit_length() - 1)]
    tensor = pltpu.with_memory_space_constraint(tensor, pltpu.HBM)
    cuts = [(0, GROUP), (GROUP, GROUP), (2 * GROUP, col_count - 2 * GROUP)]

    turned, wides = [], []
    order = [0, 4, 2, 6, 1, 5, 3, 7]
    ends = [cols for _, cols in cuts[1:]] + [0]
    fetched = []
    if direct:
        have, second_turned, second_values = join(me, first_factor, second_factor.T)
    else:
        have = second_values = second_factor.astype(F32)
        second_turned = second_values.T
    for (at, cols), following, bit in zip(cuts, ends, (4, 2, 1)):
        if direct:
            got = swap(have, "col", col_size, bit)
        (t, w, token), fetched = prepare(tensor, second_values, at, cols, fetched, following, have)
        turned.append(t)
        wides.append(w)
        if direct and bit > 1:
            have = stack([have, got], token)
    if direct:
        first_turned, gram_first, gram_second = assemble_first(
            me, [have, got], token, order, components, row_count
        )
    else:
        full = lax.all_gather(first_factor, "col", axis=1, tiled=True)
        others = lax.all_gather(second_factor, "col", axis=1, tiled=True)
        first_turned = full.T
        gram_first = jnp.dot(full, full.T, preferred_element_type=F32)
        gram_second = jnp.dot(others, others.T, preferred_element_type=F32)

    total = project(first_turned, second_turned, gram_first, turned)
    core, upper = row_bits[0], row_bits[1:]
    total, alone = core_add(total, swap(total, BOTH, every, core))
    row, col = upper[0] | core, col_bits[0]
    got = [swap(total, BOTH, every, row)] + [swap(alone, BOTH, every, o) for o in (col | core, row | col)]
    total, gram_first = split_add([total, *got])
    state = (gram_first, gram_second)
    marks = [0, 44, components]
    for n, bit in enumerate(col_bits[1:]):
        got = swap(total, BOTH, every, bit | core)
        if n < 2:
            state = (eliminate_part(state, marks[n], marks[n + 1], total),)
        total = add([total, got], state[0])

    at = me if direct else jnp.zeros((1,), jnp.int32)
    near, far = (0,), (1, 2, 3)
    frames, frames_again, sent, *sends = slab(at, (state[0], total), turned, wides, far)
    if direct:
        got = [swap(x, "col", col_size, o) for o, x in zip(far, sends)]
    kept, keep = slab(at, (frames_again,), turned, wides, near)

    gram_frames, state = frames_gram(frames_again, gram_second, 44, keep)
    if direct:
        keep = add([keep, *got], state)
        got = swap(keep, "col", col_size, 4)
        state = eliminate_part((state,), 44, components, keep)
        new = update(state, [keep, got])
        stacks = [new] + [swap(new, "col", col_size, o) for o in far]
    else:
        state = eliminate_part((state,), 44, components, keep)
        blocks = jnp.stack([keep, *sends]).transpose(2, 1, 0, 3).reshape(components, row_count)
        summed = lax.psum_scatter(blocks, "col", scatter_dimension=1, tiled=True)
        new = update(state, [summed[None]])[0]
        new = lax.all_gather(new, "col", axis=1, tiled=True).reshape(components, 2, 4, 128)
        stacks = list(new.transpose(2, 1, 0, 3))
    part = second(stacks, kept, sent)
    part = add([part, swap(part, BOTH, every, core)], part)
    got = swap(part, BOTH, every, upper[0] | core)

    new_second, *sends = mode_send(part, got, gram_frames, sent, BF16 if direct else F32)
    if not direct:
        keep = mode_keep(new_second, kept, new_second)
        blocks = jnp.stack([keep, *sends]).transpose(2, 1, 0, 3).reshape(components, row_count)
        return (frames, lax.psum_scatter(blocks, "col", scatter_dimension=1, tiled=True))
    got = [swap(x, "col", col_size, o) for o, x in zip(far, sends)]
    keep = mode_keep(new_second, kept, sends[0])
    mine, send = deal(me, [keep, *got], BF16)
    return (frames, mine + swap(send, "col", col_size, 4).astype(F32))


def solution(mesh):
    return jax.shard_map(
        local,
        mesh=mesh,
        in_specs=(P(None, "col", "row"), P(None, ("row", "col")), P(None, "col")),
        out_specs=(P(), P(None, ("row", "col"))),
        check_vma=False,
    )
```

```python
import functools

import jax
import jax.numpy as jnp
from jax import lax
from jax.experimental import pallas as pl
from jax.experimental.pallas import tpu as pltpu
from jax.sharding import PartitionSpec as P

ridge_weight = 0.05
HIGH = lax.Precision.HIGHEST
BOTH = ("row", "col")
F32, BF16 = jnp.float32, jnp.bfloat16
VM = pltpu.VMEM
MIB = 1 << 20
GROUP = 16


def vmem():
    return pl.BlockSpec(memory_space=VM)


def anywhere():
    return pl.BlockSpec(memory_space=pl.ANY)


def smem():
    return pl.BlockSpec(memory_space=pltpu.SMEM)


def shaped(shape, dtype=F32):
    return jax.ShapeDtypeStruct(shape, dtype)


def call(body, outs, ins, operands, name, scratch=(), mib=16, us=1):
    several = isinstance(outs, tuple)
    return pl.pallas_call(
        body,
        out_shape=outs,
        in_specs=ins,
        out_specs=(vmem(),) * len(outs) if several else vmem(),
        scratch_shapes=scratch,
        compiler_params=pltpu.CompilerParams(vmem_limit_bytes=mib * MIB),
        cost_estimate=pl.CostEstimate(flops=0, bytes_accessed=int(us * 3_000_000), transcendentals=0),
        name=name,
    )(*operands)


def dot(a, b, dims, precision=None):
    return lax.dot_general(a, b, (dims, ((), ())), precision=precision, preferred_element_type=F32)


def swaps(x, axes, count, bits):
    offsets = [0]
    for bit in bits:
        offsets = offsets + [o ^ bit for o in offsets]
    return [swap(x, axes, count, o) for o in offsets[1:]]


def swap(x, axes, count, offset):
    return lax.ppermute(x, axes, [(n, n ^ offset) for n in range(count)])


def join_body(me_ref, a_hbm, b_hbm, out_ref, turned_ref, second_ref, a_ref, b_ref, sems):
    del me_ref
    moves = [pltpu.make_async_copy(*pair, sems.at[n]) for n, pair in enumerate(((a_hbm, a_ref), (b_hbm, b_ref)))]
    for move in moves:
        move.start()
    for move in moves:
        move.wait()
    components = a_ref.shape[0]
    half = b_ref.shape[0] // 2
    out_ref[0, :components, :] = a_ref[...]
    b = b_ref[...].astype(F32)
    turned_ref[...] = b
    second_ref[...] = jnp.zeros_like(second_ref)
    second_ref[:, : b.shape[0]] = b.T
    pair = jnp.concatenate([b[:half], b[half:]], axis=1)
    pair = jnp.concatenate([pair, jnp.zeros((-half % 16, 2 * components), F32)], axis=0)
    out_ref[0, components:, :] = pair.astype(BF16)


def join(me, first, second_turned):
    components, width = first.shape
    cols = second_turned.shape[0]
    height = components + cols // 2 + (-(cols // 2) % 16)
    first = pltpu.with_memory_space_constraint(first, pltpu.HBM)
    second_turned = pltpu.with_memory_space_constraint(second_turned, pltpu.HBM)
    return call(
        join_body,
        (shaped((1, height, width), BF16), shaped((cols, components)), shaped((components, 128))),
        [smem()] + [anywhere()] * 2,
        (me, first, second_turned),
        "join",
        [VM(first.shape, BF16), VM(second_turned.shape, BF16), pltpu.SemaphoreType.DMA((2,))],
    )


def stack_body(*refs):
    *parts, after_ref, out_ref = refs
    del after_ref
    at = 0
    for part in parts:
        out_ref[at : at + part.shape[0]] = part[...]
        at += part.shape[0]


def stack(parts, after):
    shape = (sum(p.shape[0] for p in parts),) + parts[0].shape[1:]
    specs = [vmem()] * len(parts) + [anywhere()]
    return call(stack_body, shaped(shape, parts[0].dtype), specs, (*parts, after), "stack", us=0.2)


def paired(values):
    while len(values) > 1:
        values = [values[n] + values[n + 1] for n in range(0, len(values), 2)]
    return values[0]


def add_body(*refs):
    *parts, after_ref, out_ref = refs
    del after_ref
    out_ref[...] = paired([p[...] for p in parts])


def add(parts, after):
    specs = [vmem()] * len(parts) + [anywhere()]
    return call(add_body, shaped(parts[0].shape), specs, (*parts, after), "add", us=0.2)


def split_body(*refs):
    *parts, sum_ref, gram_ref = refs
    components = sum_ref.shape[0]
    sum_ref[...] = paired([p[:components] for p in parts])
    gram_ref[...] = parts[0][components:, :components] + parts[1][components:, :components]


def split_add(parts):
    half = parts[0].shape[0] // 2
    outs = (shaped((half, parts[0].shape[1])), shaped((half, half)))
    return call(split_body, outs, [vmem()] * len(parts), parts, "split_add", us=0.2)


def core_add_body(a_ref, b_ref, out_ref, sum_ref):
    total = a_ref[...] + b_ref[...]
    out_ref[...] = total
    sum_ref[...] = total[: sum_ref.shape[0]]


def core_add(a, b):
    outs = (shaped(a.shape), shaped((a.shape[0] // 2, a.shape[1])))
    return call(core_add_body, outs, [vmem()] * 2, (a, b), "core_add", us=0.2)


def prepare_body(at, cols, here, ahead, t_ref, b_ref, after_ref, *refs):
    del after_ref
    refs = list(refs)
    early_ref = refs.pop(0) if here else None
    out_ref, wide_ref, token_ref = refs[:3]
    next_ref = refs.pop(3) if ahead else None
    sems = refs[-1]
    blocks = t_ref.shape[0] // GROUP
    slab_ref = refs[3] if here < blocks else None

    def fetch(n, to_ref, slot, start, sem):
        return pltpu.make_async_copy(
            t_ref.at[pl.ds(n * GROUP, GROUP), pl.ds(start, to_ref.shape[2])], to_ref.at[slot], sems.at[sem, n]
        )

    for n in range(here, blocks):
        fetch(n, slab_ref, n - here, at, 0).start()
    for n in range(ahead):
        fetch(n, next_ref, n, at + cols, 1).start()
    token_ref[...] = jnp.zeros_like(token_ref)
    for j in range(cols):
        wide_ref[j] = jnp.broadcast_to(b_ref[:, at + j : at + j + 1], wide_ref.shape[1:])
    to = lax.broadcasted_iota(jnp.int32, (256, 256), 0)
    of = lax.broadcasted_iota(jnp.int32, (256, 256), 1)
    turn = jnp.where((to // GROUP) + (to % GROUP) * GROUP == of, 1.0, 0.0).astype(BF16)

    def turn_block(n, from_ref, slot):
        for g in range(0, cols, GROUP):
            block = from_ref[slot, :, g : g + GROUP, :].reshape(GROUP * GROUP, -1)
            turned = dot(turn, block, ((1,), (0,))).astype(BF16).reshape(GROUP, GROUP, -1)
            out_ref[g : g + GROUP, pl.ds(pl.multiple_of(n * GROUP, GROUP), GROUP), :] = turned

    def early(n, _):
        turn_block(n, early_ref, n)
        return 0

    def late(n, _):
        fetch(n, slab_ref, n - here, at, 0).wait()
        turn_block(n, slab_ref, n - here)
        return 0

    if here:
        lax.fori_loop(0, here, early, 0)
    if here < blocks:
        lax.fori_loop(here, blocks, late, 0)
    for n in range(ahead):
        fetch(n, next_ref, n, at + cols, 1).wait()


def prepare(tensor, second, at, cols, fetched, next_cols, after):
    frames, _, rows = tensor.shape
    components = second.shape[0]
    blocks = frames // GROUP
    here = fetched[0].shape[0] if fetched else 0
    ahead = 0 if not next_cols else blocks if here else blocks // 2
    outs = (VM((cols, frames, rows), BF16), VM((cols, components, 128), F32), shaped((8, 128)))
    if ahead:
        outs += (VM((ahead, GROUP, next_cols, rows), BF16),)
    scratch = [VM((blocks - here, GROUP, cols, rows), BF16)] if here < blocks else []
    got = call(
        functools.partial(prepare_body, at, cols, here, ahead),
        outs,
        [anywhere(), vmem(), anywhere()] + [vmem()] * len(fetched),
        (tensor, second, after, *fetched),
        "prepare",
        scratch + [pltpu.SemaphoreType.DMA((2, blocks))],
        us=cols / 8,
    )
    return got[:3], list(got[3:])


def place(at, blocks, width, full_ref):
    for offset, block in blocks:
        if len(blocks) == 1:
            full_ref[...] = block.astype(full_ref.dtype)
        else:
            lanes = pl.ds(pl.multiple_of((at ^ offset) * width, width), width)
            full_ref[:, lanes] = block.astype(full_ref.dtype)


def assemble_first_body(offsets, me_ref, *refs):
    stacks, (turned_ref, gram_ref, other_ref), (full_ref, every_ref) = refs[:-6], refs[-5:-2], refs[-2:]
    components = full_ref.shape[0]
    blocks = [s[n] for s in stacks for n in range(s.shape[0])]
    width = blocks[0].shape[1]
    place(me_ref[0] & 7, [(o, b[:components]) for o, b in zip(offsets, blocks)], width, full_ref)
    full = full_ref[...]
    gram_ref[...] = dot(full.astype(BF16), full.astype(BF16), ((1,), (1,)))
    turned_ref[...] = full.T.astype(BF16)
    height = blocks[0].shape[0] - components
    for o, b in zip(offsets, blocks):
        every_ref[pl.ds(pl.multiple_of(((me_ref[0] & 7) ^ o) * height, height), height), :] = b[components:].astype(F32)
    every = every_ref[...].T.astype(BF16)
    both = dot(every, every, ((1,), (1,)))
    other_ref[...] = both[:components, :components] + both[components:, components:]


def assemble_first(me, stacks, after, offsets, components, rows):
    height = stacks[0].shape[1] - components
    square = shaped((components, components))
    return call(
        functools.partial(assemble_first_body, offsets),
        (shaped((rows, components), BF16), square, square),
        [smem()] + [vmem()] * len(stacks) + [anywhere()],
        (me, *stacks, after),
        "assemble_first",
        [VM((components, rows), F32), VM((height * len(offsets), 2 * components), F32)],
    )


def project_body(span, turned_ref, second_ref, gram_ref, *refs):
    *t_refs, out_ref = refs
    components = turned_ref.shape[1]
    weights = turned_ref[...]
    total, at = 0.0, 0
    for t_ref in t_refs:
        cols, frames, rows = t_ref.shape

        def step(n, total, t_ref=t_ref, at=at):
            block = t_ref[pl.ds(n * span, span)].reshape(span * frames, rows)
            product = dot(block, weights, ((1,), (0,))).reshape(span, frames, components)
            scale = second_ref[pl.ds(pl.multiple_of(at + n * span, span), span), :]
            for s in range(span):
                total = total + product[s] * scale[s : s + 1, :]
            return total

        total = lax.fori_loop(0, cols // span, step, total + jnp.zeros((frames, components), F32))
        at += cols
    out_ref[:components] = total.T
    gram = gram_ref[...]
    out_ref[components:] = jnp.concatenate([gram, gram], axis=1)


def project(first_turned, second_turned, gram, turned):
    components, frames = first_turned.shape[1], turned[0].shape[1]
    return call(
        functools.partial(project_body, 8),
        shaped((2 * components, frames)),
        [vmem()] * (3 + len(turned)),
        (first_turned, second_turned, gram, *turned),
        "project",
        us=5,
    )


def eliminate(matrix, start, stop, span=4):
    size = matrix.shape[0]
    row_at = lax.broadcasted_iota(jnp.int32, (size, size), 0)
    col_at = lax.broadcasted_iota(jnp.int32, (size, size), 1)
    lane = col_at[:1]
    for k in range(start, stop, span):
        among = range(span)
        cols = [jnp.broadcast_to(matrix[:, k + n : k + n + 1], matrix.shape) for n in among]
        mine = (lane >= k) & (lane < k + span)
        rows = [
            jnp.where(mine, jnp.where(lane == k + m, 1.0, 0.0), matrix[k + m : k + m + 1]) for m in among
        ]
        block = [[cols[n][k + m : k + m + 1] for n in among] for m in among]
        for m in among:
            pivot = 1.0 / block[m][m]
            rows[m] = rows[m] * pivot
            for n in range(m + 1, span):
                block[m][n] = block[m][n] * pivot
            for other in among:
                if other != m:
                    factor = block[other][m]
                    rows[other] = rows[other] - factor * rows[m]
                    for n in range(m + 1, span):
                        block[other][n] = block[other][n] - factor * block[m][n]
        rest = jnp.where((col_at >= k) & (col_at < k + span), 0.0, matrix)
        taken = cols[0] * rows[0]
        for n in range(1, span):
            taken = taken + cols[n] * rows[n]
        matrix = rest - taken
        for m in among:
            matrix = jnp.where(row_at == k + m, rows[m], matrix)
    return matrix


def ridged(gram):
    row_at = lax.broadcasted_iota(jnp.int32, gram.shape, 0)
    col_at = lax.broadcasted_iota(jnp.int32, gram.shape, 1)
    return gram + jnp.where(row_at == col_at, ridge_weight, 0.0)


def eliminate_body(start, stop, first, *refs):
    *ins, after_ref, out_ref = refs
    del after_ref
    matrix = ridged(ins[0][...] * ins[1][...]) if first else ins[0][...]
    out_ref[...] = eliminate(matrix, start, stop)


def eliminate_part(operands, start, stop, after):
    return call(
        functools.partial(eliminate_body, start, stop, len(operands) == 2),
        shaped(operands[0].shape),
        [vmem()] * len(operands) + [anywhere()],
        (*operands, after),
        "eliminate",
    )


def block_lanes(me_ref, offset, upper):
    at = pl.multiple_of((((me_ref[0] & 3) ^ offset) + 4 * upper) * 128, 128)
    return pl.ds(at, 128)


def slab_body(groups, offsets, first, me_ref, *refs):
    heads, refs = refs[: 2 if first else 1], refs[2 if first else 1 :]
    t_refs, wide_refs, refs = refs[:groups], refs[groups : 2 * groups], refs[2 * groups :]
    if first:
        frames_ref, copy_ref, *refs = refs
        frames = dot(heads[0][...], heads[1][...], ((1,), (0,)), HIGH)
        frames_ref[...] = frames
        copy_ref[...] = frames
    else:
        frames = heads[0][...]
    z_ref, *outs = refs
    components, depth = frames.shape
    high = frames.astype(BF16)
    none = jnp.zeros_like(high)
    both = jnp.concatenate([jnp.concatenate(pair, axis=1) for pair in ((high, none), (none, high))], axis=0)
    wide = 256
    for place_at, (offset, out_ref) in enumerate(zip(offsets, outs)):
        lanes = [block_lanes(me_ref, offset, n) for n in range(2)]
        store = pl.ds(place_at * wide, wide)
        total = jnp.zeros((components, wide), F32)
        base = 0
        for t_ref, wide_ref in zip(t_refs, wide_refs):

            def step(n, total, t_ref=t_ref, wide_ref=wide_ref, base=base):
                for s in range(0, 8, 2):
                    rows = pl.ds(n * 8 + s, 2)
                    block = jnp.concatenate([t_ref[rows, :, at].reshape(2 * depth, 128) for at in lanes], axis=1)
                    product = dot(both, block, ((1,), (0,)))
                    for h in range(2):
                        j = n * 8 + s + h
                        z = product[h * components : h * components + components]
                        z_ref[base + j, :, store] = z
                        scale = wide_ref[j]
                        total = total + z * jnp.concatenate([scale, scale], axis=1)
                return total

            total = lax.fori_loop(0, t_ref.shape[0] // 8, step, total)
            base += t_ref.shape[0]
        for n in range(2):
            out_ref[n] = total[:, n * 128 : n * 128 + 128]


def slab(me, heads, turned, wides, offsets):
    _, frames, _ = turned[0].shape
    components = wides[0].shape[1]
    first = len(heads) == 2
    cols = sum(t.shape[0] for t in turned)
    outs = (VM((cols, components, 256 * len(offsets)), F32),) + (shaped((2, components, 128)),) * len(offsets)
    if first:
        outs = (shaped((components, frames)),) * 2 + outs
    return call(
        functools.partial(slab_body, len(turned), offsets, first),
        outs,
        [smem()] + [vmem()] * (len(heads) + 2 * len(turned)),
        (me, *heads, *turned, *wides),
        "slab",
        us=2 * len(offsets),
    )


def frames_gram_body(stop, frames_ref, other_ref, after_ref, gram_ref, out_ref):
    del after_ref
    frames = frames_ref[...]
    gram = dot(frames, frames, ((1,), (1,)), HIGH)
    gram_ref[...] = gram
    out_ref[...] = eliminate(ridged(gram * other_ref[...]), 0, stop)


def frames_gram(frames, other, stop, after):
    square = shaped(other.shape)
    return call(
        functools.partial(frames_gram_body, stop),
        (square, square),
        [vmem(), vmem(), anywhere()],
        (frames, other, after),
        "frames_gram",
        us=2,
    )


def update_body(inverse_ref, *refs):
    *parts, out_ref = refs
    for n in range(out_ref.shape[0]):
        summed = paired([p[n] for p in parts])
        out_ref[n] = dot(inverse_ref[...], summed, ((1,), (0,)), HIGH).astype(BF16)


def update(inverse_now, parts):
    return call(
        update_body,
        shaped(parts[0].shape, BF16),
        [vmem()] * (1 + len(parts)),
        (inverse_now, *parts),
        "update",
    )


def second_body(*refs):
    *stacks, kept_ref, sent_ref, out_ref, full_ref = refs
    cols, components, near = kept_ref.shape
    blocks = [s[n] for s in stacks for n in range(s.shape[0])]
    for n, block in enumerate(blocks):
        full_ref[:, n * 128 : n * 128 + 128] = block.astype(F32)
    lane = lax.broadcasted_iota(jnp.int32, (8, 128), 1)

    def step(n, _):
        at = pl.ds(pl.multiple_of(n * 8, 8), 8)
        mine = full_ref[at, :]
        total = jnp.zeros((8, 128), F32)
        for j in range(cols):
            products = kept_ref[j, at, :] * mine[:, :near], sent_ref[j, at, :] * mine[:, near:]
            folds = [p[:, c : c + 128] for p in products for c in range(0, p.shape[1], 128)]
            folded = paired(folds)
            total = jnp.where(lane == j, jnp.sum(folded, axis=1, keepdims=True), total)
        out_ref[at, :] = total
        return 0

    lax.fori_loop(0, components // 8, step, 0)
    full = full_ref[...].astype(BF16)
    gram = dot(full, full, ((1,), (1,)))
    out_ref[...] = jnp.concatenate([out_ref[:, :components], gram], axis=1)


def second(stacks, kept, sent):
    components = kept.shape[1]
    return call(
        second_body,
        shaped((components, 2 * components)),
        [vmem()] * (2 + len(stacks)),
        (*stacks, kept, sent),
        "second",
        [VM((components, kept.shape[2] + sent.shape[2]), F32)],
        us=2,
    )


def mode_sums(new_ref, z_ref, out_refs):
    components = new_ref.shape[0]

    def step(n, _):
        at = pl.ds(pl.multiple_of(n * 8, 8), 8)
        scale = new_ref[at, :]
        total = jnp.zeros((8, z_ref.shape[2]), F32)
        for j in range(z_ref.shape[0]):
            total = total + z_ref[j, at, :] * scale[:, j : j + 1]
        for p, out_ref in enumerate(out_refs):
            for h in range(2):
                lane = 256 * p + 128 * h
                out_ref[h, at, :] = total[:, lane : lane + 128]
        return 0

    lax.fori_loop(0, components // 8, step, 0)


def mode_send_body(mine_ref, got_ref, gram_frames_ref, sent_ref, new_ref, *refs):
    outs, sums = refs[:3], refs[3:]
    components = new_ref.shape[0]
    summed = mine_ref[...] + got_ref[...]
    solver = eliminate(ridged(summed[:, components:] * gram_frames_ref[...]), 0, components, 8)
    new_ref[...] = dot(solver, summed, ((1,), (0,)), HIGH)
    mode_sums(new_ref, sent_ref, sums)
    for out_ref, sum_ref in zip(outs, sums):
        out_ref[...] = sum_ref[...].astype(out_ref.dtype)


def mode_send(mine, got, gram_frames, sent, kind):
    components = sent.shape[1]
    shape = (2, components, 128)
    return call(
        mode_send_body,
        (shaped((components, 2 * components)),) + (shaped(shape, kind),) * 3,
        [vmem()] * 4,
        (mine, got, gram_frames, sent),
        "mode_send",
        [VM(shape, F32)] * 3,
        us=4,
    )


def mode_keep_body(new_ref, kept_ref, after_ref, out_ref):
    del after_ref
    mode_sums(new_ref, kept_ref, [out_ref])


def mode_keep(new, kept, after):
    return call(
        mode_keep_body,
        shaped((2, kept.shape[1], 128)),
        [vmem()] * 2 + [anywhere()],
        (new, kept, after),
        "mode_keep",
        us=0.5,
    )


def deal_body(me_ref, *refs):
    *parts, mine_ref, out_ref = refs
    upper = (me_ref[0] >> 2) & 1
    own, other = (paired([p[at].astype(F32) for p in parts]) for at in (upper, 1 - upper))
    mine_ref[...] = own
    out_ref[...] = other.astype(out_ref.dtype)


def deal(me, parts, kind):
    shape = parts[0].shape[1:]
    return call(
        deal_body,
        (shaped(shape), shaped(shape, kind)),
        [smem()] + [vmem()] * len(parts),
        (me, *parts),
        "deal",
        us=0.2,
    )


def local(tensor, first_factor, second_factor):
    frame_count, col_count, row_count = tensor.shape
    components = first_factor.shape[0]
    row_size, col_size = lax.axis_size("row"), lax.axis_size("col")
    every = row_size * col_size
    width = row_count // col_size
    direct = width % 128 == 0 and col_size == 8
    me = lax.axis_index(BOTH).astype(jnp.int32).reshape(1)
    col_bits = [1 << b for b in range(col_size.bit_length() - 1)]
    row_bits = [col_size << b for b in range(row_size.bit_length() - 1)]
    tensor = pltpu.with_memory_space_constraint(tensor, pltpu.HBM)
    cuts = [(0, GROUP), (GROUP, GROUP), (2 * GROUP, col_count - 2 * GROUP)]

    turned, wides = [], []
    order = [0, 4, 2, 6, 1, 5, 3, 7]
    ends = [cols for _, cols in cuts[1:]] + [0]
    fetched = []
    if direct:
        have, second_turned, second_values = join(me, first_factor, second_factor.T)
    else:
        have = second_values = second_factor.astype(F32)
        second_turned = second_values.T
    for (at, cols), following, bit in zip(cuts, ends, (4, 2, 1)):
        if direct:
            got = swap(have, "col", col_size, bit)
        (t, w, token), fetched = prepare(tensor, second_values, at, cols, fetched, following, have)
        turned.append(t)
        wides.append(w)
        if direct and bit > 1:
            have = stack([have, got], token)
    if direct:
        first_turned, gram_first, gram_second = assemble_first(
            me, [have, got], token, order, components, row_count
        )
    else:
        full = lax.all_gather(first_factor, "col", axis=1, tiled=True)
        others = lax.all_gather(second_factor, "col", axis=1, tiled=True)
        first_turned = full.T
        gram_first = jnp.dot(full, full.T, preferred_element_type=F32)
        gram_second = jnp.dot(others, others.T, preferred_element_type=F32)

    total = project(first_turned, second_turned, gram_first, turned)
    core, upper = row_bits[0], row_bits[1:]
    total, alone = core_add(total, swap(total, BOTH, every, core))
    row, col = upper[0] | core, col_bits[0]
    got = [swap(total, BOTH, every, row)] + [swap(alone, BOTH, every, o) for o in (col | core, row | col)]
    total, gram_first = split_add([total, *got])
    state = (gram_first, gram_second)
    marks = [0, 44, components]
    for n, bit in enumerate(col_bits[1:]):
        got = swap(total, BOTH, every, bit | core)
        if n < 2:
            state = (eliminate_part(state, marks[n], marks[n + 1], total),)
        total = add([total, got], state[0])

    at = me if direct else jnp.zeros((1,), jnp.int32)
    near, far = (0,), (1, 2, 3)
    frames, frames_again, sent, *sends = slab(at, (state[0], total), turned, wides, far)
    if direct:
        got = [swap(x, "col", col_size, o) for o, x in zip(far, sends)]
    kept, keep = slab(at, (frames_again,), turned, wides, near)

    gram_frames, state = frames_gram(frames_again, gram_second, 44, keep)
    if direct:
        keep = add([keep, *got], state)
        got = swap(keep, "col", col_size, 4)
        state = eliminate_part((state,), 44, components, keep)
        new = update(state, [keep, got])
        stacks = [new] + [swap(new, "col", col_size, o) for o in far]
    else:
        state = eliminate_part((state,), 44, components, keep)
        blocks = jnp.stack([keep, *sends]).transpose(2, 1, 0, 3).reshape(components, row_count)
        summed = lax.psum_scatter(blocks, "col", scatter_dimension=1, tiled=True)
        new = update(state, [summed[None]])[0]
        new = lax.all_gather(new, "col", axis=1, tiled=True).reshape(components, 2, 4, 128)
        stacks = list(new.transpose(2, 1, 0, 3))
    part = second(stacks, kept, sent)
    part = add([part, swap(part, BOTH, every, core)], part)
    got = swap(part, BOTH, every, upper[0] | core)

    new_second, *sends = mode_send(part, got, gram_frames, sent, BF16 if direct else F32)
    if not direct:
        keep = mode_keep(new_second, kept, new_second)
        blocks = jnp.stack([keep, *sends]).transpose(2, 1, 0, 3).reshape(components, row_count)
        return (frames, lax.psum_scatter(blocks, "col", scatter_dimension=1, tiled=True))
    got = [swap(x, "col", col_size, o) for o, x in zip(far, sends)]
    keep = mode_keep(new_second, kept, sends[0])
    mine, send = deal(me, [keep, *got], BF16)
    return (frames, mine + swap(send, "col", col_size, 4).astype(F32))


def solution(mesh):
    return jax.shard_map(
        local,
        mesh=mesh,
        in_specs=(P(None, "col", "row"), P(None, ("row", "col")), P(None, "col")),
        out_specs=(P(), P(None, ("row", "col"))),
        check_vma=False,
    )
```
